32 devices in a mesh: fsdp: 2 (over x), ctx: 4 (over z), tp: 4 (over y, core).
Axes of the slice: x: 2, y: 2, z: 4, core: 2. Of those that a mesh axis runs over, the one named last changes fastest.
Arguments:
- block_input: bfloat16 [4096, 6, 768], P(('ctx', 'tp'), 'fsdp'), may hold values from -6 to 6
- ln1_gain: bfloat16 [768], replicated, may hold values from 0.5 to 1.5
- ln1_bias: bfloat16 [768], replicated, may hold values from -1.5 to 1.5
- w_qkv: bfloat16 [3, 768, 768], P(None, 'fsdp', 'tp'), may hold values from -0.21875 to 0.21875
- qkv_bias: bfloat16 [2, 768], replicated, may hold values from -1.5 to 1.5
- rel_h: bfloat16 [27, 64], replicated, may hold values from -0.75 to 0.75
- rel_w: bfloat16 [27, 64], replicated, may hold values from -0.75 to 0.75
- w_proj: bfloat16 [768, 768], P('tp', 'fsdp'), may hold values from -1.25 to 1.25
- proj_bias: bfloat16 [768], replicated, may hold values from -1.5 to 1.5
- ln2_gain: bfloat16 [768], replicated, may hold values from 0.5 to 1.5
- ln2_bias: bfloat16 [768], replicated, may hold values from -1.5 to 1.5
- w_up: bfloat16 [768, 3072], P('fsdp', 'tp'), may hold values from -0.21875 to 0.21875
- up_bias: bfloat16 [3072], replicated, may hold values from -1.5 to 1.5
- w_down: bfloat16 [3072, 768], P('tp', 'fsdp'), may hold values from -0.109375 to 0.109375
- down_bias: bfloat16 [768], replicated, may hold values from -1.5 to 1.5
- cotangent: bfloat16 [4096, 6, 768], P(('ctx', 'tp'), 'fsdp'), may hold values from -6 to 6
Outputs:
- block_out: bfloat16 [4096, 6, 768], P(('ctx', 'tp'), 'fsdp')
- grad_input: bfloat16 [4096, 6, 768], P(('ctx', 'tp'), 'fsdp')
- grad_ln1_gain: float32 [768], replicated
- grad_ln1_bias: float32 [768], replicated
- grad_w_qkv: float32 [3, 768, 768], P(None, 'fsdp', 'tp')
- grad_qkv_bias: float32 [2, 768], replicated
- grad_rel_h: float32 [27, 64], replicated
- grad_rel_w: float32 [27, 64], replicated
- grad_w_proj: float32 [768, 768], P('tp', 'fsdp')
- grad_proj_bias: float32 [768], replicated
- grad_ln2_gain: float32 [768], replicated
- grad_ln2_bias: float32 [768], replicated
- grad_w_up: float32 [768, 3072], P('fsdp', 'tp')
- grad_up_bias: float32 [3072], replicated
- grad_w_down: float32 [3072, 768], P('tp', 'fsdp')
- grad_down_bias: float32 [768], replicated
The draws below stay inside these ranges and needn't reach their ends.
All inputs are finite; a program needn't handle non-finite values.
Results may differ from the reference program's by a relative error of at most 0.019.
Values may be sent and summed in bfloat16 or wider, within the bound.
A program may use at most 448 MiB of HBM per device.

```python
import jax
import jax.numpy as jnp
from jax import lax

D = 768
HEADS = 12
HEAD_DIM = 64
FF = 3072
WIN = 14
SIDE = 64
RELS = 27
PADDED = 70
NWIN = 25
HW = 4096
IMAGES = 6


def block_scale(own_key, dims, pieces, low, high):
    level, own = 1.0, jax.random.fold_in(own_key, 6)
    for axis_at, parts in pieces:
        steps = jnp.exp(jax.random.uniform(jax.random.fold_in(own, axis_at), (parts,), jnp.float32, low / len(pieces), high / len(pieces)))
        level = level * jnp.repeat(steps, dims[axis_at] // parts).reshape([-1 if axis == axis_at else 1 for axis in range(len(dims))])
    return level


def normal_values(stream_key, dims, width, bound, shards=(), kind=jnp.bfloat16):
    array = width * jax.random.normal(stream_key, dims, jnp.float32)
    if shards:
        array = array * block_scale(stream_key, dims, shards, -0.22, 0.18)
    return jnp.clip(array, -bound, bound).astype(kind)


def setup_inputs(seed: int = 0) -> dict:
    key_list = jax.random.split(jax.random.key(seed), 17)
    block_input = normal_values(key_list[0], (HW, IMAGES, D), 1.0, 6.0, ((0, 16), (1, 2)))
    ln1_gain = jnp.clip(1.0 + 0.1 * jax.random.normal(key_list[1], (D,), jnp.float32), 0.5, 1.5).astype(jnp.bfloat16)
    ln1_bias = normal_values(key_list[2], (D,), 0.3, 1.5)
    w_qkv = normal_values(key_list[3], (3, D, D), D ** -0.5, 0.21875, ((1, 2), (2, 4)))
    qkv_bias = normal_values(key_list[4], (2, D), 0.3, 1.5)
    rel_h = normal_values(key_list[5], (RELS, HEAD_DIM), HEAD_DIM ** -0.5, 0.75)
    rel_w = normal_values(key_list[6], (RELS, HEAD_DIM), HEAD_DIM ** -0.5, 0.75)
    w_proj = normal_values(key_list[7], (D, D), (D // 32) ** -0.5, 1.25, ((0, 4), (1, 2)))
    proj_bias = normal_values(key_list[8], (D,), 0.3, 1.5)
    ln2_gain = jnp.clip(1.0 + 0.1 * jax.random.normal(key_list[9], (D,), jnp.float32), 0.5, 1.5).astype(jnp.bfloat16)
    ln2_bias = normal_values(key_list[10], (D,), 0.3, 1.5)
    w_up = normal_values(key_list[11], (D, FF), D ** -0.5, 0.21875, ((0, 2), (1, 4)))
    up_bias = normal_values(key_list[12], (FF,), 0.3, 1.5)
    w_down = normal_values(key_list[13], (FF, D), FF ** -0.5, 0.109375, ((0, 4), (1, 2)))
    down_bias = normal_values(key_list[14], (D,), 0.3, 1.5)
    cotangent = normal_values(key_list[15], (HW, IMAGES, D), 1.0, 6.0, ((0, 16), (1, 2)))
    return {"block_input": block_input, "ln1_gain": ln1_gain, "ln1_bias": ln1_bias, "w_qkv": w_qkv, "qkv_bias": qkv_bias, "rel_h": rel_h, "rel_w": rel_w, "w_proj": w_proj, "proj_bias": proj_bias, "ln2_gain": ln2_gain, "ln2_bias": ln2_bias, "w_up": w_up, "up_bias": up_bias, "w_down": w_down, "down_bias": down_bias, "cotangent": cotangent}


EPSILON = 1e-06
HIGH = lax.Precision.HIGHEST

@jax.custom_vjp
def low(v):
    return lax.optimization_barrier(v.astype(jnp.bfloat16)).astype(jnp.float32)

@jax.custom_vjp
def low_back(v):
    return v

def low_keep(v):
    return (low(v), None)

def low_pass(kept, grad):
    return (grad,)

def back_keep(v):
    return (v, None)

def back_low(kept, grad):
    return (low(grad),)
low.defvjp(low_keep, low_pass)
low_back.defvjp(back_keep, back_low)

def layer_norm(rows, gain, shift):
    row_mean = lax.optimization_barrier(jnp.mean(rows, axis=-1, keepdims=True))
    centered = rows - row_mean
    row_var = lax.optimization_barrier(jnp.mean(centered * centered, axis=-1, keepdims=True))
    return centered * lax.rsqrt(row_var + EPSILON) * gain + shift

def attend(queries, keys_win, values_win, rel_h, rel_w):
    offsets = jnp.arange(WIN)[:, None] - jnp.arange(WIN)[None, :] + WIN - 1
    table_h = rel_h[offsets]
    table_w = rel_w[offsets]
    scores = jnp.einsum('wabhe,wcdhe->whabcd', queries, keys_win, precision=HIGH) * HEAD_DIM ** (-0.5)
    scores = scores + jnp.einsum('wabhe,ace->whabc', queries, table_h, precision=HIGH)[..., None]
    scores = scores + jnp.einsum('wabhe,bde->whabd', queries, table_w, precision=HIGH)[:, :, :, :, None, :]
    scores = low_back(scores.reshape(NWIN, HEADS, WIN * WIN, WIN * WIN))
    probs = low(jax.nn.softmax(scores, axis=-1))
    flat_values = values_win.reshape(NWIN, WIN * WIN, HEADS, HEAD_DIM)
    return jnp.einsum('whqk,wkhe->wqhe', probs, flat_values, precision=HIGH)

def block(image_x, ln1_gain, ln1_bias, w_qkv, qkv_bias, rel_h, rel_w, w_proj, proj_bias, ln2_gain, ln2_bias, w_up, up_bias, w_down, down_bias):
    normed = low(layer_norm(image_x, ln1_gain, ln1_bias))
    pad_extra = PADDED - SIDE
    cell_grid = jnp.pad(normed.reshape(SIDE, SIDE, D), ((0, pad_extra), (0, pad_extra), (0, 0)))
    bias_three = jnp.stack([qkv_bias[0], jnp.zeros_like(qkv_bias[0]), qkv_bias[1]])
    projected = jnp.einsum('abd,tde->abte', cell_grid, w_qkv, precision=HIGH) + bias_three
    projected = low(low_back(projected))
    per_side = PADDED // WIN
    windows = projected.reshape(per_side, WIN, per_side, WIN, 3, HEADS, HEAD_DIM)
    windows = windows.transpose(0, 2, 1, 3, 4, 5, 6).reshape(NWIN, WIN, WIN, 3, HEADS, HEAD_DIM)
    attended = attend(windows[:, :, :, 0], windows[:, :, :, 1], windows[:, :, :, 2], rel_h, rel_w)
    attended = low(low_back(attended))
    merged = attended.reshape(per_side, per_side, WIN, WIN, D).transpose(0, 2, 1, 3, 4)
    merged = merged.reshape(PADDED, PADDED, D)[:SIDE, :SIDE].reshape(SIDE * SIDE, D)
    branch = low_back(jnp.dot(merged, w_proj, precision=HIGH) + proj_bias)
    middle = image_x + branch
    normed_two = low(layer_norm(middle, ln2_gain, ln2_bias))
    gate_in = low_back(jnp.dot(normed_two, w_up, precision=HIGH) + up_bias)
    hidden = low(jax.nn.gelu(gate_in, approximate=False))
    return middle + low_back(jnp.dot(hidden, w_down, precision=HIGH) + down_bias)

def reference(block_input, ln1_gain, ln1_bias, w_qkv, qkv_bias, rel_h, rel_w, w_proj, proj_bias, ln2_gain, ln2_bias, w_up, up_bias, w_down, down_bias, cotangent):
    weights_f = tuple((weight_one.astype(jnp.float32) for weight_one in (ln1_gain, ln1_bias, w_qkv, qkv_bias, rel_h, rel_w, w_proj, proj_bias, ln2_gain, ln2_bias, w_up, up_bias, w_down, down_bias)))

    def one_image(so_far, image_pair):
        image_x, image_cot = image_pair
        image_out, pull_back = jax.vjp(block, image_x.astype(jnp.float32), *weights_f)
        grad_list = pull_back(image_cot.astype(jnp.float32))
        so_far = tuple((running + fresh_grad for running, fresh_grad in zip(so_far, grad_list[1:])))
        return (so_far, (image_out.astype(jnp.bfloat16), grad_list[0].astype(jnp.bfloat16)))
    zero_grads = tuple((jnp.zeros_like(weight_one) for weight_one in weights_f))
    totals, (outs_all, grads_in) = lax.scan(one_image, zero_grads, (jnp.moveaxis(block_input, 1, 0), jnp.moveaxis(cotangent, 1, 0)))
    return (jnp.moveaxis(outs_all, 0, 1), jnp.moveaxis(grads_in, 0, 1), totals[0], totals[1], totals[2], totals[3], totals[4], totals[5], totals[6], totals[7], totals[8], totals[9], totals[10], totals[11], totals[12], totals[13])
```

```python
import functools
import math

import jax
import jax.numpy as jnp
from jax import lax
from jax.experimental import pallas as pl
from jax.experimental.pallas import tpu as pltpu
from jax.sharding import PartitionSpec as P

HEAD_DIM = 64
HEADS = 12
WIN = 14
SIDE = 64
BANDS = 4
PAIRS = 7
D = 768
EPSILON = 1e-06
MESH = pl.DeviceIdType.MESH
BF = jnp.bfloat16
F32 = jnp.float32

FULL = 224
PART = 128
NFULL = 3
NPART = 2
PBASE = NFULL * FULL
ROWS = PBASE + NPART * PART
PIECE = 144
GROUPS = 3
SEG = 32
MASKED = -1e9
VMEM_LIMIT = 60 * 2**20


def coords():
    return lax.axis_index("fsdp"), lax.axis_index("ctx"), lax.axis_index("tp")


def part_kind(ctx, tp, k, images):
    return (3 - ctx) * 8 + tp * 2 + k


def pack_matrix():
    row = lax.broadcasted_iota(jnp.int32, (PIECE, 128), 0)
    col = lax.broadcasted_iota(jnp.int32, (PIECE, 128), 1)
    wide = row < 128
    c = jnp.where(wide, row // 32, 4)
    u = jnp.where(wide, (row % 32) // 16, (row - 128) // 8)
    b = jnp.where(wide, row % 16, (row - 128) % 8)
    source = u * SIDE + c * WIN + b
    return ((source == col) & (b < WIN)).astype(BF)


def piece_places(ctx, tp, images):
    dev = ctx * 4 + tp
    out = []
    for i in range(images):
        for u in range(2):
            m = dev * 2 + u
            band = m // PAIRS
            p = m % PAIRS
            low = band == BANDS
            for c in range(5):
                q_low = i * 5 + c
                if c < 4:
                    f = i * 4 + c
                    d_ctx = jnp.where(low, 3 - q_low // 8, band)
                    d_tp = jnp.where(low, (q_low % 8) // 2, f // 3)
                    slot = jnp.where(low, NFULL + q_low % 2, f % 3)
                    d_row = jnp.where(low, PBASE + (q_low % 2) * PART, (f % 3) * FULL) + p * 32
                    out.append((i, u, c, d_ctx, d_tp, d_row, slot, p))
                else:
                    q = jnp.where(low, q_low, 15 + (3 - band) * 3 + i)
                    d_ctx = 3 - q // 8
                    d_tp = (q % 8) // 2
                    d_row = PBASE + (q % 2) * PART + p * 16
                    out.append((i, u, c, d_ctx, d_tp, d_row, NFULL + q % 2, p))
    return out


def window_places(ctx, tp):
    out = []
    for k in range(NFULL):
        f = tp * 3 + k
        for p in range(PAIRS):
            m = ctx * PAIRS + p
            dev = m // 2
            out.append((k, p, 32, None, f // 4, m % 2, f % 4, dev // 4, dev % 4, k * FULL + p * 32))
    for k in range(NPART):
        q = (3 - ctx) * 8 + tp * 2 + k
        bottom = q < 15
        corner = bottom & (q % 5 == 4)
        right = (q >= 15) & (q < 27)
        qr = jnp.where(right, q - 15, 0)
        band = jnp.where(bottom, BANDS, 3 - qr // 3)
        image = jnp.where(bottom, q // 5, qr % 3)
        base = PBASE + k * PART
        for p in range(PAIRS):
            m = band * PAIRS + p
            dev = jnp.minimum(m // 2, 15)
            place = (image, m % 2, dev // 4, dev % 4)
            if p < 4:
                wide = bottom & jnp.logical_not(corner)
                out.append((NFULL + k, p, 32, wide, image, m % 2, q % 5, dev // 4, dev % 4, base + p * 32))
            narrow = (corner | right) if p < 4 else right
            out.append((NFULL + k, p, 16, narrow, image, m % 2, 4, dev // 4, dev % 4, base + p * 16))
    return out


def group_barrier(extra=()):
    f, c, t = coords()
    sem = pltpu.get_barrier_semaphore()
    count = 0
    for dc in range(4):
        for dt in range(4):
            if dc == 0 and dt == 0:
                continue
            pl.semaphore_signal(sem, inc=1, device_id=(f, (c + dc) % 4, (t + dt) % 4), device_id_type=MESH)
            count += 1
    for dest in extra:
        pl.semaphore_signal(sem, inc=1, device_id=dest, device_id_type=MESH)
        count += 1
    pl.semaphore_wait(sem, count)


def send_or_copy(src, dst, dest, me, send_sem, recv_sem):
    (d_ctx, d_tp), (f, ctx, tp) = dest, me
    here = (d_ctx == ctx) & (d_tp == tp)

    @pl.when(here)
    def _():
        pltpu.make_async_copy(src, dst, recv_sem).start()

    @pl.when(jnp.logical_not(here))
    def _():
        pltpu.make_async_remote_copy(
            src_ref=src, dst_ref=dst, send_sem=send_sem, recv_sem=recv_sem,
            device_id=(f, d_ctx, d_tp), device_id_type=MESH,
        ).start()


def wait_sent(src, dest, me, send_sem):
    (d_ctx, d_tp), (f, ctx, tp) = dest, me
    away = jnp.logical_not((d_ctx == ctx) & (d_tp == tp))

    @pl.when(away)
    def _():
        pltpu.make_async_copy(src, src, send_sem).wait()


def start_pieces(stage, out, a, images, me, ss, rs):
    _, ctx, tp = me
    for n, (i, u, c, d_ctx, d_tp, d_row, slot, p) in enumerate(piece_places(ctx, tp, images)):
        rows = 32 if c < 4 else 16
        src = stage.at[a, i, u, pl.ds(c * 32, rows)]
        dst = out.at[pl.ds(pl.multiple_of(d_row, 16), rows)]
        send_or_copy(src, dst, (d_ctx, d_tp), me, ss.at[a, n], rs.at[a, slot, p])


def finish_piece_sends(stage, a, images, me, ss):
    _, ctx, tp = me
    for n, (i, u, c, d_ctx, d_tp, d_row, slot, p) in enumerate(piece_places(ctx, tp, images)):
        rows = 32 if c < 4 else 16
        wait_sent(stage.at[a, i, u, pl.ds(c * 32, rows)], (d_ctx, d_tp), me, ss.at[a, n])


def wait_pieces(out, a, me, rs):
    _, ctx, tp = me
    for slot, p, rows, exists, *_rest, row in window_places(ctx, tp):
        dst = out.at[pl.ds(row, rows)]
        wait = pltpu.make_async_copy(dst, dst, rs.at[a, slot, p]).wait
        if exists is None:
            wait()
        else:
            pl.when(exists)(wait)


def block(ref, w, t, f, part=None):
    rows, cols = ((192, 384), (192, 384), (384, 768), (768, 384))[w]
    row_at, col_at = (f, t) if w == 2 else (t, f)
    start, size = row_at * rows, rows
    if part is not None:
        size = rows // 2
        start = start + part * size
    row_slice = pl.ds(pl.multiple_of(start, 16), size)
    col_slice = pl.ds(pl.multiple_of(col_at * cols, 128), cols)
    if w == 0:
        return ref.at[:, row_slice, col_slice]
    return ref.at[row_slice, col_slice]


def shard_half(ref, w, part):
    size = (96, 96, 192, 384)[w]
    if w == 0:
        return ref.at[:, pl.ds(part * size, size)]
    return ref.at[pl.ds(part * size, size)]


def remote(src, dst, dest, send_sem, recv_sem):
    return pltpu.make_async_remote_copy(
        src_ref=src, dst_ref=dst, send_sem=send_sem, recv_sem=recv_sem, device_id=dest, device_id_type=MESH
    )


class Gather:
    def __init__(self, shards, wholes, me, ss, rs, ls):
        self.shards, self.wholes = shards, wholes
        self.ss, self.rs, self.ls = ss, rs, ls
        f, c, t = me
        y = (t + 2) % 4
        s = t + 1 - 2 * (t % 2)
        self.me = me
        self.other_f, self.other_y, self.other_s = 1 - f, y, s
        self.to_x, self.to_y, self.to_s = (1 - f, c, t), (f, c, y), (f, c, s)

    def copy(self, w, k):
        f, _, t = self.me
        g, y = self.other_f, self.other_y
        whole = self.wholes[w]
        own = self.shards[w]
        if k < 3:
            src, dst = own, block(whole, w, t, f)
            dest = (self.to_x, self.to_y, self.to_s)[k]
        elif k == 3:
            src = dst = block(whole, w, t, g, 0)
            dest = self.to_y
        elif k == 4:
            src = dst = block(whole, w, y, f, 1)
            dest = self.to_x
        elif k == 5:
            src = dst = block(whole, w, t, g)
            dest = self.to_s
        elif k == 6:
            src = dst = block(whole, w, y, f)
            dest = self.to_s
        else:
            src = dst = block(whole, w, y, g, k - 7)
            dest = self.to_s
        return remote(src, dst, dest, self.ss.at[w, k], self.rs.at[w, k])

    def landed(self, w, k):
        f, _, t = self.me
        g, y, s = self.other_f, self.other_y, self.other_s
        sy = (s + 2) % 4
        whole = self.wholes[w]
        place = (
            (t, g, None), (y, f, None), (s, f, None),
            (y, g, 0), (y, g, 1),
            (s, g, None), (sy, f, None), (sy, g, 0), (sy, g, 1),
        )[k]
        return block(whole, w, *place)

    def wait_recv(self, w, k):
        dst = self.landed(w, k)
        pltpu.make_async_copy(dst, dst, self.rs.at[w, k]).wait()

    def wait_send(self, w, k):
        src = self.landed(w, k)
        pltpu.make_async_copy(src, src, self.ss.at[w, k]).wait()

    def start_own(self, w):
        f, _, t = self.me
        for k in range(3):
            self.copy(w, k).start()
        pltpu.make_async_copy(self.shards[w], block(self.wholes[w], w, t, f), self.ls.at[w]).start()

    def forward_first(self, w):
        self.wait_recv(w, 0)
        self.copy(w, 3).start()
        self.copy(w, 5).start()
        self.wait_recv(w, 1)
        self.copy(w, 4).start()
        self.copy(w, 6).start()

    def forward_second(self, w):
        self.wait_recv(w, 3)
        self.copy(w, 7).start()
        self.wait_recv(w, 4)
        self.copy(w, 8).start()

    def finish(self, w):
        f, _, t = self.me
        for k in (2, 5, 6, 7, 8):
            self.wait_recv(w, k)
        for k in range(9):
            self.wait_send(w, k)
        pltpu.make_async_copy(self.shards[w], block(self.wholes[w], w, t, f), self.ls.at[w]).wait()


def gather_kernel(images, with_weights, *refs):
    if with_weights:
        x_ref, c_ref, wq, wp, wu, wd, xw, cw, gq, gp, gu, gd, stage, ss, rs, gss, grs, gls = refs
    else:
        x_ref, c_ref, xw, cw, stage, ss, rs = refs
    me = coords()
    f, ctx, tp = me
    extra = ((1 - f, ctx, tp),) if with_weights else ()
    group_barrier(extra)
    pack = pack_matrix()
    if with_weights:
        gather = Gather((wq, wp, wu, wd), (gq, gp, gu, gd), me, gss, grs, gls)
    for a, (src, out) in enumerate(((x_ref, xw), (c_ref, cw))):
        for i in range(images):
            for u in range(2):
                stage[a, i, u] = jnp.dot(
                    pack, src[i, pl.ds(u * 128, 128)], preferred_element_type=F32
                ).astype(BF)
        start_pieces(stage, out, a, images, me, ss, rs)
        if with_weights and a == 0:
            for w in range(4):
                gather.start_own(w)
    if with_weights:
        for w in range(4):
            gather.forward_first(w)
        for w in range(4):
            gather.forward_second(w)
    for a, out in enumerate((xw, cw)):
        wait_pieces(out, a, me, rs)
        finish_piece_sends(stage, a, images, me, ss)
    if with_weights:
        for w in range(4):
            gather.finish(w)


def gather_in(x3, c3, shards):
    images = x3.shape[0]
    any_spec = pl.BlockSpec(memory_space=pl.ANY)
    vmem = pl.BlockSpec(memory_space=pltpu.VMEM)
    with_weights = shards is not None
    token_shape = jax.ShapeDtypeStruct((ROWS, D), BF)
    out_shape = [token_shape, token_shape]
    scratch = [
        pltpu.VMEM((2, images, 2, PIECE, D), BF),
        pltpu.SemaphoreType.DMA((2, images * 10)),
        pltpu.SemaphoreType.DMA((2, NFULL + NPART, PAIRS)),
    ]
    args = [x3, c3]
    if with_weights:
        args += list(shards)
        out_shape += [
            jax.ShapeDtypeStruct(s, BF) for s in ((3, D, D), (D, D), (D, 4 * D), (4 * D, D))
        ]
        scratch += [pltpu.SemaphoreType.DMA((4, 9)), pltpu.SemaphoreType.DMA((4, 9)), pltpu.SemaphoreType.DMA((4,))]
    return pl.pallas_call(
        functools.partial(gather_kernel, images, with_weights),
        out_shape=out_shape,
        in_specs=[vmem, vmem] + [any_spec] * (len(args) - 2),
        out_specs=[any_spec] * len(out_shape),
        scratch_shapes=scratch,
        compiler_params=pltpu.CompilerParams(
            collective_id=0, has_side_effects=True, vmem_limit_bytes=VMEM_LIMIT
        ),
        name="tokens_and_weights_in",
    )(*args)


STEP_ROWS = (576, 192, 768, 768)


def add_rows(dst, src, rows, cols):
    size = 96 if rows % 96 == 0 else 64

    @pl.loop(0, rows // size)
    def _(n):
        here = pl.ds(pl.multiple_of(n * size, 16), size)
        dst[here] = (dst[here].astype(F32) + src[here].astype(F32)).astype(BF)


def add_view(dst, src, w):
    if w == 0:
        for k in range(3):
            view = dst.at[k]
            add_rows(view, src.at[k], view.shape[0], view.shape[1])
    else:
        add_rows(dst, src, dst.shape[0], dst.shape[1])


def copy_f32(dst, src, w):
    if w == 0:
        for k in range(3):
            copy_f32(dst.at[k], src.at[k], 1)
        return
    rows = dst.shape[0]
    size = 96 if rows % 96 == 0 else 64

    @pl.loop(0, rows // size)
    def _(n):
        here = pl.ds(pl.multiple_of(n * size, 16), size)
        dst[here] = src[here].astype(F32)


HALF_SHAPES = ((3, 96, 384), (96, 384), (192, 768), (384, 384))
SHARD_SHAPES = ((3, 192, 384), (192, 384), (384, 768), (768, 384))


def reduce_kernel(images, with_weights, *refs):
    if with_weights:
        (y_ref, g_ref, gq, gp, gu, gd, few_ref, y_out, g_out, oq, op, ou, od, few_out,
         stage, ss, rs, r1q, r1p, r1u, r1d, raq, rap, rau, rad, rzq, rzp, rzu, rzd,
         few_in, s1, v1, s2, v2, s3, v3, fs, fr) = refs
    else:
        y_ref, g_ref, y_out, g_out, stage, ss, rs = refs
    me = coords()
    f, ctx, tp = me
    group_barrier(((1 - f, ctx, tp),) if with_weights else ())

    places = window_places(ctx, tp)
    pairs = ((y_ref, y_out), (g_ref, g_out))
    for a, (src_ref, _) in enumerate(pairs):
        for n, (slot, p, rows, exists, image, u, c, d_ctx, d_tp, row) in enumerate(places):
            def go(a=a, n=n, rows=rows, image=image, u=u, c=c, d_ctx=d_ctx, d_tp=d_tp, row=row, src_ref=src_ref):
                src = src_ref.at[pl.ds(row, rows)]
                dst = stage.at[a, image, u, pl.ds(pl.multiple_of(c * 32, 16), rows)]
                send_or_copy(src, dst, (d_ctx, d_tp), me, ss.at[a, n], rs.at[a, image, u, c])
            if exists is None:
                go()
            else:
                pl.when(exists)(go)

    if with_weights:
        grads = (gq, gp, gu, gd)
        outs = (oq, op, ou, od)
        r1, ra, rz = (r1q, r1p, r1u, r1d), (raq, rap, rau, rad), (rzq, rzp, rzu, rzd)
        g, y, s = 1 - f, (tp + 2) % 4, tp + 1 - 2 * (tp % 2)
        sy = (s + 2) % 4
        to_x, to_y, to_s = (g, ctx, tp), (f, ctx, y), (f, ctx, s)
        order = (3, 2, 1, 0)
        waits = []

        def send(src, dst, dest, send_sem, recv_sem):
            cp = remote(src, dst, dest, send_sem, recv_sem)
            cp.start()
            waits.append(cp)
            return cp

        few_out[...] = few_ref[...]
        few_steps = (to_s, to_x, to_y, (f, ctx + 1 - 2 * (ctx % 2), tp), (f, (ctx + 2) % 4, tp))

        def few_start(n):
            few_in[5 + n] = few_out[...]
            return send(few_in.at[5 + n], few_in.at[n], few_steps[n], fs.at[n], fr.at[n])

        def few_finish(cp, n):
            cp.wait_recv()
            few_out[...] = few_out[...] + few_in[n]

        first = {}
        for w in order:
            for n, t_there in enumerate((s, sy)):
                for h in range(2):
                    first[w, n, h] = send(
                        block(grads[w], w, t_there, h), r1[w].at[n, h], to_s, s1.at[w, n, h], v1.at[w, n, h]
                    )
        few = few_start(0)

        phase1 = {}
        for w in order:
            for n, t_here in enumerate((tp, y)):
                for h in range(2):
                    first[w, n, h].wait_recv()
                    add_view(block(grads[w], w, t_here, h), r1[w].at[n, h], w)
            phase1[w] = (
                send(block(grads[w], w, tp, g, 0), ra[w].at[0], to_x, s2.at[w, 0], v2.at[w, 0]),
                send(block(grads[w], w, y, g, 0), ra[w].at[1], to_x, s2.at[w, 1], v2.at[w, 1]),
                send(block(grads[w], w, y, f, 1), ra[w].at[2], to_y, s2.at[w, 2], v2.at[w, 2]),
                send(block(grads[w], w, y, g, 1), ra[w].at[3], to_y, s2.at[w, 3], v2.at[w, 3]),
            )
        few_finish(few, 0)
        few = few_start(1)
        phase2 = {}
        for w in order:
            views = (
                block(grads[w], w, tp, f, 0), block(grads[w], w, y, f, 0),
                block(grads[w], w, tp, f, 1), block(grads[w], w, tp, g, 1),
            )
            for k in range(4):
                phase1[w][k].wait_recv()
                add_view(views[k], ra[w].at[k], w)
            phase2[w] = (
                send(block(grads[w], w, y, f, 0), ra[w].at[4], to_y, s2.at[w, 4], v2.at[w, 4]),
                send(block(grads[w], w, tp, g, 1), ra[w].at[5], to_x, s2.at[w, 5], v2.at[w, 5]),
            )
        few_finish(few, 1)
        few = few_start(2)

        outer = (ctx == 0) | (ctx == 3)
        inner = jnp.logical_not(outer)
        mid_peer = (f, 3 - ctx, tp)
        in_peer = (f, jnp.where(ctx == 0, 1, 2), tp)
        out_peer = (f, jnp.where(ctx == 1, 0, 3), tp)
        for w in order:
            for k in range(2):
                phase2[w][k].wait_recv()
                add_view(block(grads[w], w, tp, f, k), ra[w].at[4 + k], w)
            mine = block(grads[w], w, tp, f)

            @pl.when(outer)
            def _(w=w, mine=mine):
                remote(mine, rz[w].at[0], in_peer, s3.at[w, 0], v3.at[w, 0]).start()
        for w in order:
            mine = block(grads[w], w, tp, f)

            @pl.when(inner)
            def _(w=w, mine=mine):
                pltpu.make_async_copy(rz[w].at[0], rz[w].at[0], v3.at[w, 0]).wait()
                add_view(mine, rz[w].at[0], w)
                remote(mine, rz[w].at[1], mid_peer, s3.at[w, 0], v3.at[w, 1]).start()
        for w in order:
            mine = block(grads[w], w, tp, f)

            @pl.when(inner)
            def _(w=w, mine=mine):
                pltpu.make_async_copy(rz[w].at[1], rz[w].at[1], v3.at[w, 1]).wait()
                add_view(rz[w].at[1], mine, w)
                remote(rz[w].at[1], rz[w].at[2], out_peer, s3.at[w, 1], v3.at[w, 2]).start()
                copy_f32(outs[w], rz[w].at[1], w)
        few_finish(few, 2)
        few = few_start(3)
        for w in order:
            @pl.when(outer)
            def _(w=w):
                pltpu.make_async_copy(rz[w].at[2], rz[w].at[2], v3.at[w, 2]).wait()
                copy_f32(outs[w], rz[w].at[2], w)
        few_finish(few, 3)
        few = few_start(4)
        few_finish(few, 4)

        for cp in waits:
            cp.wait_send()
        for w in order:
            one = rz[w].at[0]
            pltpu.make_async_copy(one, one, s3.at[w, 0]).wait()

            @pl.when(inner)
            def _(one=one, w=w):
                pltpu.make_async_copy(one, one, s3.at[w, 1]).wait()

    unpack = pack_matrix()
    for a, (src_ref, out_ref) in enumerate(pairs):
        for i in range(images):
            for u in range(2):
                for c in range(5):
                    rows = 32 if c < 4 else 16
                    dst = stage.at[a, i, u, pl.ds(c * 32, rows)]
                    pltpu.make_async_copy(dst, dst, rs.at[a, i, u, c]).wait()
                out_ref[i, pl.ds(u * 128, 128)] = lax.dot_general(
                    unpack, stage[a, i, u], (((0,), (0,)), ((), ())), preferred_element_type=F32
                ).astype(BF)
        for n, (slot, p, rows, exists, image, u, c, d_ctx, d_tp, row) in enumerate(places):
            def done(a=a, n=n, rows=rows, d_ctx=d_ctx, d_tp=d_tp, row=row, src_ref=src_ref):
                wait_sent(src_ref.at[pl.ds(row, rows)], (d_ctx, d_tp), me, ss.at[a, n])
            if exists is None:
                done()
            else:
                pl.when(exists)(done)


def send_back(y, g, images, grads=None, few=None):
    vmem = pl.BlockSpec(memory_space=pltpu.VMEM)
    with_weights = grads is not None
    n_places = NFULL * PAIRS + NPART * (4 + PAIRS)
    token = jax.ShapeDtypeStruct((images, 256, D), BF)
    out_shape = [token, token]
    args = [y, g]
    dma = pltpu.SemaphoreType.DMA
    scratch = [
        pltpu.VMEM((2, images, 2, PIECE, D), BF),
        dma((2, n_places)),
        dma((2, images, 2, 5)),
    ]
    if with_weights:
        args += list(grads) + [few]
        out_shape += [jax.ShapeDtypeStruct(s, F32) for s in SHARD_SHAPES]
        out_shape += [jax.ShapeDtypeStruct(few.shape, F32)]
        scratch += [pltpu.VMEM((2, 2) + s, BF) for s in SHARD_SHAPES]
        scratch += [pltpu.VMEM((6,) + s, BF) for s in HALF_SHAPES]
        scratch += [pltpu.VMEM((3,) + s, BF) for s in SHARD_SHAPES]
        scratch += [pltpu.VMEM((10,) + few.shape, F32)]
        scratch += [dma((4, 2, 2)), dma((4, 2, 2)), dma((4, 6)), dma((4, 6)), dma((4, 2)), dma((4, 3)), dma((5,)), dma((5,))]
    return pl.pallas_call(
        functools.partial(reduce_kernel, images, with_weights),
        out_shape=out_shape,
        in_specs=[vmem] * len(args),
        out_specs=[vmem] * len(out_shape),
        scratch_shapes=scratch,
        compiler_params=pltpu.CompilerParams(
            collective_id=1, has_side_effects=True, vmem_limit_bytes=VMEM_LIMIT
        ),
        name="tokens_and_gradients_out",
    )(*args)


def barrel(x, shift, left):
    lanes = x.shape[-1]
    for bit in (1, 2, 4, 8):
        moved = pltpu.roll(x, lanes - bit if left else bit, 1)
        x = jnp.where((shift // bit) % 2 == 1, moved, x)
    return x


def row_places(rows, narrow):
    r = lax.broadcasted_iota(jnp.int32, (rows, 128), 0)
    if narrow is None:
        return r // 16, r % 16
    is_narrow = narrow > 0
    return jnp.where(is_narrow, r // 8, r // 16), jnp.where(is_narrow, r % 8, r % 16)


def half_mask(hh):
    lane = lax.broadcasted_iota(jnp.int32, (1, 128), 1)
    return ((lane // 64) == hh).astype(BF)


def nt(a, b):
    return lax.dot_general(a, b, (((1,), (1,)), ((), ())), preferred_element_type=F32)


def tn(a, b):
    return lax.dot_general(a, b, (((0,), (0,)), ((), ())), preferred_element_type=F32)


def key_rows(ref, base, rows, col, fill):
    part = ref[pl.ds(base, rows), pl.ds(col, 128)]
    if rows == FULL:
        return part
    return jnp.concatenate([part, jnp.broadcast_to(fill, (FULL - rows, 128)).astype(BF)], axis=0)


def attention_slot(qkv, rel_cols, bias_v, e_at, o_ref, p_ref, p_at, base, rows, narrow, x_scr):
    a_row, b_row = row_places(rows, narrow)
    q_all = qkv[pl.ds(base, rows), pl.ds(0, D)]
    lane = lax.broadcasted_iota(jnp.int32, (rows, 128), 1) % SEG
    for axis, pos in ((0, a_row), (1, b_row)):
        raw = jnp.dot(q_all, rel_cols[:, pl.ds(axis * 384, 384)], preferred_element_type=F32)
        for g in range(GROUPS):
            v = barrel(raw[:, g * 128:(g + 1) * 128], jnp.maximum(13 - pos, 0), True)
            hi = v.astype(BF).astype(F32)
            lo = pltpu.roll(v - hi, 16, 1)
            mix = jnp.where(lane < WIN, hi, jnp.where(lane >= 16, lo, 0.0))
            if axis == 0:
                mix = jnp.where(lane == 15, 1.0, mix)
            x_scr[pl.ds(0, rows), pl.ds(g * 256 + axis * 128, 128)] = mix.astype(BF)
    for hp in range(6):
        q = q_all[:, hp * 128:(hp + 1) * 128]
        k = key_rows(qkv, base, rows, D + hp * 128, jnp.zeros((1, 128), BF))
        v = key_rows(qkv, base, rows, 2 * D + hp * 128, bias_v[:, pl.ds(hp * 128, 128)])
        out = jnp.zeros((rows, 128), F32)
        for hh in range(2):
            h = hp * 2 + hh
            x = x_scr[pl.ds(0, rows), pl.ds((h // 4) * 256, 256)]
            s = nt(q, k * (half_mask(hh) * 0.125)) + nt(x, e_at[h % 4])
            p = jnp.exp(s - jnp.max(s, axis=-1, keepdims=True))
            p = (p * (1.0 / jnp.sum(p, axis=-1, keepdims=True))).astype(BF)
            p_ref[p_at * HEADS + h] = p
            out = out + jnp.dot(p, v * half_mask(hh), preferred_element_type=F32)
        o_ref[pl.ds(base, rows), pl.ds(hp * 128, 128)] = out.astype(BF)


def narrow_flag(k):
    _, ctx, tp = coords()
    q = (3 - ctx) * 8 + tp * 2 + k
    is_narrow = ((q < 15) & (q % 5 == 4)) | ((q >= 15) & (q < 27))
    return jnp.where(is_narrow, 1, 0)


def attention_kernel(qkv, rel_cols, bias_v, e_ref, o_ref, pf_ref, pp_ref, x_scr):
    @pl.loop(0, NFULL)
    def _(n):
        attention_slot(qkv, rel_cols, bias_v, e_ref.at[0], o_ref, pf_ref, n,
                       pl.multiple_of(n * FULL, 16), FULL, None, x_scr)

    @pl.loop(0, NPART)
    def _(n):
        attention_slot(qkv, rel_cols, bias_v, e_ref.at[1 + n], o_ref, pp_ref, n,
                       pl.multiple_of(PBASE + n * PART, 16), PART, narrow_flag(n), x_scr)


def attention(qkv, rel_cols, bias_v, e):
    vmem = pl.BlockSpec(memory_space=pltpu.VMEM)
    return pl.pallas_call(
        attention_kernel,
        out_shape=[
            jax.ShapeDtypeStruct((ROWS, D), BF),
            jax.ShapeDtypeStruct((NFULL * HEADS, FULL, FULL), BF),
            jax.ShapeDtypeStruct((NPART * HEADS, PART, FULL), BF),
        ],
        in_specs=[vmem] * 4,
        out_specs=[vmem] * 3,
        scratch_shapes=[pltpu.VMEM((FULL, GROUPS * 256), BF)],
        compiler_params=pltpu.CompilerParams(vmem_limit_bytes=VMEM_LIMIT),
        name="attention_forward",
    )(qkv, rel_cols, bias_v, e)


def attention_back_slot(qkv, do_ref, rel_cols, bias_v, e_at, p_ref, p_at, dqkv, d_scr, acc_scr, pad_acc,
                        rel_acc, base, rows, narrow):
    a_row, b_row = row_places(rows, narrow)
    for g in range(GROUPS):
        dx = jnp.zeros((rows, 256), F32)
        for hp in (2 * g, 2 * g + 1):
            q = qkv[pl.ds(base, rows), pl.ds(hp * 128, 128)]
            k = key_rows(qkv, base, rows, D + hp * 128, jnp.zeros((1, 128), BF))
            v = key_rows(qkv, base, rows, 2 * D + hp * 128, bias_v[:, pl.ds(hp * 128, 128)])
            do = do_ref[pl.ds(base, rows), pl.ds(hp * 128, 128)]
            dq = jnp.zeros((rows, 128), F32)
            dk = jnp.zeros((FULL, 128), F32)
            dv = jnp.zeros((FULL, 128), F32)
            for hh in range(2):
                h = hp * 2 + hh
                mask = half_mask(hh)
                do_m = do * mask
                dp = nt(do_m, v)
                p_low = p_ref[p_at * HEADS + h]
                t = p_low.astype(F32)
                tp = t * dp
                ds = (tp - t * jnp.sum(tp, axis=-1, keepdims=True)).astype(BF)
                dq = dq + jnp.dot(ds, k * (mask * 0.125), preferred_element_type=F32)
                dx = dx + jnp.dot(ds, e_at[h % 4], preferred_element_type=F32)
                dk = dk + tn(ds, q * (mask * 0.125))
                dv = dv + tn(p_low, do_m)
            acc_scr[pl.ds(0, rows), pl.ds(hp * 128, 128)] = dq
            dqkv[pl.ds(base, rows), pl.ds(D + hp * 128, 128)] = dk[:rows].astype(BF)
            dqkv[pl.ds(base, rows), pl.ds(2 * D + hp * 128, 128)] = dv[:rows].astype(BF)
            if rows < FULL:
                pad_acc[:, pl.ds(hp * 128, 128)] += jnp.sum(dv[rows:], axis=0, keepdims=True)
        lane = lax.broadcasted_iota(jnp.int32, (rows, 128), 1) % SEG
        for axis, pos in ((0, a_row), (1, b_row)):
            v = jnp.where(lane < WIN, dx[:, axis * 128:(axis + 1) * 128], 0.0)
            v = barrel(v, jnp.maximum(13 - pos, 0), False)
            d_scr[pl.ds(0, rows), pl.ds(axis * 384 + g * 128, 128)] = v.astype(BF)
    d = d_scr[pl.ds(0, rows), :]
    q_all = qkv[pl.ds(base, rows), pl.ds(0, D)]
    dq = acc_scr[pl.ds(0, rows), :] + nt(d, rel_cols[...])
    dqkv[pl.ds(base, rows), pl.ds(0, D)] = dq.astype(BF)
    rel_acc[...] += tn(d, q_all)


def attention_back_kernel(qkv, do_ref, rel_cols, bias_v, e_ref, pf_ref, pp_ref, dqkv, pad_ref, rel_ref,
                          d_scr, acc_scr, rel_acc):
    pad_ref[...] = jnp.zeros_like(pad_ref)
    rel_acc[...] = jnp.zeros_like(rel_acc)

    @pl.loop(0, NFULL)
    def _(n):
        attention_back_slot(qkv, do_ref, rel_cols, bias_v, e_ref.at[0], pf_ref, n, dqkv, d_scr, acc_scr, pad_ref,
                            rel_acc, pl.multiple_of(n * FULL, 16), FULL, None)

    @pl.loop(0, NPART)
    def _(n):
        attention_back_slot(qkv, do_ref, rel_cols, bias_v, e_ref.at[1 + n], pp_ref, n, dqkv, d_scr, acc_scr, pad_ref,
                            rel_acc, pl.multiple_of(PBASE + n * PART, 16), PART, narrow_flag(n))

    lane = lax.broadcasted_iota(jnp.int32, (SEG, D), 1) // HEAD_DIM
    for axis in range(2):
        total = jnp.zeros((SEG, D), F32)
        for h in range(HEADS):
            total = total + jnp.where(lane == h, rel_acc[pl.ds(axis * 384 + h * SEG, SEG), :], 0.0)
        rel_ref[axis] = total


def attention_back(qkv, do, rel_cols, bias_v, e, pf, pp):
    vmem = pl.BlockSpec(memory_space=pltpu.VMEM)
    return pl.pallas_call(
        attention_back_kernel,
        out_shape=[
            jax.ShapeDtypeStruct((ROWS, 3 * D), BF),
            jax.ShapeDtypeStruct((1, D), F32),
            jax.ShapeDtypeStruct((2, SEG, D), F32),
        ],
        in_specs=[vmem] * 7,
        out_specs=[vmem] * 3,
        scratch_shapes=[
            pltpu.VMEM((FULL, D), BF),
            pltpu.VMEM((FULL, D), F32),
            pltpu.VMEM((D, D), F32),
        ],
        compiler_params=pltpu.CompilerParams(vmem_limit_bytes=VMEM_LIMIT),
        name="attention_backward",
    )(qkv, do, rel_cols, bias_v, e, pf, pp)


def slot_tables():
    _, ctx, tp = coords()
    r = jnp.arange(FULL)
    full_real = (r % 16) < WIN
    real = [full_real] * NFULL
    keys = [(r // 16, r % 16, full_real)]
    for k in range(NPART):
        q = (3 - ctx) * 8 + tp * 2 + k
        bottom = q < 15
        corner = bottom & (q % 5 == 4)
        right = (q >= 15) & (q < 27)
        rp = r[:PART]
        real.append(
            jnp.where(corner, rp < 64, jnp.where(right, rp < 112, bottom & (rp % 16 < WIN)))
        )
        a_right = jnp.where(r < 112, r // 8, (r - 112) // 8)
        b_right = jnp.where(r < 112, r % 8, 8 + (r - 112) % 8)
        a_corner = jnp.where(r < 64, r // 8, jnp.where(r < 128, (r - 64) // 8, 8 + (r - 128) // 16))
        b_corner = jnp.where(r < 64, r % 8, jnp.where(r < 128, 8 + (r - 64) % 8, (r - 128) % 16))
        a = jnp.where(corner, a_corner, jnp.where(right, a_right, r // 16))
        b = jnp.where(corner, b_corner, jnp.where(right, b_right, r % 16))
        keys.append((a, b, b < WIN))
    a = jnp.stack([x[0] for x in keys])[:, None, :, None]
    b = jnp.stack([x[1] for x in keys])[:, None, :, None]
    ok = jnp.stack([x[2] for x in keys])[:, None, :, None]
    col = jnp.arange(256)[None, None, None, :]
    head = jnp.arange(4)[None, :, None, None]
    mine = ((col % 128) // SEG) == head
    j = col % 16
    pos = jnp.where(col < 128, a, b)
    one = (mine & ok & (j == pos) & (j < WIN)).astype(F32)
    out = (mine & jnp.logical_not(ok) & (col < 128) & (col % SEG == 15)).astype(F32) * MASKED
    return jnp.concatenate(real)[:, None], (one + out).astype(BF)


def relative_columns(rel_h, rel_w):
    parts = []
    eye = jnp.eye(HEADS, dtype=BF)
    for rel in (rel_h, rel_w):
        rev = jnp.pad(rel[::-1], ((0, SEG - rel.shape[0]), (0, 0))).T
        wide = eye[:, None, :, None] * rev[None, :, None, :]
        parts.append(wide.reshape(D, HEADS * SEG))
    return jnp.concatenate(parts, axis=1)


def norm_stats(v):
    mean = jnp.mean(v, axis=-1, keepdims=True)
    centered = v - mean
    r = lax.rsqrt(jnp.mean(centered * centered, axis=-1, keepdims=True) + EPSILON)
    return centered * r, r


def norm_back(n, xhat, r, gain):
    m = n * gain
    return r * (m - jnp.mean(m, -1, keepdims=True) - xhat * jnp.mean(m * xhat, -1, keepdims=True))


def gelu_both(u):
    x = jnp.abs(u) * math.sqrt(0.5)
    t = 1.0 / (1.0 + 0.3275911 * x)
    e = jnp.exp(-0.5 * u * u)
    poly = t * (0.254829592 + t * (-0.284496736 + t * (1.421413741 + t * (-1.453152027 + t * 1.061405429))))
    tail = 0.5 * poly * e
    phi = jnp.where(u >= 0, 1.0 - tail, tail)
    return u * phi, phi + u * e * (1.0 / math.sqrt(2 * math.pi))


def mm(a, b, dims="mk,kn->mn"):
    return jnp.einsum(dims, a, b, preferred_element_type=F32)


def whole_weights(shards):
    wq, wp, wu, wd = shards
    wq = lax.all_gather(lax.all_gather(wq, "fsdp", axis=2, tiled=True), "tp", axis=1, tiled=True)
    wp = lax.all_gather(lax.all_gather(wp, "fsdp", axis=1, tiled=True), "tp", axis=0, tiled=True)
    wu = lax.all_gather(lax.all_gather(wu, "fsdp", axis=0, tiled=True), "tp", axis=1, tiled=True)
    wd = lax.all_gather(lax.all_gather(wd, "fsdp", axis=1, tiled=True), "tp", axis=0, tiled=True)
    return wq, wp, wu, wd


def summed_weights(grads):
    dims = ((1, 2), (0, 1), (1, 0), (0, 1))
    out = []
    for grad, (t_dim, f_dim) in zip(grads, dims):
        part = lax.psum_scatter(grad, "tp", scatter_dimension=t_dim, tiled=True)
        part = lax.psum_scatter(part, "fsdp", scatter_dimension=f_dim, tiled=True)
        out.append(lax.psum(part, "ctx").astype(F32))
    return out


def local(direct, block_input, ln1_gain, ln1_bias, w_qkv, qkv_bias, rel_h, rel_w, w_proj, proj_bias,
          ln2_gain, ln2_bias, w_up, up_bias, w_down, down_bias, cotangent):
    images = block_input.shape[1]
    x3 = jnp.transpose(block_input, (1, 0, 2))
    c3 = jnp.transpose(cotangent, (1, 0, 2))
    shards = (jnp.transpose(w_qkv, (0, 2, 1)), w_proj, w_up, w_down)
    if direct:
        xw, cw, wq, wp, wu, wd = gather_in(x3, c3, shards)
    else:
        xw, cw = gather_in(x3, c3, None)
        wq, wp, wu, wd = whole_weights(shards)
    wq = wq.reshape(3 * D, D)
    real, e = slot_tables()
    rel_cols = relative_columns(rel_h, rel_w)
    g1, b1, g2, b2 = (v.astype(F32) for v in (ln1_gain, ln1_bias, ln2_gain, ln2_bias))
    x = jnp.where(real, xw, 0).astype(F32)
    cot_low = jnp.where(real, cw, 0)
    cot = cot_low.astype(F32)
    bias_three = jnp.concatenate([qkv_bias[0], jnp.zeros_like(qkv_bias[0]), qkv_bias[1]]).astype(F32)

    xhat1, r1 = norm_stats(x)
    n1 = jnp.where(real, xhat1 * g1 + b1, 0.0).astype(BF)
    qkv = (mm(n1, wq, "mk,nk->mn") + bias_three).astype(BF)
    attended, pf, pp = attention(qkv, rel_cols, qkv_bias[1:2], e)
    middle = x + mm(attended, wp) + proj_bias.astype(F32)
    xhat2, r2 = norm_stats(middle)
    n2 = (xhat2 * g2 + b2).astype(BF)
    gate_in = mm(n2, wu) + up_bias.astype(F32)
    hidden, slope = gelu_both(gate_in)
    hidden = hidden.astype(BF)
    out = (middle + mm(hidden, wd) + down_bias.astype(F32)).astype(BF)

    d_down_bias = jnp.sum(cot, axis=0)
    d_wd = mm(hidden, cot_low, "km,kn->mn").astype(BF)
    d_gate = (mm(cot_low, wd, "mk,nk->mn") * slope).astype(BF)
    d_wu = mm(n2, d_gate, "km,kn->mn").astype(BF)
    d_up_bias = jnp.sum(d_gate, axis=0, dtype=F32)
    d_n2 = mm(d_gate, wu, "mk,nk->mn")
    d_g2 = jnp.sum(d_n2 * xhat2, axis=0)
    d_b2 = jnp.sum(d_n2, axis=0)
    d_middle = cot + norm_back(d_n2, xhat2, r2, g2)
    branch = d_middle.astype(BF)
    d_proj_bias = jnp.sum(branch, axis=0, dtype=F32)
    d_wp = mm(attended, branch, "km,kn->mn").astype(BF)
    d_att = mm(branch, wp, "mk,nk->mn").astype(BF)
    dqkv, d_pad, d_rel = attention_back(qkv, d_att, rel_cols, qkv_bias[1:2], e, pf, pp)
    d_wq = mm(dqkv, n1, "km,kn->mn").astype(BF).reshape(3, D, D)
    sums = jnp.sum(dqkv, axis=0, dtype=F32)
    d_n1 = mm(dqkv, wq)
    d_g1 = jnp.sum(jnp.where(real, d_n1 * xhat1, 0.0), axis=0)
    d_b1 = jnp.sum(jnp.where(real, d_n1, 0.0), axis=0)
    d_x = (d_middle + norm_back(d_n1, xhat1, r1, g1)).astype(BF)
    d_rel = d_rel.reshape(2, SEG, HEADS, HEAD_DIM).sum(axis=2)[:, :27][:, ::-1]

    few = (d_g1, d_b1, sums[:D], sums[2 * D:] + d_pad[0], d_rel.reshape(-1), d_proj_bias, d_g2, d_b2, d_up_bias, d_down_bias)
    sizes = [v.shape[0] for v in few]
    flat = jnp.concatenate(few)
    pad = -flat.shape[0] % 1024
    flat = jnp.pad(flat, (0, pad)).reshape(-1, 128)
    grads = (d_wq, d_wp, d_wu, d_wd)
    if direct:
        out3, dx3, oq, op, ou, od, flat = send_back(out, d_x, images, grads, flat)
    else:
        out3, dx3 = send_back(out, d_x, images)
        oq, op, ou, od = summed_weights(grads)
        flat = lax.psum(flat, ("fsdp", "ctx", "tp"))
    flat = flat.reshape(-1)
    parts, at = [], 0
    for size in sizes:
        parts.append(flat[at:at + size])
        at += size
    s_g1, s_b1, s_q, s_v, s_rel, s_proj, s_g2, s_b2, s_up, s_down = parts
    s_rel = s_rel.reshape(2, 27, HEAD_DIM)
    return (
        jnp.transpose(out3, (1, 0, 2)), jnp.transpose(dx3, (1, 0, 2)), s_g1, s_b1,
        jnp.transpose(oq, (0, 2, 1)), jnp.stack([s_q, s_v]), s_rel[0], s_rel[1],
        op, s_proj, s_g2, s_b2, ou, s_up, od, s_down,
    )


def solution(mesh):
    direct = mesh.shape["fsdp"] == 2
    rows = P(("ctx", "tp"), "fsdp", None)
    w_specs = (P(None, "fsdp", "tp"), P("tp", "fsdp"), P("fsdp", "tp"), P("tp", "fsdp"))
    return jax.shard_map(
        functools.partial(local, direct),
        mesh=mesh,
        in_specs=(rows, P(), P(), w_specs[0], P(), P(), P(), w_specs[1], P(), P(), P(), w_specs[2], P(), w_specs[3], P(), rows),
        out_specs=(rows, rows, P(), P(), w_specs[0], P(), P(), P(), w_specs[1], P(), P(), P(), w_specs[2], P(), w_specs[3], P()),
        check_vma=False,
    )
```

```python
import functools
import math

import jax
import jax.numpy as jnp
from jax import lax
from jax.experimental import pallas as pl
from jax.experimental.pallas import tpu as pltpu
from jax.sharding import PartitionSpec as P

HEAD_DIM = 64
HEADS = 12
WIN = 14
SIDE = 64
BANDS = 4
PAIRS = 7
D = 768
EPSILON = 1e-06
MESH = pl.DeviceIdType.MESH
BF = jnp.bfloat16
F32 = jnp.float32

FULL = 224
PART = 128
NFULL = 3
NPART = 2
PBASE = NFULL * FULL
ROWS = PBASE + NPART * PART
PIECE = 144
GROUPS = 3
SEG = 32
MASKED = -1e9
VMEM_LIMIT = 60 * 2**20


def coords():
    return lax.axis_index("fsdp"), lax.axis_index("ctx"), lax.axis_index("tp")


def part_kind(ctx, tp, k, images):
    return (3 - ctx) * 8 + tp * 2 + k


def pack_matrix():
    row = lax.broadcasted_iota(jnp.int32, (PIECE, 128), 0)
    col = lax.broadcasted_iota(jnp.int32, (PIECE, 128), 1)
    wide = row < 128
    c = jnp.where(wide, row // 32, 4)
    u = jnp.where(wide, (row % 32) // 16, (row - 128) // 8)
    b = jnp.where(wide, row % 16, (row - 128) % 8)
    source = u * SIDE + c * WIN + b
    return ((source == col) & (b < WIN)).astype(BF)


def piece_places(ctx, tp, images):
    dev = ctx * 4 + tp
    out = []
    for i in range(images):
        for u in range(2):
            m = dev * 2 + u
            band = m // PAIRS
            p = m % PAIRS
            low = band == BANDS
            for c in range(5):
                q_low = i * 5 + c
                if c < 4:
                    f = i * 4 + c
                    d_ctx = jnp.where(low, 3 - q_low // 8, band)
                    d_tp = jnp.where(low, (q_low % 8) // 2, f // 3)
                    slot = jnp.where(low, NFULL + q_low % 2, f % 3)
                    d_row = jnp.where(low, PBASE + (q_low % 2) * PART, (f % 3) * FULL) + p * 32
                    out.append((i, u, c, d_ctx, d_tp, d_row, slot, p))
                else:
                    q = jnp.where(low, q_low, 15 + (3 - band) * 3 + i)
                    d_ctx = 3 - q // 8
                    d_tp = (q % 8) // 2
                    d_row = PBASE + (q % 2) * PART + p * 16
                    out.append((i, u, c, d_ctx, d_tp, d_row, NFULL + q % 2, p))
    return out


def window_places(ctx, tp):
    out = []
    for k in range(NFULL):
        f = tp * 3 + k
        for p in range(PAIRS):
            m = ctx * PAIRS + p
            dev = m // 2
            out.append((k, p, 32, None, f // 4, m % 2, f % 4, dev // 4, dev % 4, k * FULL + p * 32))
    for k in range(NPART):
        q = (3 - ctx) * 8 + tp * 2 + k
        bottom = q < 15
        corner = bottom & (q % 5 == 4)
        right = (q >= 15) & (q < 27)
        qr = jnp.where(right, q - 15, 0)
        band = jnp.where(bottom, BANDS, 3 - qr // 3)
        image = jnp.where(bottom, q // 5, qr % 3)
        base = PBASE + k * PART
        for p in range(PAIRS):
            m = band * PAIRS + p
            dev = jnp.minimum(m // 2, 15)
            place = (image, m % 2, dev // 4, dev % 4)
            if p < 4:
                wide = bottom & jnp.logical_not(corner)
                out.append((NFULL + k, p, 32, wide, image, m % 2, q % 5, dev // 4, dev % 4, base + p * 32))
            narrow = (corner | right) if p < 4 else right
            out.append((NFULL + k, p, 16, narrow, image, m % 2, 4, dev // 4, dev % 4, base + p * 16))
    return out


def group_barrier(extra=()):
    f, c, t = coords()
    sem = pltpu.get_barrier_semaphore()
    count = 0
    for dc in range(4):
        for dt in range(4):
            if dc == 0 and dt == 0:
                continue
            pl.semaphore_signal(sem, inc=1, device_id=(f, (c + dc) % 4, (t + dt) % 4), device_id_type=MESH)
            count += 1
    for dest in extra:
        pl.semaphore_signal(sem, inc=1, device_id=dest, device_id_type=MESH)
        count += 1
    pl.semaphore_wait(sem, count)


def send_or_copy(src, dst, dest, me, send_sem, recv_sem):
    (d_ctx, d_tp), (f, ctx, tp) = dest, me
    here = (d_ctx == ctx) & (d_tp == tp)

    @pl.when(here)
    def _():
        pltpu.make_async_copy(src, dst, recv_sem).start()

    @pl.when(jnp.logical_not(here))
    def _():
        pltpu.make_async_remote_copy(
            src_ref=src, dst_ref=dst, send_sem=send_sem, recv_sem=recv_sem,
            device_id=(f, d_ctx, d_tp), device_id_type=MESH,
        ).start()


def wait_sent(src, dest, me, send_sem):
    (d_ctx, d_tp), (f, ctx, tp) = dest, me
    away = jnp.logical_not((d_ctx == ctx) & (d_tp == tp))

    @pl.when(away)
    def _():
        pltpu.make_async_copy(src, src, send_sem).wait()


def start_pieces(stage, out, a, images, me, ss, rs):
    _, ctx, tp = me
    for n, (i, u, c, d_ctx, d_tp, d_row, slot, p) in enumerate(piece_places(ctx, tp, images)):
        rows = 32 if c < 4 else 16
        src = stage.at[a, i, u, pl.ds(c * 32, rows)]
        dst = out.at[pl.ds(pl.multiple_of(d_row, 16), rows)]
        send_or_copy(src, dst, (d_ctx, d_tp), me, ss.at[a, n], rs.at[a, slot, p])


def finish_piece_sends(stage, a, images, me, ss):
    _, ctx, tp = me
    for n, (i, u, c, d_ctx, d_tp, d_row, slot, p) in enumerate(piece_places(ctx, tp, images)):
        rows = 32 if c < 4 else 16
        wait_sent(stage.at[a, i, u, pl.ds(c * 32, rows)], (d_ctx, d_tp), me, ss.at[a, n])


def wait_pieces(out, a, me, rs):
    _, ctx, tp = me
    for slot, p, rows, exists, *_rest, row in window_places(ctx, tp):
        dst = out.at[pl.ds(row, rows)]
        wait = pltpu.make_async_copy(dst, dst, rs.at[a, slot, p]).wait
        if exists is None:
            wait()
        else:
            pl.when(exists)(wait)


UNITS = 6
BLOCKS = ((192, 384), (192, 384), (192, 384), (192, 384), (384, 768), (768, 384))
OVER_Y = (0, 0, 0, 0, 96, 192)


def block(ref, w, t, f, part=None):
    rows, cols = BLOCKS[w]
    row_at, col_at = (f, t) if w == 4 else (t, f)
    start, size = part if part is not None else (0, rows)
    return ref.at[
        pl.ds(pl.multiple_of(row_at * rows + start, 16), size),
        pl.ds(pl.multiple_of(col_at * cols, 128), cols),
    ]


def remote(src, dst, dest, send_sem, recv_sem):
    return pltpu.make_async_remote_copy(
        src_ref=src, dst_ref=dst, send_sem=send_sem, recv_sem=recv_sem, device_id=dest, device_id_type=MESH
    )


class Gather:
    def __init__(self, shards, wholes, me, ss, rs, ls):
        self.shards, self.wholes = shards, wholes
        self.ss, self.rs, self.ls = ss, rs, ls
        f, c, t = me
        self.me = me
        self.g, self.y, self.s = 1 - f, (t + 2) % 4, t + 1 - 2 * (t % 2)
        self.to_x, self.to_y, self.to_s = (self.g, c, t), (f, c, self.y), (f, c, self.s)

    def copies(self, w):
        a = OVER_Y[w]
        return [k for k in range(9) if a or k not in (3, 7)]

    def parts(self, w):
        a, rows = OVER_Y[w], BLOCKS[w][0]
        return (0, a), (a, rows - a)

    def copy(self, w, k):
        f, _, t = self.me
        g, y = self.g, self.y
        whole = self.wholes[w]
        first, second = self.parts(w)
        if k < 3:
            src, dst = self.shards[w], block(whole, w, t, f)
            dest = (self.to_x, self.to_y, self.to_s)[k]
        else:
            src = dst = block(whole, w, *(
                (t, g, first), (y, f, second), (t, g), (y, f), (y, g, first), (y, g, second)
            )[k - 3])
            dest = (self.to_y, self.to_x, self.to_s, self.to_s, self.to_s, self.to_s)[k - 3]
        return remote(src, dst, dest, self.ss.at[w, k], self.rs.at[w, k])

    def landed(self, w, k):
        f, _, t = self.me
        g, y, s = self.g, self.y, self.s
        sy = (s + 2) % 4
        first, second = self.parts(w)
        place = (
            (t, g), (y, f), (s, f), (y, g, first), (y, g, second),
            (s, g), (sy, f), (sy, g, first), (sy, g, second),
        )[k]
        return block(self.wholes[w], w, *place)

    def wait_recv(self, w, k):
        dst = self.landed(w, k)
        pltpu.make_async_copy(dst, dst, self.rs.at[w, k]).wait()

    def start_own(self, w, ks=(0, 1, 2)):
        f, _, t = self.me
        for k in ks:
            self.copy(w, k).start()
        if 2 in ks:
            pltpu.make_async_copy(self.shards[w], block(self.wholes[w], w, t, f), self.ls.at[w]).start()

    def forward_x(self, w):
        self.wait_recv(w, 0)
        if OVER_Y[w]:
            self.copy(w, 3).start()
        self.copy(w, 5).start()

    def forward_y(self, w):
        self.wait_recv(w, 1)
        self.copy(w, 4).start()
        self.copy(w, 6).start()

    def forward_second(self, w):
        if OVER_Y[w]:
            self.wait_recv(w, 3)
            self.copy(w, 7).start()
        self.wait_recv(w, 4)
        self.copy(w, 8).start()

    def arrived(self, w):
        f, _, t = self.me
        for k in (2, 5, 6, 7, 8):
            if k in self.copies(w):
                self.wait_recv(w, k)
        pltpu.make_async_copy(self.shards[w], block(self.wholes[w], w, t, f), self.ls.at[w]).wait()

    def sent(self, w):
        for k in self.copies(w):
            src = self.landed(w, k)
            pltpu.make_async_copy(src, src, self.ss.at[w, k]).wait()


def part_facts(k):
    _, ctx, tp = coords()
    q = (3 - ctx) * 8 + tp * 2 + k
    bottom = q < 15
    corner = bottom & (q % 5 == 4)
    right = (q >= 15) & (q < 27)
    return bottom, corner, right


def row_real(slot, rows):
    r = lax.broadcasted_iota(jnp.int32, (rows, 1), 0)
    wide = (r % 16) < WIN
    if slot < NFULL:
        return wide
    bottom, corner, right = part_facts(slot - NFULL)
    limit = jnp.where(corner, 64, jnp.where(right, 112, jnp.where(bottom, PART, 0)))
    narrow = jnp.where(corner | right, 1, 0)
    return (r < limit) & (wide | (narrow > 0))


def key_places(kind, shape):
    r = lax.broadcasted_iota(jnp.int32, shape, 0)
    a, b = r // 16, r % 16
    if kind == 0:
        return a, b
    _, corner, right = part_facts(kind - 1)
    corner, right = jnp.where(corner, 1, 0), jnp.where(right, 1, 0)
    a_right = jnp.where(r < 112, r // 8, (r - 112) // 8)
    b_right = jnp.where(r < 112, r % 8, 8 + (r - 112) % 8)
    a_corner = jnp.where(r < 64, r // 8, jnp.where(r < 128, (r - 64) // 8, 8 + (r - 128) // 16))
    b_corner = jnp.where(r < 64, r % 8, jnp.where(r < 128, 8 + (r - 64) % 8, (r - 128) % 16))
    a = jnp.where(corner > 0, a_corner, jnp.where(right > 0, a_right, a))
    b = jnp.where(corner > 0, b_corner, jnp.where(right > 0, b_right, b))
    return a, b


def build_keys(e_ref):
    shape = (FULL, 128)
    col = lax.broadcasted_iota(jnp.int32, shape, 1)
    j = col % 16
    for kind in range(1 + NPART):
        a, b = key_places(kind, shape)
        ok = b < WIN
        along_a = jnp.where(ok & (j == a) & (j < WIN), 1.0, 0.0)
        along_a = jnp.where(jnp.logical_not(ok) & (col % SEG == 15), MASKED, along_a)
        along_b = jnp.where(ok & (j == b) & (j < WIN), 1.0, 0.0)
        for head in range(4):
            mine = col // SEG == head
            e_ref[kind, head, :, pl.ds(0, 128)] = jnp.where(mine, along_a, 0.0).astype(BF)
            e_ref[kind, head, :, pl.ds(128, 128)] = jnp.where(mine, along_b, 0.0).astype(BF)


def build_relative(rel_ref, out_ref):
    out_ref[...] = jnp.zeros((D, D), BF)
    i = lax.broadcasted_iota(jnp.int32, (SEG, 128), 0)
    lane = lax.broadcasted_iota(jnp.int32, (SEG, 128), 1)
    turn = (lane % SEG == 26 - i).astype(BF)
    lane64 = lax.broadcasted_iota(jnp.int32, (HEAD_DIM, 128), 1) // SEG
    for axis in range(2):
        rev = tn(rel_ref[axis], turn)
        for h in range(HEADS):
            out_ref[pl.ds(h * HEAD_DIM, HEAD_DIM), pl.ds(axis * 384 + (h // 4) * 128, 128)] = (
                jnp.where(lane64 == h % 4, rev, 0.0).astype(BF)
            )


def slots():
    return [(k, k * FULL, FULL) for k in range(NFULL)] + [
        (NFULL + k, PBASE + k * PART, PART) for k in range(NPART)
    ]


def forward_kernel(images, direct, *refs):
    if direct:
        (x_ref, c_ref, wq_s, wp_s, wu_s, wd_s, vec, rel_ref,
         x_o, c_o, n1_o, qkv_o, att_o, p_o, wq_o, wp, wu, wd, e_o, rel_o,
         stage, xw, cw, n1, qkv, att, p_buf, wq, e, rel_cols, x_scr, bias_v, ss, rs, gss, grs, gls, os) = refs
    else:
        (x_ref, c_ref, wq_s, vec, rel_ref,
         x_o, c_o, n1_o, qkv_o, att_o, p_o, e_o, rel_o,
         stage, xw, cw, n1, qkv, att, p_buf, wq, e, rel_cols, x_scr, bias_v, ss, rs, os) = refs
    me = coords()
    f, ctx, tp = me
    group_barrier(((1 - f, ctx, tp),) if direct else ())
    pack = pack_matrix()

    def stage_tokens(a, src):
        for i in range(images):
            for u in range(2):
                stage[a, i, u] = jnp.dot(
                    pack, src[i, pl.ds(u * 128, 128)], preferred_element_type=F32
                ).astype(BF)

    out_copies = []

    def write(src, dst):
        cp = pltpu.make_async_copy(src, dst, os.at[len(out_copies)])
        cp.start()
        out_copies.append(cp)

    if direct:
        shards = (wq_s.at[0], wq_s.at[1], wq_s.at[2], wp_s, wu_s, wd_s)
        gather = Gather(shards, (wq.at[0], wq.at[1], wq.at[2], wp, wu, wd), me, gss, grs, gls)
        for w in range(3):
            gather.start_own(w)
    else:
        load = pltpu.make_async_copy(wq_s, wq, os.at[15])
        load.start()
    stage_tokens(0, x_ref)
    start_pieces(stage, xw, 0, images, me, ss, rs)
    build_keys(e)
    build_relative(rel_ref, rel_cols)
    write(e, e_o)
    write(rel_cols, rel_o)
    stage_tokens(1, c_ref)
    if direct:
        for w in range(3):
            gather.forward_x(w)
            gather.forward_y(w)
        gather.start_own(3)
        gather.start_own(4)
    wait_pieces(xw, 0, me, rs)
    for slot, base, rows in slots():
        here = pl.ds(base, rows)
        real = row_real(slot, rows)
        x = jnp.where(real, xw[here].astype(F32), 0.0)
        xw[here] = x.astype(BF)
        mean = jnp.mean(x, axis=-1, keepdims=True)
        centered = x - mean
        r = lax.rsqrt(jnp.mean(centered * centered, axis=-1, keepdims=True) + EPSILON)
        n1[here] = jnp.where(
            real, centered * r * vec[pl.ds(0, 1), pl.ds(0, D)] + vec[pl.ds(1, 1), pl.ds(0, D)], 0.0
        ).astype(BF)
    write(xw, x_o)
    write(n1, n1_o)
    if direct:
        for w in range(3):
            gather.forward_second(w)
        gather.start_own(5)
        start_pieces(stage, cw, 1, images, me, ss, rs)
        for w in range(3):
            gather.arrived(w)
        write(wq, wq_o)
    else:
        load.wait()
        start_pieces(stage, cw, 1, images, me, ss, rs)

    @pl.loop(0, 6)
    def _(n):
        cols = pl.ds(pl.multiple_of((n % 2) * 384, 128), 384)
        out = nt(n1[...], wq[n // 2, cols, :])
        there = pl.ds(pl.multiple_of(n * 384, 128), 384)
        qkv[:, there] = (out + vec[pl.ds(2, 1), there]).astype(BF)

    write(qkv, qkv_o)
    bias_v[...] = vec[pl.ds(2, 1), pl.ds(2 * D, D)]

    @pl.loop(0, NFULL)
    def _(n):
        attention_slot(qkv, rel_cols, bias_v, e.at[0], att, p_buf, pl.multiple_of(n * FULL, 16), FULL, None, x_scr)
        if direct:
            @pl.when(n == 0)
            def _():
                gather.forward_x(3)
                gather.forward_y(3)
                gather.forward_x(4)
                gather.forward_y(4)

            @pl.when(n == 1)
            def _():
                gather.forward_second(3)
                gather.forward_x(5)
                gather.forward_y(5)

            @pl.when(n == 2)
            def _():
                gather.forward_second(4)

    @pl.loop(0, NPART)
    def _(n):
        attention_slot(qkv, rel_cols, bias_v, e.at[1 + n], att, p_buf,
                       pl.multiple_of(PBASE + n * PART, 16), PART, narrow_flag(n), x_scr)

    write(att, att_o)
    write(p_buf, p_o)
    if direct:
        gather.forward_second(5)
    wait_pieces(cw, 1, me, rs)
    for slot, base, rows in slots():
        here = pl.ds(base, rows)
        cw[here] = jnp.where(row_real(slot, rows), cw[here].astype(F32), 0.0).astype(BF)
    write(cw, c_o)
    if direct:
        for w in range(3, UNITS):
            gather.arrived(w)
        for w in range(UNITS):
            gather.sent(w)
    for a in range(2):
        finish_piece_sends(stage, a, images, me, ss)
    for cp in out_copies:
        cp.wait()


def forward(x3, c3, shards, wq_whole, vec, rel):
    images = x3.shape[0]
    any_spec = pl.BlockSpec(memory_space=pl.ANY)
    vmem = pl.BlockSpec(memory_space=pltpu.VMEM)
    direct = wq_whole is None
    dma = pltpu.SemaphoreType.DMA
    shape = jax.ShapeDtypeStruct
    tokens = shape((ROWS, D), BF)
    outs = [tokens, tokens, tokens, shape((ROWS, 3 * D), BF), tokens, shape((ROWS, HEADS * 256), BF)]
    if direct:
        outs += [shape(s, BF) for s in ((3, D, D), (D, D), (D, 4 * D), (4 * D, D))]
    outs += [shape((1 + NPART, 4, FULL, 256), BF), shape((D, D), BF)]
    scratch = [
        pltpu.VMEM((2, images, 2, PIECE, D), BF),
        pltpu.VMEM((ROWS, D), BF), pltpu.VMEM((ROWS, D), BF), pltpu.VMEM((ROWS, D), BF),
        pltpu.VMEM((ROWS, 3 * D), BF), pltpu.VMEM((ROWS, D), BF), pltpu.VMEM((ROWS, HEADS * 256), BF),
        pltpu.VMEM((3, D, D), BF), pltpu.VMEM((1 + NPART, 4, FULL, 256), BF), pltpu.VMEM((D, D), BF),
        pltpu.VMEM((FULL, GROUPS * 256), BF), pltpu.VMEM((1, D), F32),
        dma((2, images * 10)), dma((2, NFULL + NPART, PAIRS)),
    ]
    if direct:
        scratch += [dma((UNITS, 9)), dma((UNITS, 9)), dma((UNITS,))]
    scratch += [dma((16,))]
    weights = list(shards) if direct else [wq_whole]
    return pl.pallas_call(
        functools.partial(forward_kernel, images, direct),
        out_shape=outs,
        in_specs=[vmem, vmem] + [any_spec] * len(weights) + [vmem, vmem],
        out_specs=[any_spec] * len(outs),
        scratch_shapes=scratch,
        compiler_params=pltpu.CompilerParams(
            collective_id=0, has_side_effects=True, vmem_limit_bytes=VMEM_LIMIT
        ),
        name="forward_attention",
    )(x3, c3, *weights, vec, rel)


def grad_block(ref, w, t, f, part=None):
    rows, cols = ((192, 384), (192, 384), (384, 768), (768, 384))[w]
    row_at, col_at = (f, t) if w == 2 else (t, f)
    start, size = row_at * rows, rows
    if part is not None:
        size = rows // 2
        start = start + part * size
    row_slice = pl.ds(pl.multiple_of(start, 16), size)
    col_slice = pl.ds(pl.multiple_of(col_at * cols, 128), cols)
    if w == 0:
        return ref.at[:, row_slice, col_slice]
    return ref.at[row_slice, col_slice]


def add_rows(dst, src, rows, cols):
    size = 96 if rows % 96 == 0 else 64

    @pl.loop(0, rows // size)
    def _(n):
        here = pl.ds(pl.multiple_of(n * size, 16), size)
        dst[here] = (dst[here].astype(F32) + src[here].astype(F32)).astype(BF)


def add_view(dst, src, w):
    if w == 0:
        for k in range(3):
            view = dst.at[k]
            add_rows(view, src.at[k], view.shape[0], view.shape[1])
    else:
        add_rows(dst, src, dst.shape[0], dst.shape[1])


def copy_f32(dst, src, w):
    if w == 0:
        for k in range(3):
            copy_f32(dst.at[k], src.at[k], 1)
        return
    rows = dst.shape[0]
    size = 96 if rows % 96 == 0 else 64

    @pl.loop(0, rows // size)
    def _(n):
        here = pl.ds(pl.multiple_of(n * size, 16), size)
        dst[here] = src[here].astype(F32)


HALF_SHAPES = ((3, 96, 384), (96, 384), (192, 768), (384, 384))
SHARD_SHAPES = ((3, 192, 384), (192, 384), (384, 768), (768, 384))


def reduce_kernel(images, with_weights, *refs):
    if with_weights:
        (y_ref, g_ref, gq, gp, gu, gd, few_ref, y_out, g_out, oq, op, ou, od, few_out,
         stage, ss, rs, r1q, r1p, r1u, r1d, raq, rap, rau, rad, rzq, rzp, rzu, rzd,
         few_in, s1, v1, s2, v2, s3, v3, fs, fr) = refs
    else:
        y_ref, g_ref, y_out, g_out, stage, ss, rs = refs
    me = coords()
    f, ctx, tp = me
    group_barrier(((1 - f, ctx, tp),) if with_weights else ())

    places = window_places(ctx, tp)
    pairs = ((y_ref, y_out), (g_ref, g_out))
    for a, (src_ref, _) in enumerate(pairs):
        for n, (slot, p, rows, exists, image, u, c, d_ctx, d_tp, row) in enumerate(places):
            def go(a=a, n=n, rows=rows, image=image, u=u, c=c, d_ctx=d_ctx, d_tp=d_tp, row=row, src_ref=src_ref):
                src = src_ref.at[pl.ds(row, rows)]
                dst = stage.at[a, image, u, pl.ds(pl.multiple_of(c * 32, 16), rows)]
                send_or_copy(src, dst, (d_ctx, d_tp), me, ss.at[a, n], rs.at[a, image, u, c])
            if exists is None:
                go()
            else:
                pl.when(exists)(go)

    if with_weights:
        grads = (gq, gp, gu, gd)
        outs = (oq, op, ou, od)
        r1, ra, rz = (r1q, r1p, r1u, r1d), (raq, rap, rau, rad), (rzq, rzp, rzu, rzd)
        g, y, s = 1 - f, (tp + 2) % 4, tp + 1 - 2 * (tp % 2)
        sy = (s + 2) % 4
        to_x, to_y, to_s = (g, ctx, tp), (f, ctx, y), (f, ctx, s)
        order = (3, 2, 1, 0)
        waits = []

        def send(src, dst, dest, send_sem, recv_sem):
            cp = remote(src, dst, dest, send_sem, recv_sem)
            cp.start()
            waits.append(cp)
            return cp

        few_out[...] = few_ref[...]
        few_steps = (to_s, to_x, to_y, (f, ctx + 1 - 2 * (ctx % 2), tp), (f, (ctx + 2) % 4, tp))

        def few_start(n):
            few_in[5 + n] = few_out[...]
            return send(few_in.at[5 + n], few_in.at[n], few_steps[n], fs.at[n], fr.at[n])

        def few_finish(cp, n):
            cp.wait_recv()
            few_out[...] = few_out[...] + few_in[n]

        first = {}
        for w in order:
            for n, t_there in enumerate((s, sy)):
                for h in range(2):
                    first[w, n, h] = send(
                        grad_block(grads[w], w, t_there, h), r1[w].at[n, h], to_s, s1.at[w, n, h], v1.at[w, n, h]
                    )
        few = few_start(0)

        phase1 = {}
        for w in order:
            for n, t_here in enumerate((tp, y)):
                for h in range(2):
                    first[w, n, h].wait_recv()
                    add_view(grad_block(grads[w], w, t_here, h), r1[w].at[n, h], w)
            phase1[w] = (
                send(grad_block(grads[w], w, tp, g, 0), ra[w].at[0], to_x, s2.at[w, 0], v2.at[w, 0]),
                send(grad_block(grads[w], w, y, g, 0), ra[w].at[1], to_x, s2.at[w, 1], v2.at[w, 1]),
                send(grad_block(grads[w], w, y, f, 1), ra[w].at[2], to_y, s2.at[w, 2], v2.at[w, 2]),
                send(grad_block(grads[w], w, y, g, 1), ra[w].at[3], to_y, s2.at[w, 3], v2.at[w, 3]),
            )
        few_finish(few, 0)
        few = few_start(1)
        phase2 = {}
        for w in order:
            views = (
                grad_block(grads[w], w, tp, f, 0), grad_block(grads[w], w, y, f, 0),
                grad_block(grads[w], w, tp, f, 1), grad_block(grads[w], w, tp, g, 1),
            )
            for k in range(4):
                phase1[w][k].wait_recv()
                add_view(views[k], ra[w].at[k], w)
            phase2[w] = (
                send(grad_block(grads[w], w, y, f, 0), ra[w].at[4], to_y, s2.at[w, 4], v2.at[w, 4]),
                send(grad_block(grads[w], w, tp, g, 1), ra[w].at[5], to_x, s2.at[w, 5], v2.at[w, 5]),
            )
        few_finish(few, 1)
        few = few_start(2)

        outer = (ctx == 0) | (ctx == 3)
        inner = jnp.logical_not(outer)
        mid_peer = (f, 3 - ctx, tp)
        in_peer = (f, jnp.where(ctx == 0, 1, 2), tp)
        out_peer = (f, jnp.where(ctx == 1, 0, 3), tp)
        for w in order:
            for k in range(2):
                phase2[w][k].wait_recv()
                add_view(grad_block(grads[w], w, tp, f, k), ra[w].at[4 + k], w)
            mine = grad_block(grads[w], w, tp, f)

            @pl.when(outer)
            def _(w=w, mine=mine):
                remote(mine, rz[w].at[0], in_peer, s3.at[w, 0], v3.at[w, 0]).start()
        for w in order:
            mine = grad_block(grads[w], w, tp, f)

            @pl.when(inner)
            def _(w=w, mine=mine):
                pltpu.make_async_copy(rz[w].at[0], rz[w].at[0], v3.at[w, 0]).wait()
                add_view(mine, rz[w].at[0], w)
                remote(mine, rz[w].at[1], mid_peer, s3.at[w, 0], v3.at[w, 1]).start()
        for w in order:
            mine = grad_block(grads[w], w, tp, f)

            @pl.when(inner)
            def _(w=w, mine=mine):
                pltpu.make_async_copy(rz[w].at[1], rz[w].at[1], v3.at[w, 1]).wait()
                add_view(rz[w].at[1], mine, w)
                remote(rz[w].at[1], rz[w].at[2], out_peer, s3.at[w, 1], v3.at[w, 2]).start()
                copy_f32(outs[w], rz[w].at[1], w)
        few_finish(few, 2)
        few = few_start(3)
        for w in order:
            @pl.when(outer)
            def _(w=w):
                pltpu.make_async_copy(rz[w].at[2], rz[w].at[2], v3.at[w, 2]).wait()
                copy_f32(outs[w], rz[w].at[2], w)
        few_finish(few, 3)
        few = few_start(4)
        few_finish(few, 4)

        for cp in waits:
            cp.wait_send()
        for w in order:
            one = rz[w].at[0]
            pltpu.make_async_copy(one, one, s3.at[w, 0]).wait()

            @pl.when(inner)
            def _(one=one, w=w):
                pltpu.make_async_copy(one, one, s3.at[w, 1]).wait()

    unpack = pack_matrix()
    for a, (src_ref, out_ref) in enumerate(pairs):
        for i in range(images):
            for u in range(2):
                for c in range(5):
                    rows = 32 if c < 4 else 16
                    dst = stage.at[a, i, u, pl.ds(c * 32, rows)]
                    pltpu.make_async_copy(dst, dst, rs.at[a, i, u, c]).wait()
                out_ref[i, pl.ds(u * 128, 128)] = lax.dot_general(
                    unpack, stage[a, i, u], (((0,), (0,)), ((), ())), preferred_element_type=F32
                ).astype(BF)
        for n, (slot, p, rows, exists, image, u, c, d_ctx, d_tp, row) in enumerate(places):
            def done(a=a, n=n, rows=rows, d_ctx=d_ctx, d_tp=d_tp, row=row, src_ref=src_ref):
                wait_sent(src_ref.at[pl.ds(row, rows)], (d_ctx, d_tp), me, ss.at[a, n])
            if exists is None:
                done()
            else:
                pl.when(exists)(done)


def send_back(y, g, images, grads=None, few=None):
    vmem = pl.BlockSpec(memory_space=pltpu.VMEM)
    with_weights = grads is not None
    n_places = NFULL * PAIRS + NPART * (4 + PAIRS)
    token = jax.ShapeDtypeStruct((images, 256, D), BF)
    out_shape = [token, token]
    args = [y, g]
    dma = pltpu.SemaphoreType.DMA
    scratch = [
        pltpu.VMEM((2, images, 2, PIECE, D), BF),
        dma((2, n_places)),
        dma((2, images, 2, 5)),
    ]
    if with_weights:
        args += list(grads) + [few]
        out_shape += [jax.ShapeDtypeStruct(s, F32) for s in SHARD_SHAPES]
        out_shape += [jax.ShapeDtypeStruct(few.shape, F32)]
        scratch += [pltpu.VMEM((2, 2) + s, BF) for s in SHARD_SHAPES]
        scratch += [pltpu.VMEM((6,) + s, BF) for s in HALF_SHAPES]
        scratch += [pltpu.VMEM((3,) + s, BF) for s in SHARD_SHAPES]
        scratch += [pltpu.VMEM((10,) + few.shape, F32)]
        scratch += [dma((4, 2, 2)), dma((4, 2, 2)), dma((4, 6)), dma((4, 6)), dma((4, 2)), dma((4, 3)), dma((5,)), dma((5,))]
    return pl.pallas_call(
        functools.partial(reduce_kernel, images, with_weights),
        out_shape=out_shape,
        in_specs=[vmem] * len(args),
        out_specs=[vmem] * len(out_shape),
        scratch_shapes=scratch,
        compiler_params=pltpu.CompilerParams(
            collective_id=1, has_side_effects=True, vmem_limit_bytes=VMEM_LIMIT
        ),
        name="tokens_and_gradients_out",
    )(*args)


def barrel(x, shift, left):
    lanes = x.shape[-1]
    for bit in (1, 2, 4, 8):
        moved = pltpu.roll(x, lanes - bit if left else bit, 1)
        x = jnp.where((shift // bit) % 2 == 1, moved, x)
    return x


def row_places(rows, narrow):
    r = lax.broadcasted_iota(jnp.int32, (rows, 128), 0)
    if narrow is None:
        return r // 16, r % 16
    is_narrow = narrow > 0
    return jnp.where(is_narrow, r // 8, r // 16), jnp.where(is_narrow, r % 8, r % 16)


def half_mask(hh):
    lane = lax.broadcasted_iota(jnp.int32, (1, 128), 1)
    return ((lane // 64) == hh).astype(BF)


def nt(a, b):
    return lax.dot_general(a, b, (((1,), (1,)), ((), ())), preferred_element_type=F32)


def tn(a, b):
    return lax.dot_general(a, b, (((0,), (0,)), ((), ())), preferred_element_type=F32)


def key_rows(ref, base, rows, col, fill):
    part = ref[pl.ds(base, rows), pl.ds(col, 128)]
    if rows == FULL:
        return part
    return jnp.concatenate([part, jnp.broadcast_to(fill, (FULL - rows, 128)).astype(BF)], axis=0)


def attention_slot(qkv, rel_cols, bias_v, e_at, o_ref, p_ref, base, rows, narrow, x_scr):
    a_row, b_row = row_places(rows, narrow)
    q_all = qkv[pl.ds(base, rows), pl.ds(0, D)]
    lane = lax.broadcasted_iota(jnp.int32, (rows, 128), 1) % SEG
    for axis, pos in ((0, a_row), (1, b_row)):
        raw = jnp.dot(q_all, rel_cols[:, pl.ds(axis * 384, 384)], preferred_element_type=F32)
        for g in range(GROUPS):
            v = barrel(raw[:, g * 128:(g + 1) * 128], jnp.maximum(13 - pos, 0), True)
            hi = v.astype(BF).astype(F32)
            lo = pltpu.roll(v - hi, 16, 1)
            mix = jnp.where(lane < WIN, hi, jnp.where(lane >= 16, lo, 0.0))
            if axis == 0:
                mix = jnp.where(lane == 15, 1.0, mix)
            x_scr[pl.ds(0, rows), pl.ds(g * 256 + axis * 128, 128)] = mix.astype(BF)
    for hp in range(6):
        q = q_all[:, hp * 128:(hp + 1) * 128]
        k = key_rows(qkv, base, rows, D + hp * 128, jnp.zeros((1, 128), BF))
        v = key_rows(qkv, base, rows, 2 * D + hp * 128, bias_v[:, pl.ds(hp * 128, 128)])
        out = jnp.zeros((rows, 128), F32)
        for hh in range(2):
            h = hp * 2 + hh
            x = x_scr[pl.ds(0, rows), pl.ds((h // 4) * 256, 256)]
            s = nt(q, k * (half_mask(hh) * 0.125)) + nt(x, e_at[h % 4])
            p = jnp.exp(s - jnp.max(s, axis=-1, keepdims=True))
            p = (p * (1.0 / jnp.sum(p, axis=-1, keepdims=True))).astype(BF)
            p_ref[pl.ds(base, rows), pl.ds(h * 256, FULL)] = p
            out = out + jnp.dot(p, v * half_mask(hh), preferred_element_type=F32)
        o_ref[pl.ds(base, rows), pl.ds(hp * 128, 128)] = out.astype(BF)


def narrow_flag(k):
    _, ctx, tp = coords()
    q = (3 - ctx) * 8 + tp * 2 + k
    is_narrow = ((q < 15) & (q % 5 == 4)) | ((q >= 15) & (q < 27))
    return jnp.where(is_narrow, 1, 0)


def attention_back_slot(qkv, do_ref, rel_cols, bias_v, e_at, p_ref, dqkv, d_scr, acc_scr, pad_acc,
                        rel_acc, base, rows, narrow):
    a_row, b_row = row_places(rows, narrow)
    for g in range(GROUPS):
        dx = jnp.zeros((rows, 256), F32)
        for hp in (2 * g, 2 * g + 1):
            q = qkv[pl.ds(base, rows), pl.ds(hp * 128, 128)]
            k = key_rows(qkv, base, rows, D + hp * 128, jnp.zeros((1, 128), BF))
            v = key_rows(qkv, base, rows, 2 * D + hp * 128, bias_v[:, pl.ds(hp * 128, 128)])
            do = do_ref[pl.ds(base, rows), pl.ds(hp * 128, 128)]
            dq = jnp.zeros((rows, 128), F32)
            dk = jnp.zeros((FULL, 128), F32)
            dv = jnp.zeros((FULL, 128), F32)
            for hh in range(2):
                h = hp * 2 + hh
                mask = half_mask(hh)
                do_m = do * mask
                dp = nt(do_m, v)
                p_low = p_ref[pl.ds(base, rows), pl.ds(h * 256, FULL)]
                t = p_low.astype(F32)
                tp = t * dp
                ds = (tp - t * jnp.sum(tp, axis=-1, keepdims=True)).astype(BF)
                dq = dq + jnp.dot(ds, k * (mask * 0.125), preferred_element_type=F32)
                dx = dx + jnp.dot(ds, e_at[h % 4], preferred_element_type=F32)
                dk = dk + tn(ds, q * (mask * 0.125))
                dv = dv + tn(p_low, do_m)
            acc_scr[pl.ds(0, rows), pl.ds(hp * 128, 128)] = dq
            dqkv[pl.ds(base, rows), pl.ds(D + hp * 128, 128)] = dk[:rows].astype(BF)
            dqkv[pl.ds(base, rows), pl.ds(2 * D + hp * 128, 128)] = dv[:rows].astype(BF)
            if rows < FULL:
                pad_acc[:, pl.ds(hp * 128, 128)] += jnp.sum(dv[rows:], axis=0, keepdims=True)
        lane = lax.broadcasted_iota(jnp.int32, (rows, 128), 1) % SEG
        for axis, pos in ((0, a_row), (1, b_row)):
            v = jnp.where(lane < WIN, dx[:, axis * 128:(axis + 1) * 128], 0.0)
            v = barrel(v, jnp.maximum(13 - pos, 0), False)
            d_scr[pl.ds(0, rows), pl.ds(axis * 384 + g * 128, 128)] = v.astype(BF)
    d = d_scr[pl.ds(0, rows), :]
    q_all = qkv[pl.ds(base, rows), pl.ds(0, D)]
    dq = acc_scr[pl.ds(0, rows), :] + nt(d, rel_cols[...])
    dqkv[pl.ds(base, rows), pl.ds(0, D)] = dq.astype(BF)
    rel_acc[...] += tn(d, q_all)


def attention_back_kernel(qkv, do_ref, rel_cols, bias_v, e_ref, p_ref, dqkv, pad_ref, rel_ref,
                          d_scr, acc_scr, rel_acc):
    pad_ref[...] = jnp.zeros_like(pad_ref)
    rel_acc[...] = jnp.zeros_like(rel_acc)

    @pl.loop(0, NFULL)
    def _(n):
        attention_back_slot(qkv, do_ref, rel_cols, bias_v, e_ref.at[0], p_ref, dqkv, d_scr, acc_scr, pad_ref,
                            rel_acc, pl.multiple_of(n * FULL, 16), FULL, None)

    @pl.loop(0, NPART)
    def _(n):
        attention_back_slot(qkv, do_ref, rel_cols, bias_v, e_ref.at[1 + n], p_ref, dqkv, d_scr, acc_scr, pad_ref,
                            rel_acc, pl.multiple_of(PBASE + n * PART, 16), PART, narrow_flag(n))

    lane = lax.broadcasted_iota(jnp.int32, (SEG, D), 1) // HEAD_DIM
    for axis in range(2):
        total = jnp.zeros((SEG, D), F32)
        for h in range(HEADS):
            total = total + jnp.where(lane == h, rel_acc[pl.ds(axis * 384 + h * SEG, SEG), :], 0.0)
        rel_ref[axis] = total


def attention_back(qkv, do, rel_cols, bias_v, e, p):
    vmem = pl.BlockSpec(memory_space=pltpu.VMEM)
    return pl.pallas_call(
        attention_back_kernel,
        out_shape=[
            jax.ShapeDtypeStruct((ROWS, 3 * D), BF),
            jax.ShapeDtypeStruct((1, D), F32),
            jax.ShapeDtypeStruct((2, SEG, D), F32),
        ],
        in_specs=[vmem] * 6,
        out_specs=[vmem] * 3,
        scratch_shapes=[
            pltpu.VMEM((FULL, D), BF),
            pltpu.VMEM((FULL, D), F32),
            pltpu.VMEM((D, D), F32),
        ],
        compiler_params=pltpu.CompilerParams(vmem_limit_bytes=VMEM_LIMIT),
        name="attention_backward",
    )(qkv, do, rel_cols, bias_v, e, p)


def real_rows():
    _, ctx, tp = coords()
    r = jnp.arange(FULL)
    real = [(r % 16) < WIN] * NFULL
    for k in range(NPART):
        q = (3 - ctx) * 8 + tp * 2 + k
        bottom = q < 15
        corner = bottom & (q % 5 == 4)
        right = (q >= 15) & (q < 27)
        rp = r[:PART]
        real.append(
            jnp.where(corner, rp < 64, jnp.where(right, rp < 112, bottom & (rp % 16 < WIN)))
        )
    return jnp.concatenate(real)[:, None]


def norm_stats(v):
    mean = jnp.mean(v, axis=-1, keepdims=True)
    centered = v - mean
    r = lax.rsqrt(jnp.mean(centered * centered, axis=-1, keepdims=True) + EPSILON)
    return centered * r, r


def norm_back(n, xhat, r, gain):
    m = n * gain
    return r * (m - jnp.mean(m, -1, keepdims=True) - xhat * jnp.mean(m * xhat, -1, keepdims=True))


def gelu_both(u):
    x = jnp.abs(u) * math.sqrt(0.5)
    t = 1.0 / (1.0 + 0.3275911 * x)
    e = jnp.exp(-0.5 * u * u)
    poly = t * (0.254829592 + t * (-0.284496736 + t * (1.421413741 + t * (-1.453152027 + t * 1.061405429))))
    tail = 0.5 * poly * e
    phi = jnp.where(u >= 0, 1.0 - tail, tail)
    return u * phi, phi + u * e * (1.0 / math.sqrt(2 * math.pi))


def mm(a, b, dims="mk,kn->mn"):
    return jnp.einsum(dims, a, b, preferred_element_type=F32)


def whole_weights(shards):
    wq, wp, wu, wd = shards
    wq = lax.all_gather(lax.all_gather(wq, "fsdp", axis=2, tiled=True), "tp", axis=1, tiled=True)
    wp = lax.all_gather(lax.all_gather(wp, "fsdp", axis=1, tiled=True), "tp", axis=0, tiled=True)
    wu = lax.all_gather(lax.all_gather(wu, "fsdp", axis=0, tiled=True), "tp", axis=1, tiled=True)
    wd = lax.all_gather(lax.all_gather(wd, "fsdp", axis=1, tiled=True), "tp", axis=0, tiled=True)
    return wq, wp, wu, wd


def summed_weights(grads):
    dims = ((1, 2), (0, 1), (1, 0), (0, 1))
    out = []
    for grad, (t_dim, f_dim) in zip(grads, dims):
        part = lax.psum_scatter(grad, "tp", scatter_dimension=t_dim, tiled=True)
        part = lax.psum_scatter(part, "fsdp", scatter_dimension=f_dim, tiled=True)
        out.append(lax.psum(part, "ctx").astype(F32))
    return out


def local(direct, block_input, ln1_gain, ln1_bias, w_qkv, qkv_bias, rel_h, rel_w, w_proj, proj_bias,
          ln2_gain, ln2_bias, w_up, up_bias, w_down, down_bias, cotangent):
    images = block_input.shape[1]
    x3 = jnp.transpose(block_input, (1, 0, 2))
    c3 = jnp.transpose(cotangent, (1, 0, 2))
    shards = (jnp.transpose(w_qkv, (0, 2, 1)), w_proj, w_up, w_down)
    zero = jnp.zeros_like(ln1_gain)
    bias_row = jnp.concatenate([qkv_bias[0], zero, qkv_bias[1]])
    vec = jnp.stack([jnp.tile(ln1_gain, 3), jnp.tile(ln1_bias, 3), bias_row]).astype(F32)
    rel = jnp.pad(jnp.stack([rel_h, rel_w]), ((0, 0), (0, SEG - rel_h.shape[0]), (0, 0)))
    if direct:
        x_low, cot_low, n1, qkv, attended, probs, wq, wp, wu, wd, e, rel_cols = forward(x3, c3, shards, None, vec, rel)
    else:
        wq, wp, wu, wd = whole_weights(shards)
        x_low, cot_low, n1, qkv, attended, probs, e, rel_cols = forward(x3, c3, None, wq, vec, rel)
    wq = wq.reshape(3 * D, D)
    real = real_rows()
    g1, g2, b2 = (v.astype(F32) for v in (ln1_gain, ln2_gain, ln2_bias))
    x, cot = x_low.astype(F32), cot_low.astype(F32)
    xhat1, r1 = norm_stats(x)
    middle = x + mm(attended, wp) + proj_bias.astype(F32)
    xhat2, r2 = norm_stats(middle)
    n2 = (xhat2 * g2 + b2).astype(BF)
    gate_in = mm(n2, wu) + up_bias.astype(F32)
    hidden, slope = gelu_both(gate_in)
    hidden = hidden.astype(BF)
    out = (middle + mm(hidden, wd) + down_bias.astype(F32)).astype(BF)

    d_down_bias = jnp.sum(cot, axis=0)
    d_wd = mm(hidden, cot_low, "km,kn->mn").astype(BF)
    d_gate = (mm(cot_low, wd, "mk,nk->mn") * slope).astype(BF)
    d_wu = mm(n2, d_gate, "km,kn->mn").astype(BF)
    d_up_bias = jnp.sum(d_gate, axis=0, dtype=F32)
    d_n2 = mm(d_gate, wu, "mk,nk->mn")
    d_g2 = jnp.sum(d_n2 * xhat2, axis=0)
    d_b2 = jnp.sum(d_n2, axis=0)
    d_middle = cot + norm_back(d_n2, xhat2, r2, g2)
    branch = d_middle.astype(BF)
    d_proj_bias = jnp.sum(branch, axis=0, dtype=F32)
    d_wp = mm(attended, branch, "km,kn->mn").astype(BF)
    d_att = mm(branch, wp, "mk,nk->mn").astype(BF)
    dqkv, d_pad, d_rel = attention_back(qkv, d_att, rel_cols, qkv_bias[1:2].astype(F32), e, probs)
    d_wq = mm(dqkv, n1, "km,kn->mn").astype(BF).reshape(3, D, D)
    sums = jnp.sum(dqkv, axis=0, dtype=F32)
    d_n1 = mm(dqkv, wq)
    d_g1 = jnp.sum(jnp.where(real, d_n1 * xhat1, 0.0), axis=0)
    d_b1 = jnp.sum(jnp.where(real, d_n1, 0.0), axis=0)
    d_x = (d_middle + norm_back(d_n1, xhat1, r1, g1)).astype(BF)
    d_rel = d_rel.reshape(2, SEG, HEADS, HEAD_DIM).sum(axis=2)[:, :27][:, ::-1]

    few = (d_g1, d_b1, sums[:D], sums[2 * D:] + d_pad[0], d_rel.reshape(-1), d_proj_bias, d_g2, d_b2, d_up_bias, d_down_bias)
    sizes = [v.shape[0] for v in few]
    flat = jnp.concatenate(few)
    pad = -flat.shape[0] % 1024
    flat = jnp.pad(flat, (0, pad)).reshape(-1, 128)
    grads = (d_wq, d_wp, d_wu, d_wd)
    if direct:
        out3, dx3, oq, op, ou, od, flat = send_back(out, d_x, images, grads, flat)
    else:
        out3, dx3 = send_back(out, d_x, images)
        oq, op, ou, od = summed_weights(grads)
        flat = lax.psum(flat, ("fsdp", "ctx", "tp"))
    flat = flat.reshape(-1)
    parts, at = [], 0
    for size in sizes:
        parts.append(flat[at:at + size])
        at += size
    s_g1, s_b1, s_q, s_v, s_rel, s_proj, s_g2, s_b2, s_up, s_down = parts
    s_rel = s_rel.reshape(2, 27, HEAD_DIM)
    return (
        jnp.transpose(out3, (1, 0, 2)), jnp.transpose(dx3, (1, 0, 2)), s_g1, s_b1,
        jnp.transpose(oq, (0, 2, 1)), jnp.stack([s_q, s_v]), s_rel[0], s_rel[1],
        op, s_proj, s_g2, s_b2, ou, s_up, od, s_down,
    )


def solution(mesh):
    direct = mesh.shape["fsdp"] == 2
    rows = P(("ctx", "tp"), "fsdp", None)
    w_specs = (P(None, "fsdp", "tp"), P("tp", "fsdp"), P("fsdp", "tp"), P("tp", "fsdp"))
    return jax.shard_map(
        functools.partial(local, direct),
        mesh=mesh,
        in_specs=(rows, P(), P(), w_specs[0], P(), P(), P(), w_specs[1], P(), P(), P(), w_specs[2], P(), w_specs[3], P(), rows),
        out_specs=(rows, rows, P(), P(), w_specs[0], P(), P(), P(), w_specs[1], P(), P(), P(), w_specs[2], P(), w_specs[3], P()),
        check_vma=False,
    )
```

```python
import functools
import math

import jax
import jax.numpy as jnp
from jax import lax
from jax.experimental import pallas as pl
from jax.experimental.pallas import tpu as pltpu
from jax.sharding import PartitionSpec as P

HEAD_DIM = 64
HEADS = 12
WIN = 14
SIDE = 64
BANDS = 4
PAIRS = 7
D = 768
EPSILON = 1e-06
MESH = pl.DeviceIdType.MESH
BF = jnp.bfloat16
F32 = jnp.float32

FULL = 224
PART = 128
NFULL = 3
NPART = 2
PBASE = NFULL * FULL
ROWS = PBASE + NPART * PART
PIECE = 144
GROUPS = 3
SEG = 32
MASKED = -1e9
VMEM_LIMIT = 60 * 2**20
VMEM_BACK = 63 * 2**20


def coords():
    return lax.axis_index("fsdp"), lax.axis_index("ctx"), lax.axis_index("tp")


def part_kind(ctx, tp, k, images):
    return (3 - ctx) * 8 + tp * 2 + k


def pack_matrix():
    row = lax.broadcasted_iota(jnp.int32, (PIECE, 128), 0)
    col = lax.broadcasted_iota(jnp.int32, (PIECE, 128), 1)
    wide = row < 128
    c = jnp.where(wide, row // 32, 4)
    u = jnp.where(wide, (row % 32) // 16, (row - 128) // 8)
    b = jnp.where(wide, row % 16, (row - 128) % 8)
    source = u * SIDE + c * WIN + b
    return ((source == col) & (b < WIN)).astype(BF)


def piece_places(ctx, tp, images):
    dev = ctx * 4 + tp
    out = []
    for i in range(images):
        for u in range(2):
            m = dev * 2 + u
            band = m // PAIRS
            p = m % PAIRS
            low = band == BANDS
            for c in range(5):
                q_low = i * 5 + c
                if c < 4:
                    f = i * 4 + c
                    d_ctx = jnp.where(low, 3 - q_low // 8, band)
                    d_tp = jnp.where(low, (q_low % 8) // 2, f // 3)
                    slot = jnp.where(low, NFULL + q_low % 2, f % 3)
                    d_row = jnp.where(low, PBASE + (q_low % 2) * PART, (f % 3) * FULL) + p * 32
                    out.append((i, u, c, d_ctx, d_tp, d_row, slot, p))
                else:
                    q = jnp.where(low, q_low, 15 + (3 - band) * 3 + i)
                    d_ctx = 3 - q // 8
                    d_tp = (q % 8) // 2
                    d_row = PBASE + (q % 2) * PART + p * 16
                    out.append((i, u, c, d_ctx, d_tp, d_row, NFULL + q % 2, p))
    return out


def window_places(ctx, tp):
    out = []
    for k in range(NFULL):
        f = tp * 3 + k
        for p in range(PAIRS):
            m = ctx * PAIRS + p
            dev = m // 2
            out.append((k, p, 32, None, f // 4, m % 2, f % 4, dev // 4, dev % 4, k * FULL + p * 32))
    for k in range(NPART):
        q = (3 - ctx) * 8 + tp * 2 + k
        bottom = q < 15
        corner = bottom & (q % 5 == 4)
        right = (q >= 15) & (q < 27)
        qr = jnp.where(right, q - 15, 0)
        band = jnp.where(bottom, BANDS, 3 - qr // 3)
        image = jnp.where(bottom, q // 5, qr % 3)
        base = PBASE + k * PART
        for p in range(PAIRS):
            m = band * PAIRS + p
            dev = jnp.minimum(m // 2, 15)
            place = (image, m % 2, dev // 4, dev % 4)
            if p < 4:
                wide = bottom & jnp.logical_not(corner)
                out.append((NFULL + k, p, 32, wide, image, m % 2, q % 5, dev // 4, dev % 4, base + p * 32))
            narrow = (corner | right) if p < 4 else right
            out.append((NFULL + k, p, 16, narrow, image, m % 2, 4, dev // 4, dev % 4, base + p * 16))
    return out


def group_barrier(extra=()):
    f, c, t = coords()
    sem = pltpu.get_barrier_semaphore()
    count = 0
    for dc in range(4):
        for dt in range(4):
            if dc == 0 and dt == 0:
                continue
            pl.semaphore_signal(sem, inc=1, device_id=(f, (c + dc) % 4, (t + dt) % 4), device_id_type=MESH)
            count += 1
    for dest in extra:
        pl.semaphore_signal(sem, inc=1, device_id=dest, device_id_type=MESH)
        count += 1
    pl.semaphore_wait(sem, count)


def send_or_copy(src, dst, dest, me, send_sem, recv_sem):
    (d_ctx, d_tp), (f, ctx, tp) = dest, me
    here = (d_ctx == ctx) & (d_tp == tp)

    @pl.when(here)
    def _():
        pltpu.make_async_copy(src, dst, recv_sem).start()

    @pl.when(jnp.logical_not(here))
    def _():
        pltpu.make_async_remote_copy(
            src_ref=src, dst_ref=dst, send_sem=send_sem, recv_sem=recv_sem,
            device_id=(f, d_ctx, d_tp), device_id_type=MESH,
        ).start()


def wait_sent(src, dest, me, send_sem):
    (d_ctx, d_tp), (f, ctx, tp) = dest, me
    away = jnp.logical_not((d_ctx == ctx) & (d_tp == tp))

    @pl.when(away)
    def _():
        pltpu.make_async_copy(src, src, send_sem).wait()


def start_pieces(stage, out, a, images, me, ss, rs):
    _, ctx, tp = me
    for n, (i, u, c, d_ctx, d_tp, d_row, slot, p) in enumerate(piece_places(ctx, tp, images)):
        rows = 32 if c < 4 else 16
        src = stage.at[a, i, u, pl.ds(c * 32, rows)]
        dst = out.at[pl.ds(pl.multiple_of(d_row, 16), rows)]
        send_or_copy(src, dst, (d_ctx, d_tp), me, ss.at[a, n], rs.at[a, slot, p])


def finish_piece_sends(stage, a, images, me, ss):
    _, ctx, tp = me
    for n, (i, u, c, d_ctx, d_tp, d_row, slot, p) in enumerate(piece_places(ctx, tp, images)):
        rows = 32 if c < 4 else 16
        wait_sent(stage.at[a, i, u, pl.ds(c * 32, rows)], (d_ctx, d_tp), me, ss.at[a, n])


def wait_pieces(out, a, me, rs):
    _, ctx, tp = me
    for slot, p, rows, exists, *_rest, row in window_places(ctx, tp):
        dst = out.at[pl.ds(row, rows)]
        wait = pltpu.make_async_copy(dst, dst, rs.at[a, slot, p]).wait
        if exists is None:
            wait()
        else:
            pl.when(exists)(wait)


UNITS = 6
BLOCKS = ((192, 384), (192, 384), (192, 384), (192, 384), (384, 768), (768, 384))
OVER_Y = (0, 0, 0, 0, 96, 192)


def block(ref, w, t, f, part=None):
    rows, cols = BLOCKS[w]
    start, size = part if part is not None else (0, rows)
    if w == 4:
        return ref.at[pl.ds(pl.multiple_of(t * D + f * rows + start, 16), size)]
    return ref.at[
        pl.ds(pl.multiple_of(t * rows + start, 16), size),
        pl.ds(pl.multiple_of(f * cols, 128), cols),
    ]


def remote(src, dst, dest, send_sem, recv_sem):
    return pltpu.make_async_remote_copy(
        src_ref=src, dst_ref=dst, send_sem=send_sem, recv_sem=recv_sem, device_id=dest, device_id_type=MESH
    )


class Gather:
    def __init__(self, shards, wholes, me, ss, rs, ls):
        self.shards, self.wholes = shards, wholes
        self.ss, self.rs, self.ls = ss, rs, ls
        f, c, t = me
        self.me = me
        self.g, self.y, self.s = 1 - f, (t + 2) % 4, t + 1 - 2 * (t % 2)
        self.to_x, self.to_y, self.to_s = (self.g, c, t), (f, c, self.y), (f, c, self.s)

    def copies(self, w):
        a = OVER_Y[w]
        return [k for k in range(9) if a or k not in (3, 7)]

    def parts(self, w):
        a, rows = OVER_Y[w], BLOCKS[w][0]
        return (0, a), (a, rows - a)

    def copy(self, w, k):
        f, _, t = self.me
        g, y = self.g, self.y
        whole = self.wholes[w]
        first, second = self.parts(w)
        if k < 3:
            src, dst = self.shards[w], block(whole, w, t, f)
            dest = (self.to_x, self.to_y, self.to_s)[k]
        else:
            src = dst = block(whole, w, *(
                (t, g, first), (y, f, second), (t, g), (y, f), (y, g, first), (y, g, second)
            )[k - 3])
            dest = (self.to_y, self.to_x, self.to_s, self.to_s, self.to_s, self.to_s)[k - 3]
        return remote(src, dst, dest, self.ss.at[w, k], self.rs.at[w, k])

    def landed(self, w, k):
        f, _, t = self.me
        g, y, s = self.g, self.y, self.s
        sy = (s + 2) % 4
        first, second = self.parts(w)
        place = (
            (t, g), (y, f), (s, f), (y, g, first), (y, g, second),
            (s, g), (sy, f), (sy, g, first), (sy, g, second),
        )[k]
        return block(self.wholes[w], w, *place)

    def wait_recv(self, w, k):
        dst = self.landed(w, k)
        pltpu.make_async_copy(dst, dst, self.rs.at[w, k]).wait()

    def start_own(self, w, ks=(0, 1, 2)):
        f, _, t = self.me
        for k in ks:
            self.copy(w, k).start()
        if 2 in ks:
            pltpu.make_async_copy(self.shards[w], block(self.wholes[w], w, t, f), self.ls.at[w]).start()

    def forward_x(self, w):
        self.wait_recv(w, 0)
        if OVER_Y[w]:
            self.copy(w, 3).start()
        self.copy(w, 5).start()

    def forward_y(self, w):
        self.wait_recv(w, 1)
        self.copy(w, 4).start()
        self.copy(w, 6).start()

    def forward_second(self, w):
        if OVER_Y[w]:
            self.wait_recv(w, 3)
            self.copy(w, 7).start()
        self.wait_recv(w, 4)
        self.copy(w, 8).start()

    def arrived(self, w):
        f, _, t = self.me
        for k in (2, 5, 6, 7, 8):
            if k in self.copies(w):
                self.wait_recv(w, k)
        pltpu.make_async_copy(self.shards[w], block(self.wholes[w], w, t, f), self.ls.at[w]).wait()

    def sent(self, w):
        for k in self.copies(w):
            src = self.landed(w, k)
            pltpu.make_async_copy(src, src, self.ss.at[w, k]).wait()


def part_facts(k):
    _, ctx, tp = coords()
    q = (3 - ctx) * 8 + tp * 2 + k
    bottom = q < 15
    corner = bottom & (q % 5 == 4)
    right = (q >= 15) & (q < 27)
    return bottom, corner, right


def row_real(slot, rows):
    r = lax.broadcasted_iota(jnp.int32, (rows, 1), 0)
    wide = (r % 16) < WIN
    if slot < NFULL:
        return wide
    bottom, corner, right = part_facts(slot - NFULL)
    limit = jnp.where(corner, 64, jnp.where(right, 112, jnp.where(bottom, PART, 0)))
    narrow = jnp.where(corner | right, 1, 0)
    return (r < limit) & (wide | (narrow > 0))


def key_places(kind, shape):
    r = lax.broadcasted_iota(jnp.int32, shape, 0)
    a, b = r // 16, r % 16
    if kind == 0:
        return a, b
    _, corner, right = part_facts(kind - 1)
    corner, right = jnp.where(corner, 1, 0), jnp.where(right, 1, 0)
    a_right = jnp.where(r < 112, r // 8, (r - 112) // 8)
    b_right = jnp.where(r < 112, r % 8, 8 + (r - 112) % 8)
    a_corner = jnp.where(r < 64, r // 8, jnp.where(r < 128, (r - 64) // 8, 8 + (r - 128) // 16))
    b_corner = jnp.where(r < 64, r % 8, jnp.where(r < 128, 8 + (r - 64) % 8, (r - 128) % 16))
    a = jnp.where(corner > 0, a_corner, jnp.where(right > 0, a_right, a))
    b = jnp.where(corner > 0, b_corner, jnp.where(right > 0, b_right, b))
    return a, b


def build_keys(e_ref):
    shape = (FULL, 128)
    col = lax.broadcasted_iota(jnp.int32, shape, 1)
    j = col % 16
    for kind in range(1 + NPART):
        a, b = key_places(kind, shape)
        ok = b < WIN
        along_a = jnp.where(ok & (j == a) & (j < WIN), 1.0, 0.0)
        along_a = jnp.where(jnp.logical_not(ok) & (col % SEG == 15), MASKED, along_a)
        along_b = jnp.where(ok & (j == b) & (j < WIN), 1.0, 0.0)
        for head in range(4):
            mine = col // SEG == head
            e_ref[kind, head, :, pl.ds(0, 128)] = jnp.where(mine, along_a, 0.0).astype(BF)
            e_ref[kind, head, :, pl.ds(128, 128)] = jnp.where(mine, along_b, 0.0).astype(BF)


def build_relative(rel_ref, out_ref):
    out_ref[...] = jnp.zeros((D, D), BF)
    i = lax.broadcasted_iota(jnp.int32, (SEG, 128), 0)
    lane = lax.broadcasted_iota(jnp.int32, (SEG, 128), 1)
    turn = (lane % SEG == 26 - i).astype(BF)
    lane64 = lax.broadcasted_iota(jnp.int32, (HEAD_DIM, 128), 1) // SEG
    for axis in range(2):
        rev = tn(rel_ref[axis], turn)
        for h in range(HEADS):
            out_ref[pl.ds(h * HEAD_DIM, HEAD_DIM), pl.ds(axis * 384 + (h // 4) * 128, 128)] = (
                jnp.where(lane64 == h % 4, rev, 0.0).astype(BF)
            )


def slots():
    return [(k, k * FULL, FULL) for k in range(NFULL)] + [
        (NFULL + k, PBASE + k * PART, PART) for k in range(NPART)
    ]


def forward_kernel(images, direct, *refs):
    if direct:
        (x_ref, c_ref, wq_s, wp_s, wu_s, wd_s, vec, rel_ref,
         x_o, c_o, n1_o, qkv_o, att_o, p_o, wq_o, wp, wu, wd, e_o, rel_o,
         stage, xw, cw, n1, qkv, att, p_buf, wq, e, rel_cols, x_scr, bias_v, ss, rs, gss, grs, gls, os) = refs
    else:
        (x_ref, c_ref, wq_s, vec, rel_ref,
         x_o, c_o, n1_o, qkv_o, att_o, p_o, e_o, rel_o,
         stage, xw, cw, n1, qkv, att, p_buf, wq, e, rel_cols, x_scr, bias_v, ss, rs, os) = refs
    me = coords()
    f, ctx, tp = me
    group_barrier(((1 - f, ctx, tp),) if direct else ())
    pack = pack_matrix()

    def stage_tokens(a, src):
        for i in range(images):
            for u in range(2):
                stage[a, i, u] = jnp.dot(
                    pack, src[i, pl.ds(u * 128, 128)], preferred_element_type=F32
                ).astype(BF)

    out_copies = []

    def write(src, dst):
        cp = pltpu.make_async_copy(src, dst, os.at[len(out_copies)])
        cp.start()
        out_copies.append(cp)

    if direct:
        shards = (wq_s.at[0], wq_s.at[1], wq_s.at[2], wp_s, wu_s, wd_s)
        gather = Gather(shards, (wq.at[0], wq.at[1], wq.at[2], wp, wu, wd), me, gss, grs, gls)
        for w in range(3):
            gather.start_own(w)
    else:
        load = pltpu.make_async_copy(wq_s, wq, os.at[15])
        load.start()
    stage_tokens(0, x_ref)
    start_pieces(stage, xw, 0, images, me, ss, rs)
    build_keys(e)
    build_relative(rel_ref, rel_cols)
    write(e, e_o)
    write(rel_cols, rel_o)
    stage_tokens(1, c_ref)
    if direct:
        for w in range(3):
            gather.forward_x(w)
            gather.forward_y(w)
        gather.start_own(3)
        gather.start_own(4)
    wait_pieces(xw, 0, me, rs)
    for slot, base, rows in slots():
        here = pl.ds(base, rows)
        real = row_real(slot, rows)
        x = jnp.where(real, xw[here].astype(F32), 0.0)
        xw[here] = x.astype(BF)
        mean = jnp.mean(x, axis=-1, keepdims=True)
        centered = x - mean
        r = lax.rsqrt(jnp.mean(centered * centered, axis=-1, keepdims=True) + EPSILON)
        n1[here] = jnp.where(
            real, centered * r * vec[pl.ds(0, 1), pl.ds(0, D)] + vec[pl.ds(1, 1), pl.ds(0, D)], 0.0
        ).astype(BF)
    write(xw, x_o)
    write(n1, n1_o)
    if direct:
        for w in range(3):
            gather.forward_second(w)
        gather.start_own(5)
        start_pieces(stage, cw, 1, images, me, ss, rs)
        for w in range(3):
            gather.arrived(w)
        write(wq, wq_o)
    else:
        load.wait()
        start_pieces(stage, cw, 1, images, me, ss, rs)

    @pl.loop(0, 6)
    def _(n):
        cols = pl.ds(pl.multiple_of((n % 2) * 384, 128), 384)
        out = nt(n1[...], wq[n // 2, cols, :])
        there = pl.ds(pl.multiple_of(n * 384, 128), 384)
        qkv[:, there] = (out + vec[pl.ds(2, 1), there]).astype(BF)

    write(qkv, qkv_o)
    bias_v[...] = vec[pl.ds(2, 1), pl.ds(2 * D, D)]

    @pl.loop(0, NFULL)
    def _(n):
        attention_slot(qkv, rel_cols, bias_v, e.at[0], att, p_buf, pl.multiple_of(n * FULL, 16), FULL, None, x_scr)
        if direct:
            @pl.when(n == 0)
            def _():
                gather.forward_x(3)
                gather.forward_y(3)
                gather.forward_x(4)
                gather.forward_y(4)

            @pl.when(n == 1)
            def _():
                gather.forward_second(3)
                gather.forward_x(5)
                gather.forward_y(5)

            @pl.when(n == 2)
            def _():
                gather.forward_second(4)

    @pl.loop(0, NPART)
    def _(n):
        attention_slot(qkv, rel_cols, bias_v, e.at[1 + n], att, p_buf,
                       pl.multiple_of(PBASE + n * PART, 16), PART, narrow_flag(n), x_scr)

    write(att, att_o)
    write(p_buf, p_o)
    if direct:
        gather.forward_second(5)
    wait_pieces(cw, 1, me, rs)
    for slot, base, rows in slots():
        here = pl.ds(base, rows)
        cw[here] = jnp.where(row_real(slot, rows), cw[here].astype(F32), 0.0).astype(BF)
    write(cw, c_o)
    if direct:
        for w in range(3, UNITS):
            gather.arrived(w)
        for w in range(UNITS):
            gather.sent(w)
    for a in range(2):
        finish_piece_sends(stage, a, images, me, ss)
    for cp in out_copies:
        cp.wait()


def forward(x3, c3, shards, wq_whole, vec, rel):
    images = x3.shape[0]
    any_spec = pl.BlockSpec(memory_space=pl.ANY)
    vmem = pl.BlockSpec(memory_space=pltpu.VMEM)
    direct = wq_whole is None
    dma = pltpu.SemaphoreType.DMA
    shape = jax.ShapeDtypeStruct
    tokens = shape((ROWS, D), BF)
    outs = [tokens, tokens, tokens, shape((ROWS, 3 * D), BF), tokens, shape((ROWS, HEADS * 256), BF)]
    if direct:
        outs += [shape(s, BF) for s in ((3, D, D), (D, D), (4 * D, D), (4 * D, D))]
    outs += [shape((1 + NPART, 4, FULL, 256), BF), shape((D, D), BF)]
    scratch = [
        pltpu.VMEM((2, images, 2, PIECE, D), BF),
        pltpu.VMEM((ROWS, D), BF), pltpu.VMEM((ROWS, D), BF), pltpu.VMEM((ROWS, D), BF),
        pltpu.VMEM((ROWS, 3 * D), BF), pltpu.VMEM((ROWS, D), BF), pltpu.VMEM((ROWS, HEADS * 256), BF),
        pltpu.VMEM((3, D, D), BF), pltpu.VMEM((1 + NPART, 4, FULL, 256), BF), pltpu.VMEM((D, D), BF),
        pltpu.VMEM((FULL, GROUPS * 256), BF), pltpu.VMEM((1, D), F32),
        dma((2, images * 10)), dma((2, NFULL + NPART, PAIRS)),
    ]
    if direct:
        scratch += [dma((UNITS, 9)), dma((UNITS, 9)), dma((UNITS,))]
    scratch += [dma((16,))]
    weights = list(shards) if direct else [wq_whole]
    return pl.pallas_call(
        functools.partial(forward_kernel, images, direct),
        out_shape=outs,
        in_specs=[vmem, vmem] + [any_spec] * len(weights) + [vmem, vmem],
        out_specs=[any_spec] * len(outs),
        scratch_shapes=scratch,
        compiler_params=pltpu.CompilerParams(
            collective_id=0, has_side_effects=True, vmem_limit_bytes=VMEM_LIMIT
        ),
        name="forward_attention",
    )(x3, c3, *weights, vec, rel)


def barrel(x, shift, left):
    lanes = x.shape[-1]
    for bit in (1, 2, 4, 8):
        moved = pltpu.roll(x, lanes - bit if left else bit, 1)
        x = jnp.where((shift // bit) % 2 == 1, moved, x)
    return x


def row_places(rows, narrow):
    r = lax.broadcasted_iota(jnp.int32, (rows, 128), 0)
    if narrow is None:
        return r // 16, r % 16
    is_narrow = narrow > 0
    return jnp.where(is_narrow, r // 8, r // 16), jnp.where(is_narrow, r % 8, r % 16)


def half_mask(hh):
    lane = lax.broadcasted_iota(jnp.int32, (1, 128), 1)
    return ((lane // 64) == hh).astype(BF)


def nt(a, b):
    return lax.dot_general(a, b, (((1,), (1,)), ((), ())), preferred_element_type=F32)


def tn(a, b):
    return lax.dot_general(a, b, (((0,), (0,)), ((), ())), preferred_element_type=F32)


def key_rows(ref, base, rows, col, fill):
    part = ref[pl.ds(base, rows), pl.ds(col, 128)]
    if rows == FULL:
        return part
    return jnp.concatenate([part, jnp.broadcast_to(fill, (FULL - rows, 128)).astype(BF)], axis=0)


def attention_slot(qkv, rel_cols, bias_v, e_at, o_ref, p_ref, base, rows, narrow, x_scr):
    a_row, b_row = row_places(rows, narrow)
    q_all = qkv[pl.ds(base, rows), pl.ds(0, D)]
    lane = lax.broadcasted_iota(jnp.int32, (rows, 128), 1) % SEG
    for axis, pos in ((0, a_row), (1, b_row)):
        raw = jnp.dot(q_all, rel_cols[:, pl.ds(axis * 384, 384)], preferred_element_type=F32)
        for g in range(GROUPS):
            v = barrel(raw[:, g * 128:(g + 1) * 128], jnp.maximum(13 - pos, 0), True)
            hi = v.astype(BF).astype(F32)
            lo = pltpu.roll(v - hi, 16, 1)
            mix = jnp.where(lane < WIN, hi, jnp.where(lane >= 16, lo, 0.0))
            if axis == 0:
                mix = jnp.where(lane == 15, 1.0, mix)
            x_scr[pl.ds(0, rows), pl.ds(g * 256 + axis * 128, 128)] = mix.astype(BF)
    for hp in range(6):
        q = q_all[:, hp * 128:(hp + 1) * 128]
        k = key_rows(qkv, base, rows, D + hp * 128, jnp.zeros((1, 128), BF))
        v = key_rows(qkv, base, rows, 2 * D + hp * 128, bias_v[:, pl.ds(hp * 128, 128)])
        out = jnp.zeros((rows, 128), F32)
        for hh in range(2):
            h = hp * 2 + hh
            x = x_scr[pl.ds(0, rows), pl.ds((h // 4) * 256, 256)]
            s = nt(q, k * (half_mask(hh) * 0.125)) + nt(x, e_at[h % 4])
            p = jnp.exp(s - jnp.max(s, axis=-1, keepdims=True))
            p = (p * (1.0 / jnp.sum(p, axis=-1, keepdims=True))).astype(BF)
            p_ref[pl.ds(base, rows), pl.ds(h * 256, FULL)] = p
            out = out + jnp.dot(p, v * half_mask(hh), preferred_element_type=F32)
        o_ref[pl.ds(base, rows), pl.ds(hp * 128, 128)] = out.astype(BF)


def narrow_flag(k):
    _, ctx, tp = coords()
    q = (3 - ctx) * 8 + tp * 2 + k
    is_narrow = ((q < 15) & (q % 5 == 4)) | ((q >= 15) & (q < 27))
    return jnp.where(is_narrow, 1, 0)


def attention_back_slot(qkv, do_ref, rel_cols, bias_v, e_at, p_ref, d_scr, acc_scr, pad_acc, rel_acc, base, rows, narrow):
    a_row, b_row = row_places(rows, narrow)
    here = pl.ds(base, rows)
    for g in range(GROUPS):
        dx = jnp.zeros((rows, 256), F32)
        for hp in (2 * g, 2 * g + 1):
            cols = pl.ds(hp * 128, 128)
            k_cols, v_cols = pl.ds(D + hp * 128, 128), pl.ds(2 * D + hp * 128, 128)
            q = qkv[here, cols]
            k = key_rows(qkv, base, rows, D + hp * 128, jnp.zeros((1, 128), BF))
            v = key_rows(qkv, base, rows, 2 * D + hp * 128, bias_v[:, cols])
            do = do_ref[here, cols]
            dq = jnp.zeros((rows, 128), F32)
            dk = jnp.zeros((FULL, 128), F32)
            dv = jnp.zeros((FULL, 128), F32)
            for hh in range(2):
                h = hp * 2 + hh
                mask = half_mask(hh)
                do_m = do * mask
                dp = nt(do_m, v)
                p_low = p_ref[pl.ds(0, rows), pl.ds(h * 256, FULL)]
                t = p_low.astype(F32)
                tp = t * dp
                ds = (tp - t * jnp.sum(tp, axis=-1, keepdims=True)).astype(BF)
                dq = dq + jnp.dot(ds, k * (mask * 0.125), preferred_element_type=F32)
                dx = dx + jnp.dot(ds, e_at[h % 4], preferred_element_type=F32)
                dk = dk + tn(ds, q * (mask * 0.125))
                dv = dv + tn(p_low, do_m)
            acc_scr[pl.ds(0, rows), cols] = dq
            qkv[here, k_cols] = dk[:rows].astype(BF)
            qkv[here, v_cols] = dv[:rows].astype(BF)
            if rows < FULL:
                pad_acc[:, cols] += jnp.sum(dv[rows:], axis=0, keepdims=True)
        lane = lax.broadcasted_iota(jnp.int32, (rows, 128), 1) % SEG
        for axis, pos in ((0, a_row), (1, b_row)):
            v = jnp.where(lane < WIN, dx[:, axis * 128:(axis + 1) * 128], 0.0)
            v = barrel(v, jnp.maximum(13 - pos, 0), False)
            d_scr[pl.ds(0, rows), pl.ds(axis * 384 + g * 128, 128)] = v.astype(BF)
    d = d_scr[pl.ds(0, rows), :]
    rel_acc[pl.ds(0, D)] += tn(d, qkv[here, pl.ds(0, D)])
    qkv[here, pl.ds(0, D)] = (acc_scr[pl.ds(0, rows), :] + nt(d, rel_cols[...])).astype(BF)


TILE = (D, D, 192, 192, 192, 192)
HALVES = ((384, D), (D, 384), (192, 384), (192, 384), (192, 384), (192, 384))
CHUNK = ROWS // 2
SUMS = 16
FEW = 12 * 6 + 2 * SEG


def add_rows(dst, src):
    rows = dst.shape[0]
    size = 64

    @pl.loop(0, rows // size)
    def _(n):
        here = pl.ds(pl.multiple_of(n * size, 16), size)
        dst[here] = (dst[here].astype(F32) + src[here].astype(F32)).astype(BF)


class Reduce:
    def __init__(self, grads, me, outs, r1, rx, ry, rz, s1, v1, s2, v2, s3, v3, sz, vz, so):
        self.grads, self.outs = grads, outs
        self.r1u, self.r1d, self.r1p = r1
        self.rx, self.ry, self.rz = rx, ry, rz
        self.s1, self.v1, self.s2, self.v2, self.s3, self.v3 = s1, v1, s2, v2, s3, v3
        self.sz, self.vz, self.so = sz, vz, so
        f, ctx, tp = me
        self.f, self.g = f, 1 - f
        self.c, self.own = tp % 2, tp // 2
        self.to_s = (f, ctx, tp + 1 - 2 * self.c)
        self.to_x = (1 - f, ctx, tp)
        self.to_y = (f, ctx, (tp + 2) % 4)
        self.outer = (ctx == 0) | (ctx == 3)
        self.inner = jnp.logical_not(self.outer)
        self.to_mid = (f, 3 - ctx, tp)
        self.to_in = (f, jnp.where(ctx == 0, 1, 2), tp)
        self.to_out = (f, jnp.where(ctx == 1, 0, 3), tp)

    def tile(self, w, t):
        return self.grads[w].at[pl.ds(pl.multiple_of(t * TILE[w], 16), TILE[w])]

    def half(self, w, t, f):
        if w == 0:
            return self.grads[w].at[pl.ds(pl.multiple_of(t * D + f * 384, 16), 384)]
        return self.grads[w].at[
            pl.ds(pl.multiple_of(t * TILE[w], 16), TILE[w]), pl.ds(pl.multiple_of(f * 384, 128), 384)
        ]

    def landing(self, w, j):
        if w < 2:
            return (self.r1u, self.r1d)[w].at[j]
        if w == 2:
            return self.r1p.at[j]
        return self.r1d.at[(w - 3) // 2, pl.ds(((w - 3) % 2) * 384 + j * 192, 192)]

    def core_copy(self, w, j):
        src = self.tile(w, 1 - self.c + 2 * j)
        return remote(src, self.landing(w, j), self.to_s, self.s1.at[w, j], self.v1.at[w, j])

    def core_send(self, w, j):
        self.core_copy(w, j).start()

    def x_copy(self, w, j):
        src = self.half(w, self.c + 2 * j, self.g)
        return remote(src, self.rx[w].at[j], self.to_x, self.s2.at[w, j], self.v2.at[w, j])

    def core_add(self, w, j):
        self.core_copy(w, j).wait_recv()
        add_rows(self.tile(w, self.c + 2 * j), self.landing(w, j))
        self.x_copy(w, j).start()

    def y_copy(self, w):
        src = self.half(w, self.c + 2 * (1 - self.own), self.f)
        return remote(src, self.ry[w], self.to_y, self.s3.at[w], self.v3.at[w])

    def x_add(self, w, j):
        self.x_copy(w, j).wait_recv()
        add_rows(self.half(w, self.c + 2 * j, self.f), self.rx[w].at[j])

        @pl.when(self.own != j)
        def _():
            self.y_copy(w).start()

    def mine(self, w):
        return self.half(w, self.c + 2 * self.own, self.f)

    def y_add(self, w):
        self.y_copy(w).wait_recv()
        add_rows(self.mine(w), self.ry[w])

        @pl.when(self.outer)
        def _():
            remote(self.mine(w), self.rz[w].at[0], self.to_in, self.sz.at[w, 0], self.vz.at[w, 0]).start()

    def z_wait(self, w, slot, sem):
        view = self.rz[w].at[slot]
        pltpu.make_async_copy(view, view, sem).wait()

    def z_mid(self, w):
        @pl.when(self.inner)
        def _():
            self.z_wait(w, 0, self.vz.at[w, 0])
            add_rows(self.mine(w), self.rz[w].at[0])
            remote(self.mine(w), self.rz[w].at[1], self.to_mid, self.sz.at[w, 0], self.vz.at[w, 1]).start()

    def z_out(self, w):
        @pl.when(self.inner)
        def _():
            self.z_wait(w, 1, self.vz.at[w, 1])
            add_rows(self.rz[w].at[1], self.mine(w))
            remote(self.rz[w].at[1], self.rz[w].at[0], self.to_out, self.sz.at[w, 1], self.vz.at[w, 2]).start()
            pltpu.make_async_copy(self.rz[w].at[1], self.outs[w], self.so.at[w]).start()

    def z_end(self, w):
        @pl.when(self.outer)
        def _():
            self.z_wait(w, 0, self.vz.at[w, 2])
            pltpu.make_async_copy(self.rz[w].at[0], self.outs[w], self.so.at[w]).start()

    def sent(self, w):
        for j in range(2):
            self.core_copy(w, j).wait_send()
            self.x_copy(w, j).wait_send()
        self.y_copy(w).wait_send()
        self.z_wait(w, 0, self.sz.at[w, 0])

        @pl.when(self.inner)
        def _():
            self.z_wait(w, 0, self.sz.at[w, 1])

        pltpu.make_async_copy(self.rz[w].at[0], self.outs[w], self.so.at[w]).wait()


def backward_kernel(images, direct, *refs):
    it = iter(refs)

    def take(n):
        return [next(it) for _ in range(n)]

    x_h, c_h, n1_h, qkv_h, att_h, p_h, wq_h, wp_h, wu_h, wd_h, e_h, rel_h, vec = take(13)
    staged, few_out = take(2)
    outs = take(6)
    cot, att, n2, xhat2, hid, dg = take(6)
    x = hid
    acc, dn2 = take(2)
    wu, wd, wp, wq, dwq, qkv, p_buf, e, rel_cols, d_scr, acc_scr = take(11)
    bias_v, pad_acc, sums, r2, real = take(5)
    ls, ss, rs = take(3)
    if direct:
        r1 = take(3)
        rx, ry, rz = take(6), take(6), take(6)
        few_in, = take(1)
        sems = take(9)
        few_s, few_r = take(2)
    me = coords()
    f, ctx, tp = me
    loads = {}

    def load(name, src, dst):
        loads[name] = pltpu.make_async_copy(src, dst, ls.at[len(loads)])
        loads[name].start()

    load("att", att_h, att)
    load("wp", wp_h, wp)
    load("x", x_h, x)
    load("wu", wu_h, wu)
    load("wd", wd_h, wd)
    load("cot", c_h, cot)
    load("qkv", qkv_h, qkv)
    load("e", e_h, e)
    load("rel", rel_h, rel_cols)
    load("wq", wq_h, wq)

    def p_copy(slot):
        base, rows = (slot * FULL, FULL) if slot < NFULL else (PBASE + (slot - NFULL) * PART, PART)
        return pltpu.make_async_copy(
            p_h.at[pl.ds(base, rows)], p_buf.at[slot % 2, pl.ds(0, rows)], ls.at[12 + slot % 2]
        )

    p_copy(0).start()
    p_copy(1).start()
    group_barrier(((1 - f, ctx, tp),) if direct else ())
    grads = (wu, wd, wp, dwq.at[0], dwq.at[1], dwq.at[2])
    red = Reduce(grads, me, outs, r1, rx, ry, rz, *sems) if direct else None
    c = tp % 2
    sums[...] = jnp.zeros_like(sums)
    pad_acc[...] = jnp.zeros_like(pad_acc)
    bias_v[...] = vec[5:6, :]
    for slot, base, rows in slots():
        real[pl.ds(base, rows)] = jnp.where(row_real(slot, rows), 1.0, 0.0)

    def row_chunks(body):
        @pl.loop(0, ROWS // CHUNK)
        def _(n):
            body(pl.ds(pl.multiple_of(n * CHUNK, 16), CHUNK))

    for name in ("att", "wp", "x"):
        loads[name].wait()

    def project(here):
        mid = x[here].astype(F32) + jnp.dot(att[here], wp[...], preferred_element_type=F32) + vec[3:4, :]
        mean = jnp.mean(mid, axis=-1, keepdims=True)
        centered = mid - mean
        r = lax.rsqrt(jnp.mean(centered * centered, axis=-1, keepdims=True) + EPSILON)
        xhat = centered * r
        r2[here] = r
        xhat2[here] = xhat.astype(BF)
        n2[here] = (xhat * vec[1:2, :] + vec[2:3, :]).astype(BF)
        acc[here] = mid + vec[4:5, :]
        dn2[here] = jnp.zeros((CHUNK, D), F32)

    row_chunks(project)

    for name in ("wu", "wd", "cot"):
        loads[name].wait()
    for t in range(4):
        base = t * D

        @pl.loop(0, 3)
        def _(j, base=base, t=t):
            units = pl.ds(pl.multiple_of(j * 256, 128), 256)
            gate = jnp.dot(n2[...], wu[pl.ds(base, D), units], preferred_element_type=F32)
            up_bias = jnp.where(j == 0, vec[6 + t:7 + t, 0:256], jnp.where(
                j == 1, vec[6 + t:7 + t, 256:512], vec[6 + t:7 + t, 512:768]))
            hidden, slope = gelu_both(gate + up_bias)
            hid[:, units] = hidden.astype(BF)
            there = pl.ds(pl.multiple_of(base + j * 256, 16), 256)
            d_gate = (nt(cot[...], wd[there, :]) * slope).astype(BF)
            dg[:, units] = d_gate
            sums[pl.ds(8 + t, 1), units] = jnp.sum(d_gate.astype(F32), axis=0, keepdims=True)

        tile = pl.ds(base, D)

        def through(here, tile=tile):
            acc[here] += jnp.dot(hid[here], wd[tile, :], preferred_element_type=F32)
            dn2[here] += nt(dg[here], wu[tile, :])

        row_chunks(through)

        @pl.loop(0, 3)
        def _(j, base=base):
            part = pl.ds(pl.multiple_of(j * 256, 128), 256)
            there = pl.ds(pl.multiple_of(base + j * 256, 16), 256)
            wd[there, :] = tn(hid[:, part], cot[...]).astype(BF)
            wu[there, :] = tn(n2[:, part], dg[...]).astype(BF)

        if direct:
            @pl.when(c != t % 2)
            def _(t=t):
                red.core_send(1, t // 2)
                red.core_send(0, t // 2)

            if t:
                @pl.when(c == (t - 1) % 2)
                def _(t=t):
                    red.core_add(1, (t - 1) // 2)
                    red.core_add(0, (t - 1) // 2)

    def back_two(here):
        n = dn2[here]
        xhat = xhat2[here].astype(F32)
        c_rows = cot[here].astype(F32)
        m = n * vec[1:2, :]
        sums[5:6, :] += jnp.sum(n * xhat, axis=0, keepdims=True)
        sums[6:7, :] += jnp.sum(n, axis=0, keepdims=True)
        sums[7:8, :] += jnp.sum(c_rows, axis=0, keepdims=True)
        mean = jnp.mean(m, axis=-1, keepdims=True)
        mean_x = jnp.mean(m * xhat, axis=-1, keepdims=True)
        d_mid = c_rows + r2[here] * (m - mean - xhat * mean_x)
        dn2[here] = d_mid
        branch = d_mid.astype(BF)
        n2[here] = branch
        sums[4:5, :] += jnp.sum(branch.astype(F32), axis=0, keepdims=True)
        dg[here] = acc[here].astype(BF)
        hid[here] = nt(branch, wp[...]).astype(BF)

    row_chunks(back_two)
    places = window_places(ctx, tp)

    def tokens_out(a, src_ref):
        for n, (slot, p, rows, exists, image, u, col, d_ctx, d_tp, row) in enumerate(places):
            def go(n=n, rows=rows, image=image, u=u, col=col, d_ctx=d_ctx, d_tp=d_tp, row=row):
                src = src_ref.at[pl.ds(row, rows)]
                dst = staged.at[a, image, u, pl.ds(pl.multiple_of(col * 32, 16), rows)]
                send_or_copy(src, dst, (d_ctx, d_tp), me, ss.at[a, n], rs.at[a, image, u, col])
            if exists is None:
                go()
            else:
                pl.when(exists)(go)

    def tokens_done(a, src_ref):
        for i in range(images):
            for u in range(2):
                for col in range(5):
                    dst = staged.at[a, i, u, pl.ds(col * 32, 32 if col < 4 else 16)]
                    pltpu.make_async_copy(dst, dst, rs.at[a, i, u, col]).wait()
        for n, (slot, p, rows, exists, image, u, col, d_ctx, d_tp, row) in enumerate(places):
            def done(n=n, rows=rows, d_ctx=d_ctx, d_tp=d_tp, row=row):
                wait_sent(src_ref.at[pl.ds(row, rows)], (d_ctx, d_tp), me, ss.at[a, n])
            if exists is None:
                done()
            else:
                pl.when(exists)(done)

    tokens_out(0, dg)

    @pl.loop(0, 3)
    def _(j):
        part = pl.ds(pl.multiple_of(j * 256, 128), 256)
        wp[pl.ds(pl.multiple_of(j * 256, 16), 256), :] = tn(att[:, part], n2[...]).astype(BF)

    if direct:
        @pl.when(c == 1)
        def _():
            red.core_add(1, 1)
            red.core_add(0, 1)

        red.core_send(2, 0)
        red.core_send(2, 1)
        red.x_add(1, 0)

    load_n1 = pltpu.make_async_copy(n1_h, n2, ls.at[11])
    load_n1.start()
    load_x = pltpu.make_async_copy(x_h, xhat2, ls.at[14])
    load_x.start()
    for name in ("qkv", "e", "rel"):
        loads[name].wait()
    acc[pl.ds(0, D)] = jnp.zeros((D, D), F32)
    for slot, base, rows in slots():
        p_copy(slot).wait()
        kind = 0 if slot < NFULL else 1 + slot - NFULL
        narrow = None if slot < NFULL else narrow_flag(slot - NFULL)
        attention_back_slot(qkv, hid, rel_cols, bias_v, e.at[kind], p_buf.at[slot % 2], d_scr, acc_scr,
                            pad_acc, acc, base, rows, narrow)
        if slot + 2 < NFULL + NPART:
            p_copy(slot + 2).start()
        if direct:
            if slot == 0:
                red.x_add(0, 0)
                red.core_add(2, 0)
                red.core_add(2, 1)
            elif slot == 2:
                red.x_add(1, 1)
            elif slot == 3:
                red.y_add(1)

    load_n1.wait()
    load_x.wait()
    loads["wq"].wait()
    for w in range(3):
        @pl.loop(0, 3)
        def _(j, w=w):
            part = pl.ds(pl.multiple_of(w * D + j * 256, 128), 256)
            d_cols = qkv[:, part]
            dwq[w, pl.ds(pl.multiple_of(j * 256, 16), 256), :] = tn(d_cols, n2[...]).astype(BF)

        if direct:
            red.core_send(3 + w, 0)
            red.core_send(3 + w, 1)

    def back_one(here):
        d_qkv = qkv[here, :]
        n = jnp.zeros((CHUNK, D), F32)
        for w in range(3):
            n = n + jnp.dot(d_qkv[:, w * D:(w + 1) * D], wq[w], preferred_element_type=F32)
        sums[2:3, :] += jnp.sum(d_qkv[:, :D].astype(F32), axis=0, keepdims=True)
        sums[3:4, :] += jnp.sum(d_qkv[:, 2 * D:].astype(F32), axis=0, keepdims=True)
        n = n * real[here]
        rows = xhat2[here].astype(F32)
        centered = rows - jnp.mean(rows, axis=-1, keepdims=True)
        r = lax.rsqrt(jnp.mean(centered * centered, axis=-1, keepdims=True) + EPSILON)
        xhat = centered * r
        sums[0:1, :] += jnp.sum(n * xhat, axis=0, keepdims=True)
        sums[1:2, :] += jnp.sum(n, axis=0, keepdims=True)
        m = n * vec[0:1, :]
        mean = jnp.mean(m, axis=-1, keepdims=True)
        mean_x = jnp.mean(m * xhat, axis=-1, keepdims=True)
        cot[here] = (dn2[here] + r * (m - mean - xhat * mean_x)).astype(BF)

    if direct:
        for w in range(3):
            red.core_add(3 + w, 0)
            red.core_add(3 + w, 1)
        red.x_add(0, 1)
        red.y_add(0)
        red.z_mid(1)
    row_chunks(back_one)
    tokens_out(1, cot)

    sums[3:4, :] += pad_acc[...]
    order = (0, 1, 2, 3, 4, 5, 6, 7, 8, 9, 10, 11)
    for n, row in enumerate(order):
        for k in range(6):
            few_out[pl.ds(n * 6 + k, 1), :] = sums[pl.ds(row, 1), pl.ds(k * 128, 128)]
    lane = lax.broadcasted_iota(jnp.int32, (SEG, 128), 1) // HEAD_DIM
    for axis in range(2):
        total = jnp.zeros((SEG, 128), F32)
        for h in range(HEADS):
            piece = acc[pl.ds(axis * 384 + h * SEG, SEG), pl.ds((h // 2) * 128, 128)]
            total = total + jnp.where(lane == h % 2, piece, 0.0)
        few_out[pl.ds(72 + axis * SEG, SEG), :] = total

    if direct:
        steps = (red.to_s, red.to_x, red.to_y, (f, ctx + 1 - 2 * (ctx % 2), tp), (f, (ctx + 2) % 4, tp))

        def few_copy(n):
            return remote(few_in.at[5 + n], few_in.at[n], steps[n], few_s.at[n], few_r.at[n])

        def few_start(n):
            few_in[5 + n] = few_out[...]
            few_copy(n).start()

        def few_add(n):
            few_copy(n).wait_recv()
            few_out[...] = few_out[...] + few_in[n]

        few_start(0)
        for w in (2, 3, 4, 5):
            red.x_add(w, 0)
            red.x_add(w, 1)
        red.z_out(1)
        red.z_mid(0)
        few_add(0)
        few_start(1)
        for w in (2, 3, 4, 5):
            red.y_add(w)
        few_add(1)
        few_start(2)
        for w in (2, 3, 4, 5):
            red.z_mid(w)
        few_add(2)
        few_start(3)
        for w in (0, 2, 3, 4, 5):
            red.z_out(w)
        few_add(3)
        few_start(4)
        for w in (1, 0, 2, 3, 4, 5):
            red.z_end(w)
        few_add(4)
        for w in range(6):
            red.sent(w)
        for n in range(5):
            few_copy(n).wait_send()
    else:
        for n, src in enumerate((wu, wd, wp, dwq.at[0], dwq.at[1], dwq.at[2])):
            cp = pltpu.make_async_copy(src, outs[n], ls.at[n])
            cp.start()
            cp.wait()
    tokens_done(0, dg)
    tokens_done(1, cot)


def backward(inputs, vec, images, direct):
    any_spec = pl.BlockSpec(memory_space=pl.ANY)
    vmem = pl.BlockSpec(memory_space=pltpu.VMEM)
    dma = pltpu.SemaphoreType.DMA
    shape = jax.ShapeDtypeStruct
    n_places = NFULL * PAIRS + NPART * (4 + PAIRS)
    wholes = ((4 * D, D), (4 * D, D), (D, D), (D, D), (D, D), (D, D))
    out_shape = [shape((2, images, 2, PIECE, D), BF), shape((FEW, 128), F32)]
    out_shape += [shape(s, BF) for s in (HALVES if direct else wholes)]
    v = pltpu.VMEM
    scratch = [v((ROWS, D), BF)] * 6 + [v((ROWS, D), F32)] * 2
    scratch += [
        v((4 * D, D), BF), v((4 * D, D), BF), v((D, D), BF), v((3, D, D), BF), v((3, D, D), BF),
        v((ROWS, 3 * D), BF), v((2, FULL, HEADS * 256), BF), v((1 + NPART, 4, FULL, 256), BF), v((D, D), BF),
        v((FULL, D), BF), v((FULL, D), F32),
        v((1, D), F32), v((1, D), F32), v((SUMS, D), F32), v((ROWS, 1), F32), v((ROWS, 1), F32),
        dma((15,)), dma((2, n_places)), dma((2, images, 2, 5)),
    ]
    if direct:
        scratch += [v((2, D, D), BF), v((2, D, D), BF), v((2, 192, D), BF)]
        scratch += [v((2,) + s, BF) for s in HALVES]
        scratch += [v(s, BF) for s in HALVES]
        scratch += [v((2,) + s, BF) for s in HALVES]
        scratch += [v((10, FEW, 128), F32)]
        scratch += [dma((6, 2)), dma((6, 2)), dma((6, 2)), dma((6, 2)), dma((6,)), dma((6,)), dma((6, 2)), dma((6, 3)), dma((6,))]
        scratch += [dma((5,)), dma((5,))]
    return pl.pallas_call(
        functools.partial(backward_kernel, images, direct),
        out_shape=out_shape,
        in_specs=[any_spec] * len(inputs) + [vmem],
        out_specs=[any_spec, vmem] + [any_spec] * 6,
        scratch_shapes=scratch,
        compiler_params=pltpu.CompilerParams(
            collective_id=1, has_side_effects=True, vmem_limit_bytes=VMEM_BACK
        ),
        name="backward",
    )(*inputs, vec)


def results_kernel(images, staged, *refs):
    n = (len(refs) - 2) // 2
    grads, outs = refs[:n], refs[n + 2:]
    unpack = pack_matrix()
    for a in range(2):
        for i in range(images):
            for u in range(2):
                refs[n + a][i, pl.ds(u * 128, 128)] = tn(unpack, staged[a, i, u]).astype(BF)
    for src, dst in zip(grads, outs):
        rows = src.shape[0]

        @pl.loop(0, rows // 64)
        def _(k, src=src, dst=dst):
            here = pl.ds(pl.multiple_of(k * 64, 16), 64)
            dst[here] = src[here].astype(F32)


def results(staged, grads):
    images = staged.shape[1]
    vmem = pl.BlockSpec(memory_space=pltpu.VMEM)
    tokens = jax.ShapeDtypeStruct((images, 256, D), BF)
    outs = [tokens, tokens] + [jax.ShapeDtypeStruct(g.shape, F32) for g in grads]
    return pl.pallas_call(
        functools.partial(results_kernel, images),
        out_shape=outs,
        in_specs=[vmem] * (1 + len(grads)),
        out_specs=[vmem] * len(outs),
        compiler_params=pltpu.CompilerParams(vmem_limit_bytes=VMEM_LIMIT),
        name="results",
    )(staged, *grads)


def gelu_both(u):
    x = jnp.abs(u) * math.sqrt(0.5)
    t = 1.0 / (1.0 + 0.3275911 * x)
    e = jnp.exp(-0.5 * u * u)
    poly = t * (0.254829592 + t * (-0.284496736 + t * (1.421413741 + t * (-1.453152027 + t * 1.061405429))))
    tail = 0.5 * poly * e
    phi = jnp.where(u >= 0, 1.0 - tail, tail)
    return u * phi, phi + u * e * (1.0 / math.sqrt(2 * math.pi))


def whole_weights(shards):
    wq, wp, wu, wd = shards
    wq = lax.all_gather(lax.all_gather(wq, "fsdp", axis=2, tiled=True), "tp", axis=1, tiled=True)
    wp = lax.all_gather(lax.all_gather(wp, "fsdp", axis=1, tiled=True), "tp", axis=0, tiled=True)
    wu = lax.all_gather(lax.all_gather(wu, "fsdp", axis=0, tiled=True), "tp", axis=1, tiled=True)
    wd = lax.all_gather(lax.all_gather(wd, "fsdp", axis=1, tiled=True), "tp", axis=0, tiled=True)
    return wq, wp, wu, wd


def summed_weights(grads):
    out = []
    for w, grad in enumerate(grads):
        part = lax.psum_scatter(grad, "tp", scatter_dimension=0, tiled=True)
        part = lax.psum_scatter(part, "fsdp", scatter_dimension=0 if w == 0 else 1, tiled=True)
        out.append(lax.psum(part, "ctx").astype(F32))
    return out


def local(direct, block_input, ln1_gain, ln1_bias, w_qkv, qkv_bias, rel_h, rel_w, w_proj, proj_bias,
          ln2_gain, ln2_bias, w_up, up_bias, w_down, down_bias, cotangent):
    images = block_input.shape[1]
    x3 = jnp.transpose(block_input, (1, 0, 2))
    c3 = jnp.transpose(cotangent, (1, 0, 2))
    shards = (jnp.transpose(w_qkv, (0, 2, 1)), w_proj, w_up, w_down)
    zero = jnp.zeros_like(ln1_gain)
    bias_row = jnp.concatenate([qkv_bias[0], zero, qkv_bias[1]])
    vec = jnp.stack([jnp.tile(ln1_gain, 3), jnp.tile(ln1_bias, 3), bias_row]).astype(F32)
    vec_back = jnp.stack(
        [ln1_gain, ln2_gain, ln2_bias, proj_bias, down_bias, qkv_bias[1]]
        + list(up_bias.reshape(4, D)) + [zero] * 6
    ).astype(F32)
    rel = jnp.pad(jnp.stack([rel_h, rel_w]), ((0, 0), (0, SEG - rel_h.shape[0]), (0, 0)))
    if direct:
        x, cot, n1, qkv, att, probs, wq, wp, wu, wd, e, rel_cols = forward(x3, c3, shards, None, vec, rel)
    else:
        wq, wp, wu, wd = whole_weights(shards)
        wu = jnp.swapaxes(wu.reshape(D, 4, D), 0, 1).reshape(4 * D, D)
        x, cot, n1, qkv, att, probs, e, rel_cols = forward(x3, c3, None, wq, vec, rel)
    staged, few, *grads = backward((x, cot, n1, qkv, att, probs, wq, wp, wu, wd, e, rel_cols), vec_back, images, direct)
    if direct:
        out3, dx3, ou, od, op, oq, ok, ov = results(staged, grads)
    else:
        out3, dx3 = results(staged, ())
        ou, od, op, oq, ok, ov = summed_weights(grads)
        few = lax.psum(few, ("fsdp", "ctx", "tp"))
    rows = few[:72].reshape(12, D)
    rel_sum = few[72:].reshape(2, SEG, 2, HEAD_DIM).sum(axis=2)[:, :27][:, ::-1]
    return (
        jnp.transpose(out3, (1, 0, 2)), jnp.transpose(dx3, (1, 0, 2)), rows[0], rows[1],
        jnp.transpose(jnp.stack([oq, ok, ov]), (0, 2, 1)), rows[2:4], rel_sum[0], rel_sum[1],
        op, rows[4], rows[5], rows[6], ou, rows[8:].reshape(4 * D), od, rows[7],
    )


def solution(mesh):
    direct = mesh.shape["fsdp"] == 2
    rows = P(("ctx", "tp"), "fsdp", None)
    w_specs = (P(None, "fsdp", "tp"), P("tp", "fsdp"), P("fsdp", "tp"), P("tp", "fsdp"))
    return jax.shard_map(
        functools.partial(local, direct),
        mesh=mesh,
        in_specs=(rows, P(), P(), w_specs[0], P(), P(), P(), w_specs[1], P(), P(), P(), w_specs[2], P(), w_specs[3], P(), rows),
        out_specs=(rows, rows, P(), P(), w_specs[0], P(), P(), P(), w_specs[1], P(), P(), P(), w_specs[2], P(), w_specs[3], P()),
        check_vma=False,
    )
```

```python
import functools
import math

import jax
import jax.numpy as jnp
from jax import lax
from jax.experimental import pallas as pl
from jax.experimental.pallas import tpu as pltpu
from jax.sharding import PartitionSpec as P

HEAD_DIM = 64
HEADS = 12
WIN = 14
SIDE = 64
BANDS = 4
PAIRS = 7
D = 768
EPSILON = 1e-06
MESH = pl.DeviceIdType.MESH
BF = jnp.bfloat16
F32 = jnp.float32

FULL = 224
PART = 128
NFULL = 3
NPART = 2
PBASE = NFULL * FULL
ROWS = PBASE + NPART * PART
PIECE = 144
HALF_HEADS = 6
HALF = HALF_HEADS * HEAD_DIM
RELS = 2 * WIN - 1
SEG = 32
MASKED = -1e9
VMEM_LIMIT = 60 * 2**20
VMEM_BACK = 63 * 2**20


def coords():
    return lax.axis_index("fsdp"), lax.axis_index("ctx"), lax.axis_index("tp")


def part_kind(ctx, tp, k, images):
    return (3 - ctx) * 8 + tp * 2 + k


def pack_matrix():
    row = lax.broadcasted_iota(jnp.int32, (PIECE, 128), 0)
    col = lax.broadcasted_iota(jnp.int32, (PIECE, 128), 1)
    wide = row < 128
    c = jnp.where(wide, row // 32, 4)
    u = jnp.where(wide, (row % 32) // 16, (row - 128) // 8)
    b = jnp.where(wide, row % 16, (row - 128) % 8)
    source = u * SIDE + c * WIN + b
    return ((source == col) & (b < WIN)).astype(BF)


def piece_places(ctx, tp, images):
    dev = ctx * 4 + tp
    out = []
    for i in range(images):
        for u in range(2):
            m = dev * 2 + u
            band = m // PAIRS
            p = m % PAIRS
            low = band == BANDS
            for c in range(5):
                q_low = i * 5 + c
                if c < 4:
                    f = i * 4 + c
                    d_ctx = jnp.where(low, 3 - q_low // 8, band)
                    d_tp = jnp.where(low, (q_low % 8) // 2, f // 3)
                    slot = jnp.where(low, NFULL + q_low % 2, f % 3)
                    d_row = jnp.where(low, PBASE + (q_low % 2) * PART, (f % 3) * FULL) + p * 32
                    out.append((i, u, c, d_ctx, d_tp, d_row, slot, p))
                else:
                    q = jnp.where(low, q_low, 15 + (3 - band) * 3 + i)
                    d_ctx = 3 - q // 8
                    d_tp = (q % 8) // 2
                    d_row = PBASE + (q % 2) * PART + p * 16
                    out.append((i, u, c, d_ctx, d_tp, d_row, NFULL + q % 2, p))
    return out


def window_places(ctx, tp):
    out = []
    for k in range(NFULL):
        f = tp * 3 + k
        for p in range(PAIRS):
            m = ctx * PAIRS + p
            dev = m // 2
            out.append((k, p, 32, None, f // 4, m % 2, f % 4, dev // 4, dev % 4, k * FULL + p * 32))
    for k in range(NPART):
        q = (3 - ctx) * 8 + tp * 2 + k
        bottom = q < 15
        corner = bottom & (q % 5 == 4)
        right = (q >= 15) & (q < 27)
        qr = jnp.where(right, q - 15, 0)
        band = jnp.where(bottom, BANDS, 3 - qr // 3)
        image = jnp.where(bottom, q // 5, qr % 3)
        base = PBASE + k * PART
        for p in range(PAIRS):
            m = band * PAIRS + p
            dev = jnp.minimum(m // 2, 15)
            place = (image, m % 2, dev // 4, dev % 4)
            if p < 4:
                wide = bottom & jnp.logical_not(corner)
                out.append((NFULL + k, p, 32, wide, image, m % 2, q % 5, dev // 4, dev % 4, base + p * 32))
            narrow = (corner | right) if p < 4 else right
            out.append((NFULL + k, p, 16, narrow, image, m % 2, 4, dev // 4, dev % 4, base + p * 16))
    return out


def group_barrier(extra=()):
    f, c, t = coords()
    sem = pltpu.get_barrier_semaphore()
    count = 0
    for dc in range(4):
        for dt in range(4):
            if dc == 0 and dt == 0:
                continue
            pl.semaphore_signal(sem, inc=1, device_id=(f, (c + dc) % 4, (t + dt) % 4), device_id_type=MESH)
            count += 1
    for dest in extra:
        pl.semaphore_signal(sem, inc=1, device_id=dest, device_id_type=MESH)
        count += 1
    pl.semaphore_wait(sem, count)


def send_or_copy(src, dst, dest, me, send_sem, recv_sem):
    (d_ctx, d_tp), (f, ctx, tp) = dest, me
    here = (d_ctx == ctx) & (d_tp == tp)

    @pl.when(here)
    def _():
        pltpu.make_async_copy(src, dst, recv_sem).start()

    @pl.when(jnp.logical_not(here))
    def _():
        pltpu.make_async_remote_copy(
            src_ref=src, dst_ref=dst, send_sem=send_sem, recv_sem=recv_sem,
            device_id=(f, d_ctx, d_tp), device_id_type=MESH,
        ).start()


def wait_sent(src, dest, me, send_sem):
    (d_ctx, d_tp), (f, ctx, tp) = dest, me
    away = jnp.logical_not((d_ctx == ctx) & (d_tp == tp))

    @pl.when(away)
    def _():
        pltpu.make_async_copy(src, src, send_sem).wait()


def start_pieces(stage, out, a, images, me, ss, rs):
    _, ctx, tp = me
    for n, (i, u, c, d_ctx, d_tp, d_row, slot, p) in enumerate(piece_places(ctx, tp, images)):
        rows = 32 if c < 4 else 16
        src = stage.at[a, i, u, pl.ds(c * 32, rows)]
        dst = out.at[pl.ds(pl.multiple_of(d_row, 16), rows)]
        send_or_copy(src, dst, (d_ctx, d_tp), me, ss.at[a, n], rs.at[a, slot, p])


def finish_piece_sends(stage, a, images, me, ss):
    _, ctx, tp = me
    for n, (i, u, c, d_ctx, d_tp, d_row, slot, p) in enumerate(piece_places(ctx, tp, images)):
        rows = 32 if c < 4 else 16
        wait_sent(stage.at[a, i, u, pl.ds(c * 32, rows)], (d_ctx, d_tp), me, ss.at[a, n])


def wait_pieces(out, a, me, rs):
    _, ctx, tp = me
    for slot, p, rows, exists, *_rest, row in window_places(ctx, tp):
        dst = out.at[pl.ds(row, rows)]
        wait = pltpu.make_async_copy(dst, dst, rs.at[a, slot, p]).wait
        if exists is None:
            wait()
        else:
            pl.when(exists)(wait)


UNITS = 6
BLOCKS = ((192, 384), (192, 384), (192, 384), (192, 384), (384, 768), (768, 384))
Z_UNITS = (4, 5)


def block(ref, w, t, f, part=None):
    rows, cols = BLOCKS[w]
    start, size = part if part is not None else (0, rows)
    if w == 4:
        return ref.at[pl.ds(pl.multiple_of(t * D + f * rows + start, 16), size)]
    return ref.at[
        pl.ds(pl.multiple_of(t * rows + start, 16), size),
        pl.ds(pl.multiple_of(f * cols, 128), cols),
    ]


def remote(src, dst, dest, send_sem, recv_sem):
    return pltpu.make_async_remote_copy(
        src_ref=src, dst_ref=dst, send_sem=send_sem, recv_sem=recv_sem, device_id=dest, device_id_type=MESH
    )


class Gather:
    def __init__(self, shards, wholes, me, ss, rs, ls):
        self.shards, self.wholes = shards, wholes
        self.ss, self.rs, self.ls = ss, rs, ls
        f, c, t = me
        self.me = me
        self.g, self.y, self.s = 1 - f, (t + 2) % 4, t + 1 - 2 * (t % 2)
        self.to_x, self.to_y, self.to_s = (self.g, c, t), (f, c, self.y), (f, c, self.s)
        self.to_z = (f, c + 1 - 2 * (c % 2), t)
        self.parity = c % 2

    def copies(self, w):
        return range(13) if w in Z_UNITS else range(7)

    def part(self, w, theirs=False):
        if w not in Z_UNITS:
            return None
        half = BLOCKS[w][0] // 2
        return ((1 - self.parity if theirs else self.parity) * half, half)

    def own(self, w, part):
        if part is None:
            return self.shards[w]
        return self.shards[w].at[pl.ds(pl.multiple_of(part[0], 16), part[1])]

    def copy(self, w, k):
        f, _, t = self.me
        g, y = self.g, self.y
        whole = self.wholes[w]
        part, other = self.part(w), self.part(w, True)
        if k < 3:
            part = None if k == 2 else part
            src, dst = self.own(w, part), block(whole, w, t, f, part)
            dest = (self.to_x, self.to_y, self.to_s)[k]
        else:
            src = dst = block(whole, w, *(
                (y, f, part), (t, g, part), (y, f, part), (y, g, part),
                (t, g, part), (y, f, part), (y, g, part), (t, g, other), (y, f, other), (y, g, other),
            )[k - 3])
            dest = (self.to_x,) + (self.to_s,) * 3 + (self.to_z,) * 3 + (self.to_s,) * 3
            dest = dest[k - 3]
        return remote(src, dst, dest, self.ss.at[w, k], self.rs.at[w, k])

    def landed(self, w, k):
        f, _, t = self.me
        g, y, s = self.g, self.y, self.s
        sy = (s + 2) % 4
        part, other = self.part(w), self.part(w, True)
        place = (
            (t, g, part), (y, f, part), (s, f), (y, g, part), (s, g, part), (sy, f, part), (sy, g, part),
            (t, g, other), (y, f, other), (y, g, other), (s, g, other), (sy, f, other), (sy, g, other),
        )[k]
        return block(self.wholes[w], w, *place)

    def wait_recv(self, w, k):
        dst = self.landed(w, k)
        pltpu.make_async_copy(dst, dst, self.rs.at[w, k]).wait()

    def start_own(self, w, ks=(0, 1, 2)):
        f, _, t = self.me
        for k in ks:
            self.copy(w, k).start()
        if 2 in ks:
            pltpu.make_async_copy(self.shards[w], block(self.wholes[w], w, t, f), self.ls.at[w]).start()

    def on(self, w, arrived, sends):
        self.wait_recv(w, arrived)
        for k in sends:
            if k in self.copies(w):
                self.copy(w, k).start()

    def forward_x(self, w):
        self.on(w, 0, (7, 4))

    def forward_y(self, w):
        self.on(w, 1, (3, 8, 5))

    def forward_second(self, w):
        self.on(w, 3, (9, 6))

    def forward_z(self, w):
        for k in range(3):
            self.on(w, 7 + k, (10 + k,))

    def arrived(self, w, ks=(2, 4, 5, 6, 10, 11, 12)):
        f, _, t = self.me
        for k in ks:
            if k in self.copies(w):
                self.wait_recv(w, k)
        if 2 in ks:
            pltpu.make_async_copy(self.shards[w], block(self.wholes[w], w, t, f), self.ls.at[w]).wait()

    def sent(self, w):
        for k in self.copies(w):
            self.copy(w, k).wait_send()


def part_facts(k):
    _, ctx, tp = coords()
    q = (3 - ctx) * 8 + tp * 2 + k
    bottom = q < 15
    corner = bottom & (q % 5 == 4)
    right = (q >= 15) & (q < 27)
    return bottom, corner, right


def row_real(slot, rows):
    r = lax.broadcasted_iota(jnp.int32, (rows, 1), 0)
    wide = (r % 16) < WIN
    if slot < NFULL:
        return wide
    bottom, corner, right = part_facts(slot - NFULL)
    limit = jnp.where(corner, 64, jnp.where(right, 112, jnp.where(bottom, PART, 0)))
    narrow = jnp.where(corner | right, 1, 0)
    return (r < limit) & (wide | (narrow > 0))


def key_places(kind, shape):
    r = lax.broadcasted_iota(jnp.int32, shape, 0)
    a, b = r // 16, r % 16
    if kind == 0:
        return a, b
    _, corner, right = part_facts(kind - 1)
    corner, right = jnp.where(corner, 1, 0), jnp.where(right, 1, 0)
    a_right = jnp.where(r < 112, r // 8, (r - 112) // 8)
    b_right = jnp.where(r < 112, r % 8, 8 + (r - 112) % 8)
    a_corner = jnp.where(r < 64, r // 8, jnp.where(r < 128, (r - 64) // 8, 8 + (r - 128) // 16))
    b_corner = jnp.where(r < 64, r % 8, jnp.where(r < 128, 8 + (r - 64) % 8, (r - 128) % 16))
    a = jnp.where(corner > 0, a_corner, jnp.where(right > 0, a_right, a))
    b = jnp.where(corner > 0, b_corner, jnp.where(right > 0, b_right, b))
    return a, b


def build_keys(e_ref):
    shape = (FULL, 128)
    col = lax.broadcasted_iota(jnp.int32, shape, 1)
    j = col % 16
    for kind in range(1 + NPART):
        a, b = key_places(kind, shape)
        ok = b < WIN
        along_a = jnp.where(ok & (j == a) & (j < WIN), 1.0, 0.0)
        along_a = jnp.where(jnp.logical_not(ok) & (col % SEG == 15), MASKED, along_a)
        along_b = jnp.where(ok & (j == b) & (j < WIN), 1.0, 0.0)
        for head in range(3):
            mine = col // SEG == head
            e_ref[kind, head, :, pl.ds(0, 128)] = jnp.where(mine, along_a, 0.0).astype(BF)
            e_ref[kind, head, :, pl.ds(128, 128)] = jnp.where(mine, along_b, 0.0).astype(BF)


def build_relative(rel_refs, out_ref):
    out_ref[...] = jnp.zeros(out_ref.shape, BF)
    i = lax.broadcasted_iota(jnp.int32, (RELS, 128), 0)
    lane = lax.broadcasted_iota(jnp.int32, (RELS, 128), 1)
    turn = (lane % SEG == 26 - i).astype(BF)
    lane64 = lax.broadcasted_iota(jnp.int32, (HEAD_DIM, 128), 1) // SEG
    for axis in range(2):
        rev = tn(rel_refs[axis][...], turn)
        for h in range(HALF_HEADS):
            out_ref[pl.ds(h * HEAD_DIM, HEAD_DIM), pl.ds((h // 3) * 256 + axis * 128, 128)] = (
                jnp.where(lane64 == h % 3, rev, 0.0).astype(BF)
            )


def slots():
    return [(k, k * FULL, FULL) for k in range(NFULL)] + [
        (NFULL + k, PBASE + k * PART, PART) for k in range(NPART)
    ]


def half_cols(start, half):
    return pl.ds(pl.multiple_of(start + half * HALF, 128), HALF)


def norm(rows):
    centered = rows - jnp.mean(rows, axis=-1, keepdims=True)
    r = lax.rsqrt(jnp.mean(centered * centered, axis=-1, keepdims=True) + EPSILON)
    return centered * r, r


def forward_kernel(images, direct, *refs):
    it = iter(refs)

    def take(n):
        return [next(it) for _ in range(n)]

    x_ref, c_ref = take(2)
    weights = take(4 if direct else 2)
    g1_ref, b1_ref, qkv_b, g2_ref, b2_ref, pb_ref, db_ref, relh_ref, relw_ref = take(9)
    x_o, c_o, n1_o, qkv_o, att_o, p_o, mid_o, xhat_o, n2_o, r2_o = take(10)
    if direct:
        wq_o, wp_o, wu, wd = take(4)
    e_o, rel_o = take(2)
    stage, xw, cw, n1, qkv, att, p_buf, mid, xhat2, n2, r2 = take(11)
    wq, wp, e, rel_blk, x_scr, bias_v, vec, ss, rs = take(9)
    if direct:
        gss, grs, gls = take(3)
    os, = take(1)
    me = coords()
    f, ctx, tp = me
    pack = pack_matrix()

    def stage_tokens(a, src):
        for i in range(images):
            for u in range(2):
                stage[a, i, u] = jnp.dot(
                    pack, src[i, pl.ds(u * 128, 128)], preferred_element_type=F32
                ).astype(BF)

    out_copies = []

    def write(src, dst):
        cp = pltpu.make_async_copy(src, dst, os.at[len(out_copies)])
        cp.start()
        out_copies.append(cp)

    stage_tokens(0, x_ref)
    group_barrier(((1 - f, ctx, tp),) if direct else ())
    start_pieces(stage, xw, 0, images, me, ss, rs)
    if direct:
        wq_s, wp_s, wu_s, wd_s = weights
        shards = (wq_s.at[0], wq_s.at[1], wq_s.at[2], wp_s, wu_s, wd_s)
        gather = Gather(shards, (wq.at[0], wq.at[1], wq.at[2], wp, wu, wd), me, gss, grs, gls)
        for w in range(3):
            gather.start_own(w, (0, 2))
    else:
        load = (pltpu.make_async_copy(weights[0], wq, os.at[18]), pltpu.make_async_copy(weights[1], wp, os.at[19]))
        for cp in load:
            cp.start()
    build_keys(e)
    build_relative((relh_ref, relw_ref), rel_blk)
    write(e, e_o)
    write(rel_blk, rel_o)
    rows = [g1_ref[...], b1_ref[...], qkv_b[0, :], None, qkv_b[1, :], g2_ref[...], b2_ref[...], pb_ref[...], db_ref[...]]
    for n, row in enumerate(rows):
        vec[n:n + 1, :] = jnp.zeros((1, D), F32) if row is None else row.astype(F32).reshape(1, D)
    bias_v[...] = vec[4:5, :]
    stage_tokens(1, c_ref)
    if direct:
        for w in range(3):
            gather.on(w, 0, (4,))
    wait_pieces(xw, 0, me, rs)
    if direct:
        for w in range(3):
            gather.start_own(w, (1,))
    for slot, base, rows in slots():
        here = pl.ds(base, rows)
        real = row_real(slot, rows)
        x = jnp.where(real, xw[here].astype(F32), 0.0)
        xw[here] = x.astype(BF)
        xhat, _ = norm(x)
        n1[here] = jnp.where(real, xhat * vec[0:1, :] + vec[1:2, :], 0.0).astype(BF)
    write(xw, x_o)
    write(n1, n1_o)
    if direct:
        for w in range(3):
            gather.arrived(w, (2, 4))
        gather.start_own(4)
    else:
        for cp in load:
            cp.wait()
        start_pieces(stage, cw, 1, images, me, ss, rs)

    for turn in range(2):
        half = tp // 2 if turn == 0 else 1 - tp // 2

        @pl.loop(0, 3)
        def _(n, half=half):
            out = nt(n1[...], wq[n, half_cols(0, half), :]) + vec[pl.ds(2 + n, 1), half_cols(0, half)]
            qkv[:, half_cols(n * D, half)] = out.astype(BF)

        @pl.loop(0, NFULL)
        def _(n, half=half, turn=turn):
            attention_half(qkv, rel_blk, bias_v, e.at[0], att, p_buf, pl.multiple_of(n * FULL, 16), FULL, None, x_scr, half)
            if not direct:
                return
            if turn == 0:
                @pl.when(n == 0)
                def _():
                    for w in range(3):
                        gather.on(w, 1, (3, 5))
                    gather.start_own(3)
                    gather.start_own(5)

                @pl.when(n == 1)
                def _():
                    gather.forward_x(4)
                    start_pieces(stage, cw, 1, images, me, ss, rs)

                @pl.when(n == 2)
                def _():
                    gather.forward_y(4)
                    for w in range(3):
                        gather.on(w, 3, (6,))
            else:
                @pl.when(n == 0)
                def _():
                    gather.forward_x(3)
                    gather.forward_y(3)
                    gather.forward_x(5)

                @pl.when(n == 1)
                def _():
                    gather.forward_y(5)
                    gather.forward_second(4)

                @pl.when(n == 2)
                def _():
                    gather.forward_second(3)

        @pl.loop(0, NPART)
        def _(n, half=half):
            attention_half(qkv, rel_blk, bias_v, e.at[1 + n], att, p_buf,
                           pl.multiple_of(PBASE + n * PART, 16), PART, narrow_flag(n), x_scr, half)

        if direct:
            if turn == 0:
                for w in range(3):
                    gather.arrived(w, (5, 6))
                write(wq, wq_o)
            else:
                gather.forward_second(5)
                gather.forward_z(4)

    write(qkv, qkv_o)
    write(att, att_o)
    write(p_buf, p_o)
    if direct:
        gather.arrived(3)
        write(wp, wp_o)

    @pl.loop(0, ROWS // CHUNK)
    def _(n):
        here = pl.ds(pl.multiple_of(n * CHUNK, 16), CHUNK)
        middle = xw[here].astype(F32) + jnp.dot(att[here], wp[...], preferred_element_type=F32) + vec[7:8, :]
        xhat, r = norm(middle)
        r2[here] = r
        xhat2[here] = xhat.astype(BF)
        n2[here] = (xhat * vec[5:6, :] + vec[6:7, :]).astype(BF)
        mid[here] = middle + vec[8:9, :]

    for src, dst in ((n2, n2_o), (mid, mid_o), (xhat2, xhat_o), (r2, r2_o)):
        write(src, dst)
    if direct:
        gather.forward_z(5)
    wait_pieces(cw, 1, me, rs)
    for slot, base, rows in slots():
        here = pl.ds(base, rows)
        cw[here] = jnp.where(row_real(slot, rows), cw[here].astype(F32), 0.0).astype(BF)
    write(cw, c_o)
    if direct:
        for w in (4, 5):
            gather.arrived(w)
        for w in range(UNITS):
            gather.sent(w)
    for a in range(2):
        finish_piece_sends(stage, a, images, me, ss)
    for cp in out_copies:
        cp.wait()


def forward(x3, c3, shards, whole, small):
    images = x3.shape[0]
    any_spec = pl.BlockSpec(memory_space=pl.ANY)
    vmem = pl.BlockSpec(memory_space=pltpu.VMEM)
    direct = whole is None
    dma = pltpu.SemaphoreType.DMA
    shape = jax.ShapeDtypeStruct
    tokens = shape((ROWS, D), BF)
    keys = (1 + NPART, 3, FULL, 256)
    outs = [tokens, tokens, tokens, shape((ROWS, 3 * D), BF), tokens, shape((ROWS, HEADS * 256), BF)]
    outs += [shape((ROWS, D), F32), tokens, tokens, shape((ROWS, 1), F32)]
    if direct:
        outs += [shape(s, BF) for s in ((3, D, D), (D, D), (4 * D, D), (4 * D, D))]
    outs += [shape(keys, BF), shape((HALF, 512), BF)]
    v = pltpu.VMEM
    scratch = [v((2, images, 2, PIECE, D), BF)] + [v((ROWS, D), BF)] * 3
    scratch += [v((ROWS, 3 * D), BF), v((ROWS, D), BF), v((ROWS, HEADS * 256), BF)]
    scratch += [v((ROWS, D), F32), v((ROWS, D), BF), v((ROWS, D), BF), v((ROWS, 1), F32)]
    scratch += [v((3, D, D), BF), v((D, D), BF), v(keys, BF), v((HALF, 512), BF), v((FULL, 512), BF)]
    scratch += [v((1, D), F32), v((16, D), F32)]
    scratch += [dma((2, images * 10)), dma((2, NFULL + NPART, PAIRS))]
    if direct:
        scratch += [dma((UNITS, 13)), dma((UNITS, 13)), dma((UNITS,))]
    scratch += [dma((20,))]
    weights = list(shards) if direct else list(whole)
    return pl.pallas_call(
        functools.partial(forward_kernel, images, direct),
        out_shape=outs,
        in_specs=[vmem, vmem] + [any_spec] * len(weights) + [vmem] * len(small),
        out_specs=[any_spec] * len(outs),
        scratch_shapes=scratch,
        compiler_params=pltpu.CompilerParams(
            collective_id=0, has_side_effects=True, vmem_limit_bytes=VMEM_LIMIT
        ),
        name="forward",
    )(x3, c3, *weights, *small)


def barrel(x, shift, left):
    lanes = x.shape[-1]
    for bit in (1, 2, 4, 8):
        moved = pltpu.roll(x, lanes - bit if left else bit, 1)
        x = jnp.where((shift // bit) % 2 == 1, moved, x)
    return x


def row_places(rows, narrow):
    r = lax.broadcasted_iota(jnp.int32, (rows, 128), 0)
    if narrow is None:
        return r // 16, r % 16
    is_narrow = narrow > 0
    return jnp.where(is_narrow, r // 8, r // 16), jnp.where(is_narrow, r % 8, r % 16)


def half_mask(hh):
    lane = lax.broadcasted_iota(jnp.int32, (1, 128), 1)
    return ((lane // 64) == hh).astype(BF)


def nt(a, b):
    return lax.dot_general(a, b, (((1,), (1,)), ((), ())), preferred_element_type=F32)


def tn(a, b):
    return lax.dot_general(a, b, (((0,), (0,)), ((), ())), preferred_element_type=F32)


def key_rows(ref, base, rows, col, fill):
    part = ref[pl.ds(base, rows), pl.ds(pl.multiple_of(col, 128), 128)]
    if rows == FULL:
        return part
    return jnp.concatenate([part, jnp.broadcast_to(fill, (FULL - rows, 128)).astype(BF)], axis=0)


def attention_half(qkv, rel_blk, bias_v, e_at, o_ref, p_ref, base, rows, narrow, x_scr, half):
    a_row, b_row = row_places(rows, narrow)
    here = pl.ds(base, rows)
    q_all = qkv[here, half_cols(0, half)]
    lane = lax.broadcasted_iota(jnp.int32, (rows, 128), 1) % SEG
    raw = jnp.dot(q_all, rel_blk[...], preferred_element_type=F32)
    for g in range(2):
        for axis, pos in ((0, a_row), (1, b_row)):
            at = g * 256 + axis * 128
            v = barrel(raw[:, at:at + 128], jnp.maximum(13 - pos, 0), True)
            hi = v.astype(BF).astype(F32)
            lo = pltpu.roll(v - hi, 16, 1)
            mix = jnp.where(lane < WIN, hi, jnp.where(lane >= 16, lo, 0.0))
            if axis == 0:
                mix = jnp.where(lane == 15, 1.0, mix)
            x_scr[pl.ds(0, rows), pl.ds(at, 128)] = mix.astype(BF)
    for hp in range(3):
        cols = pl.ds(pl.multiple_of(half * HALF + hp * 128, 128), 128)
        q = q_all[:, hp * 128:(hp + 1) * 128]
        k = key_rows(qkv, base, rows, D + half * HALF + hp * 128, jnp.zeros((1, 128), BF))
        v = key_rows(qkv, base, rows, 2 * D + half * HALF + hp * 128, bias_v[:, cols])
        out = jnp.zeros((rows, 128), F32)
        for hh in range(2):
            h = hp * 2 + hh
            x = x_scr[pl.ds(0, rows), pl.ds((h // 3) * 256, 256)]
            s = nt(q, k * (half_mask(hh) * 0.125)) + nt(x, e_at[h % 3])
            p = jnp.exp(s - jnp.max(s, axis=-1, keepdims=True))
            p = (p * (1.0 / jnp.sum(p, axis=-1, keepdims=True))).astype(BF)
            p_ref[here, pl.ds(pl.multiple_of((half * HALF_HEADS + h) * 256, 128), FULL)] = p
            out = out + jnp.dot(p, v * half_mask(hh), preferred_element_type=F32)
        o_ref[here, cols] = out.astype(BF)


def narrow_flag(k):
    _, ctx, tp = coords()
    q = (3 - ctx) * 8 + tp * 2 + k
    is_narrow = ((q < 15) & (q % 5 == 4)) | ((q >= 15) & (q < 27))
    return jnp.where(is_narrow, 1, 0)


def attention_back_half(qkv, do_ref, rel_blk, bias_v, e_at, p_ref, d_scr, acc_scr, pad_acc, rel_acc, base, rows,
                        narrow, half):
    a_row, b_row = row_places(rows, narrow)
    here = pl.ds(base, rows)
    dx = [jnp.zeros((rows, 256), F32)] * 2
    for hp in range(3):
        cols = pl.ds(pl.multiple_of(half * HALF + hp * 128, 128), 128)
        k_at, v_at = D + half * HALF + hp * 128, 2 * D + half * HALF + hp * 128
        q = qkv[here, cols]
        k = key_rows(qkv, base, rows, k_at, jnp.zeros((1, 128), BF))
        v = key_rows(qkv, base, rows, v_at, bias_v[:, cols])
        do = do_ref[here, cols]
        dq = jnp.zeros((rows, 128), F32)
        dk = jnp.zeros((FULL, 128), F32)
        dv = jnp.zeros((FULL, 128), F32)
        for hh in range(2):
            h = hp * 2 + hh
            mask = half_mask(hh)
            do_m = do * mask
            dp = nt(do_m, v)
            p_low = p_ref[pl.ds(0, rows), pl.ds(h * 256, FULL)]
            t = p_low.astype(F32)
            tp = t * dp
            ds = (tp - t * jnp.sum(tp, axis=-1, keepdims=True)).astype(BF)
            dq = dq + jnp.dot(ds, k * (mask * 0.125), preferred_element_type=F32)
            dx[h // 3] = dx[h // 3] + jnp.dot(ds, e_at[h % 3], preferred_element_type=F32)
            dk = dk + tn(ds, q * (mask * 0.125))
            dv = dv + tn(p_low, do_m)
        acc_scr[pl.ds(0, rows), pl.ds(hp * 128, 128)] = dq
        qkv[here, pl.ds(pl.multiple_of(k_at, 128), 128)] = dk[:rows].astype(BF)
        qkv[here, pl.ds(pl.multiple_of(v_at, 128), 128)] = dv[:rows].astype(BF)
        if rows < FULL:
            pad_acc[:, cols] += jnp.sum(dv[rows:], axis=0, keepdims=True)
    lane = lax.broadcasted_iota(jnp.int32, (rows, 128), 1) % SEG
    for g in range(2):
        for axis, pos in ((0, a_row), (1, b_row)):
            v = jnp.where(lane < WIN, dx[g][:, axis * 128:(axis + 1) * 128], 0.0)
            v = barrel(v, jnp.maximum(13 - pos, 0), False)
            d_scr[pl.ds(0, rows), pl.ds(g * 256 + axis * 128, 128)] = v.astype(BF)
    d = d_scr[pl.ds(0, rows), :]
    rel_acc[pl.ds(0, 512), pl.ds(0, HALF)] += tn(d, qkv[here, half_cols(0, half)])
    qkv[here, half_cols(0, half)] = (acc_scr[pl.ds(0, rows), :] + nt(d, rel_blk[...])).astype(BF)


TILE = (D, D, 192, 192, 192, 192)
HALVES = ((384, D), (D, 384), (192, 384), (192, 384), (192, 384), (192, 384))
Z_PIECES = (2, 2, 1, 1, 1, 1)
CHUNK = ROWS // 2
SUMS = 16
FEW = 12 * 6 + 2 * SEG


def add_rows(dst, src):
    rows = dst.shape[0]
    size = 64

    @pl.loop(0, rows // size)
    def _(n):
        here = pl.ds(pl.multiple_of(n * size, 16), size)
        dst[here] = (dst[here].astype(F32) + src[here].astype(F32)).astype(BF)


class Reduce:
    def __init__(self, grads, me, outs, r1, rx, ry, rz, s1, v1, s2, v2, s3, v3, sz, vz, so):
        self.grads, self.outs = grads, outs
        self.r1u, self.r1d, self.r1p = r1
        self.rx, self.ry, self.rz = rx, ry, rz
        self.s1, self.v1, self.s2, self.v2, self.s3, self.v3 = s1, v1, s2, v2, s3, v3
        self.sz, self.vz, self.so = sz, vz, so
        f, ctx, tp = me
        self.f, self.g = f, 1 - f
        self.c, self.own = tp % 2, tp // 2
        self.to_s = (f, ctx, tp + 1 - 2 * self.c)
        self.to_x = (1 - f, ctx, tp)
        self.to_y = (f, ctx, (tp + 2) % 4)
        self.outer = (ctx == 0) | (ctx == 3)
        self.inner = jnp.logical_not(self.outer)
        self.to_mid = (f, 3 - ctx, tp)
        self.to_in = (f, jnp.where(ctx == 0, 1, 2), tp)
        self.to_out = (f, jnp.where(ctx == 1, 0, 3), tp)

    def tile(self, w, t):
        return self.grads[w].at[pl.ds(pl.multiple_of(t * TILE[w], 16), TILE[w])]

    def half(self, w, t, f):
        if w == 0:
            return self.grads[w].at[pl.ds(pl.multiple_of(t * D + f * 384, 16), 384)]
        return self.grads[w].at[
            pl.ds(pl.multiple_of(t * TILE[w], 16), TILE[w]), pl.ds(pl.multiple_of(f * 384, 128), 384)
        ]

    def landing(self, w, j):
        if w < 2:
            return (self.r1u, self.r1d)[w].at[j]
        if w == 2:
            return self.r1p.at[j]
        return self.r1d.at[(w - 3) // 2, pl.ds(pl.multiple_of(((w - 3) % 2) * 384 + j * 192, 16), 192)]

    def core_copy(self, w, j):
        src = self.tile(w, 1 - self.c + 2 * j)
        return remote(src, self.landing(w, j), self.to_s, self.s1.at[w, j], self.v1.at[w, j])

    def core_send(self, w, j):
        self.core_copy(w, j).start()

    def x_copy(self, w, j):
        src = self.half(w, self.c + 2 * j, self.g)
        return remote(src, self.rx[w].at[j], self.to_x, self.s2.at[w, j], self.v2.at[w, j])

    def core_add(self, w, j):
        self.core_copy(w, j).wait_recv()
        add_rows(self.tile(w, self.c + 2 * j), self.landing(w, j))
        self.x_copy(w, j).start()

    def y_copy(self, w):
        src = self.half(w, self.c + 2 * (1 - self.own), self.f)
        return remote(src, self.ry[w], self.to_y, self.s3.at[w], self.v3.at[w])

    def x_add(self, w, j):
        self.x_copy(w, j).wait_recv()
        add_rows(self.half(w, self.c + 2 * j, self.f), self.rx[w].at[j])

        @pl.when(self.own != j)
        def _():
            self.y_copy(w).start()

    def mine(self, w):
        return self.half(w, self.c + 2 * self.own, self.f)

    def y_add(self, w):
        self.y_copy(w).wait_recv()
        add_rows(self.mine(w), self.ry[w])

        for h in range(Z_PIECES[w]):
            self.z_in(w, h)

    def z_view(self, ref, w, h):
        size = HALVES[w][0] // Z_PIECES[w]
        return ref.at[pl.ds(h * size, size)]

    def z_mine(self, w, h):
        t, size = self.c + 2 * self.own, HALVES[w][0] // Z_PIECES[w]
        if w == 0:
            return self.grads[w].at[pl.ds(pl.multiple_of(t * D + self.f * 384 + h * size, 16), size)]
        return self.grads[w].at[
            pl.ds(pl.multiple_of(t * TILE[w] + h * size, 16), size), pl.ds(pl.multiple_of(self.f * 384, 128), 384)
        ]

    def z_slot(self, w, slot, h):
        return self.z_view(self.rz[w].at[slot], w, h)

    def z_in(self, w, h):
        @pl.when(self.outer)
        def _():
            remote(
                self.z_mine(w, h), self.z_slot(w, 0, h), self.to_in, self.sz.at[w, h, 0], self.vz.at[w, h, 0]
            ).start()

    def z_wait(self, w, h, sem):
        view = self.z_slot(w, 0, h)
        pltpu.make_async_copy(view, view, sem).wait()

    def z_mid(self, w, h):
        @pl.when(self.inner)
        def _():
            self.z_wait(w, h, self.vz.at[w, h, 0])
            mine = self.z_mine(w, h)
            add_rows(mine, self.z_slot(w, 0, h))
            remote(mine, self.z_slot(w, 1, h), self.to_mid, self.sz.at[w, h, 0], self.vz.at[w, h, 1]).start()

    def z_out(self, w, h):
        @pl.when(self.inner)
        def _():
            self.z_wait(w, h, self.vz.at[w, h, 1])
            total = self.z_slot(w, 1, h)
            add_rows(total, self.z_mine(w, h))
            remote(total, self.z_slot(w, 0, h), self.to_out, self.sz.at[w, h, 1], self.vz.at[w, h, 2]).start()
            pltpu.make_async_copy(total, self.z_view(self.outs[w], w, h), self.so.at[w, h]).start()

    def z_end(self, w, h):
        @pl.when(self.outer)
        def _():
            self.z_wait(w, h, self.vz.at[w, h, 2])
            pltpu.make_async_copy(self.z_slot(w, 0, h), self.z_view(self.outs[w], w, h), self.so.at[w, h]).start()

    def sent(self, w):
        for j in range(2):
            self.core_copy(w, j).wait_send()
            self.x_copy(w, j).wait_send()
        self.y_copy(w).wait_send()
        for h in range(Z_PIECES[w]):
            self.z_wait(w, h, self.sz.at[w, h, 0])

            @pl.when(self.inner)
            def _(h=h):
                self.z_wait(w, h, self.sz.at[w, h, 1])

            self.z_wait(w, h, self.so.at[w, h])


def backward_kernel(images, direct, *refs):
    it = iter(refs)

    def take(n):
        return [next(it) for _ in range(n)]

    x_h, c_h, n1_h, qkv_h, att_h, p_h, mid_h, xhat_h, n2_h, r2_h, wq_h, wp_h, wu_h, wd_h, e_h, rel_h = take(16)
    g1_ref, g2_ref, qkv_b, up_ref = take(4)
    staged, few_out = take(2)
    outs = take(4)
    outs = outs[:3] + [outs[3].at[pl.ds(k * 192, 192)] if direct else outs[3].at[k] for k in range(3)]
    cot, att, n2, xhat2, hid, dg = take(6)
    acc, dn2 = take(2)
    wu, wd, wp, wq, dwq, qkv, p_buf, e, rel_blk, d_scr, acc_scr = take(11)
    bias_v, pad_acc, sums, r2, real, vec = take(6)
    ls, ss, rs = take(3)
    if direct:
        r1 = take(3)
        rx, ry, rz = take(6), take(6), take(6)
        few_in, = take(1)
        sems = take(9)
        few_s, few_r = take(2)
    me = coords()
    f, ctx, tp = me
    c, own = tp % 2, tp // 2
    pair_at = (1 - own, own)
    tile_at = [2 * pair_at[n // 2] + n % 2 for n in range(4)]
    loads = {}

    def load(name, src, dst):
        loads[name] = pltpu.make_async_copy(src, dst, ls.at[len(loads)])
        loads[name].start()

    def rows_of(t):
        return pl.ds(pl.multiple_of(t * D, 16), D)

    load("n2", n2_h, n2)
    for n, t in enumerate(tile_at):
        load(("wu", n), wu_h.at[rows_of(t)], wu.at[rows_of(t)])
        if n == 0:
            load("cot", c_h, cot)
        load(("wd", n), wd_h.at[rows_of(t)], wd.at[rows_of(t)])
        if n == 0:
            load("acc", mid_h, acc)
    load("xhat", xhat_h, xhat2)
    load("r2", r2_h, r2)
    load("wp", wp_h, wp)
    load("att", att_h, att)
    load("qkv", qkv_h, qkv)
    load("e", e_h, e)
    load("rel", rel_h, rel_blk)
    load("wq", wq_h, wq)
    steps = [(turn, slot) for turn in range(2) for slot in range(NFULL + NPART)]

    def p_copy(n):
        turn, slot = steps[n]
        base, rows = (slot * FULL, FULL) if slot < NFULL else (PBASE + (slot - NFULL) * PART, PART)
        cols = pl.ds(pl.multiple_of(pair_at[turn] * HALF_HEADS * 256, 128), HALF_HEADS * 256)
        return pltpu.make_async_copy(
            p_h.at[pl.ds(base, rows), cols], p_buf.at[n % 2, pl.ds(0, rows)], ls.at[20 + n % 2]
        )

    p_copy(0).start()
    p_copy(1).start()
    group_barrier(((1 - f, ctx, tp),) if direct else ())
    grads = (wu, wd, wp, dwq.at[0], dwq.at[1], dwq.at[2])
    red = Reduce(grads, me, outs, r1, rx, ry, rz, *sems) if direct else None
    sums[...] = jnp.zeros_like(sums)
    pad_acc[...] = jnp.zeros_like(pad_acc)
    vec[0:1, :] = g1_ref[...].astype(F32).reshape(1, D)
    vec[5:6, :] = g2_ref[...].astype(F32).reshape(1, D)
    bias_v[...] = qkv_b[1, :].astype(F32).reshape(1, D)
    up_all = up_ref[...].astype(F32)
    for k in range(4):
        vec[9 + k:10 + k, :] = up_all[k * D:(k + 1) * D].reshape(1, D)
    for slot, base, rows in slots():
        real[pl.ds(base, rows)] = jnp.where(row_real(slot, rows), 1.0, 0.0)

    def row_chunks(body):
        @pl.loop(0, ROWS // CHUNK)
        def _(n):
            body(pl.ds(pl.multiple_of(n * CHUNK, 16), CHUNK))

    for name in ("n2", "cot"):
        loads[name].wait()
    for n in range(4):
        loads["wu", n].wait()
        loads["wd", n].wait()
        pair = pair_at[n // 2]
        t = tile_at[n]
        base = pl.multiple_of(t * D, 16)

        @pl.loop(0, 3)
        def _(j, base=base, t=t):
            units = pl.ds(pl.multiple_of(j * 256, 128), 256)
            gate = jnp.dot(n2[...], wu[pl.ds(base, D), units], preferred_element_type=F32)
            hidden, slope = gelu_both(gate + vec[pl.ds(9 + t, 1), units])
            hid[:, units] = hidden.astype(BF)
            there = pl.ds(pl.multiple_of(base + j * 256, 16), 256)
            d_gate = (nt(cot[...], wd[there, :]) * slope).astype(BF)
            dg[:, units] = d_gate
            sums[pl.ds(8 + t, 1), units] = jnp.sum(d_gate.astype(F32), axis=0, keepdims=True)

        if direct and n:
            @pl.when(c == (n - 1) % 2)
            def _(n=n):
                red.core_add(1, pair_at[(n - 1) // 2])
                red.core_add(0, pair_at[(n - 1) // 2])

        tile = pl.ds(base, D)

        if n == 0:
            loads["acc"].wait()

        def through(here, tile=tile, n=n):
            acc[here] += jnp.dot(hid[here], wd[tile, :], preferred_element_type=F32)
            more = nt(dg[here], wu[tile, :])
            dn2[here] = dn2[here] + more if n else more

        row_chunks(through)

        @pl.loop(0, 3)
        def _(j, base=base):
            part = pl.ds(pl.multiple_of(j * 256, 128), 256)
            there = pl.ds(pl.multiple_of(base + j * 256, 16), 256)
            wd[there, :] = tn(hid[:, part], cot[...]).astype(BF)
            wu[there, :] = tn(n2[:, part], dg[...]).astype(BF)

        if direct:
            @pl.when(c != n % 2)
            def _(pair=pair):
                red.core_send(1, pair)
                red.core_send(0, pair)

    if direct:
        red.x_add(1, pair_at[0])
        red.x_add(0, pair_at[0])

    for name in ("xhat", "r2", "wp", "att"):
        loads[name].wait()
    load_n1 = pltpu.make_async_copy(n1_h, n2, ls.at[22])
    load_n1.start()

    def back_two(here):
        n = dn2[here]
        xhat = xhat2[here].astype(F32)
        c_rows = cot[here].astype(F32)
        m = n * vec[5:6, :]
        sums[5:6, :] += jnp.sum(n * xhat, axis=0, keepdims=True)
        sums[6:7, :] += jnp.sum(n, axis=0, keepdims=True)
        sums[7:8, :] += jnp.sum(c_rows, axis=0, keepdims=True)
        mean = jnp.mean(m, axis=-1, keepdims=True)
        mean_x = jnp.mean(m * xhat, axis=-1, keepdims=True)
        d_mid = c_rows + r2[here] * (m - mean - xhat * mean_x)
        dn2[here] = d_mid
        branch = d_mid.astype(BF)
        xhat2[here] = branch
        sums[4:5, :] += jnp.sum(branch.astype(F32), axis=0, keepdims=True)
        dg[here] = acc[here].astype(BF)
        hid[here] = nt(branch, wp[...]).astype(BF)

    for n in range(ROWS // CHUNK):
        back_two(pl.ds(n * CHUNK, CHUNK))
        if direct and n == 0:
            @pl.when(c == 1)
            def _():
                red.core_add(1, own)
                red.core_add(0, own)
    places = window_places(ctx, tp)

    def tokens_out(a, src_ref):
        for n, (slot, p, rows, exists, image, u, col, d_ctx, d_tp, row) in enumerate(places):
            def go(n=n, rows=rows, image=image, u=u, col=col, d_ctx=d_ctx, d_tp=d_tp, row=row):
                src = src_ref.at[pl.ds(row, rows)]
                dst = staged.at[a, image, u, pl.ds(pl.multiple_of(col * 32, 16), rows)]
                send_or_copy(src, dst, (d_ctx, d_tp), me, ss.at[a, n], rs.at[a, image, u, col])
            if exists is None:
                go()
            else:
                pl.when(exists)(go)

    def tokens_done(a, src_ref):
        for i in range(images):
            for u in range(2):
                for col in range(5):
                    dst = staged.at[a, i, u, pl.ds(col * 32, 32 if col < 4 else 16)]
                    pltpu.make_async_copy(dst, dst, rs.at[a, i, u, col]).wait()
        for n, (slot, p, rows, exists, image, u, col, d_ctx, d_tp, row) in enumerate(places):
            def done(n=n, rows=rows, d_ctx=d_ctx, d_tp=d_tp, row=row):
                wait_sent(src_ref.at[pl.ds(row, rows)], (d_ctx, d_tp), me, ss.at[a, n])
            if exists is None:
                done()
            else:
                pl.when(exists)(done)

    @pl.loop(0, 3)
    def _(j):
        part = pl.ds(pl.multiple_of(j * 256, 128), 256)
        wp[pl.ds(pl.multiple_of(j * 256, 16), 256), :] = tn(att[:, part], xhat2[...]).astype(BF)

    if direct:
        red.core_send(2, 0)
        red.core_send(2, 1)

    load_x = pltpu.make_async_copy(x_h, xhat2, ls.at[23])
    load_x.start()
    for name in ("qkv", "e", "rel"):
        loads[name].wait()
    load_n1.wait()
    acc[pl.ds(0, 512), pl.ds(0, HALF)] = jnp.zeros((512, HALF), F32)
    for n, (turn, slot) in enumerate(steps):
        pair = pair_at[turn]
        p_copy(n).wait()
        base, rows = (slot * FULL, FULL) if slot < NFULL else (PBASE + (slot - NFULL) * PART, PART)
        kind = 0 if slot < NFULL else 1 + slot - NFULL
        narrow = None if slot < NFULL else narrow_flag(slot - NFULL)
        attention_back_half(qkv, hid, rel_blk, bias_v, e.at[kind], p_buf.at[n % 2], d_scr, acc_scr,
                            pad_acc, acc, base, rows, narrow, pair)
        if n + 2 < len(steps):
            p_copy(n + 2).start()
        if slot == NFULL + NPART - 1:
            for w in range(3):
                d_cols = half_cols(w * D, pair)
                dwq[w, half_cols(0, pair), :] = tn(qkv[:, d_cols], n2[...]).astype(BF)
                if direct:
                    red.core_send(3 + w, pair)
        if n == 2:
            tokens_out(0, dg)
        if not direct:
            continue
        if n == 0:
            red.core_add(2, 0)
            red.core_add(2, 1)
        elif n == 5:
            for w in (3, 4, 5):
                red.core_add(w, pair_at[0])
        elif n == 6:
            red.x_add(1, own)
            red.y_add(1)
        elif n == 7:
            red.x_add(0, own)
            red.y_add(0)
        elif n == 8:
            red.z_mid(1, 0)
        elif n == 9:
            red.z_mid(1, 1)
            for w in (3, 4, 5):
                red.core_add(w, own)

    load_x.wait()
    loads["wq"].wait()

    def back_one(here):
        d_qkv = qkv[here, :]
        n = jnp.zeros((CHUNK, D), F32)
        for w in range(3):
            n = n + jnp.dot(d_qkv[:, w * D:(w + 1) * D], wq[w], preferred_element_type=F32)
        sums[2:3, :] += jnp.sum(d_qkv[:, :D].astype(F32), axis=0, keepdims=True)
        sums[3:4, :] += jnp.sum(d_qkv[:, 2 * D:].astype(F32), axis=0, keepdims=True)
        n = n * real[here]
        rows = xhat2[here].astype(F32)
        centered = rows - jnp.mean(rows, axis=-1, keepdims=True)
        r = lax.rsqrt(jnp.mean(centered * centered, axis=-1, keepdims=True) + EPSILON)
        xhat = centered * r
        sums[0:1, :] += jnp.sum(n * xhat, axis=0, keepdims=True)
        sums[1:2, :] += jnp.sum(n, axis=0, keepdims=True)
        m = n * vec[0:1, :]
        mean = jnp.mean(m, axis=-1, keepdims=True)
        mean_x = jnp.mean(m * xhat, axis=-1, keepdims=True)
        cot[here] = (dn2[here] + r * (m - mean - xhat * mean_x)).astype(BF)

    if direct:
        red.x_add(2, 0)
        red.x_add(2, 1)
        red.z_mid(0, 0)
        red.z_out(1, 0)
    back_one(pl.ds(0, CHUNK))
    if direct:
        red.z_mid(0, 1)
        red.z_out(1, 1)
        for w in (3, 4, 5):
            red.x_add(w, pair_at[0])
        red.y_add(2)
    back_one(pl.ds(CHUNK, CHUNK))
    tokens_out(1, cot)

    sums[3:4, :] += pad_acc[...]
    order = (0, 1, 2, 3, 4, 5, 6, 7, 8, 9, 10, 11)
    for n, row in enumerate(order):
        for k in range(6):
            few_out[pl.ds(n * 6 + k, 1), :] = sums[pl.ds(row, 1), pl.ds(k * 128, 128)]
    lane = lax.broadcasted_iota(jnp.int32, (SEG, 128), 1) // HEAD_DIM
    for axis in range(2):
        total = jnp.zeros((SEG, 128), F32)
        for h in range(HALF_HEADS):
            piece = acc[pl.ds((h // 3) * 256 + axis * 128 + (h % 3) * SEG, SEG), pl.ds((h // 2) * 128, 128)]
            total = total + jnp.where(lane == h % 2, piece, 0.0)
        few_out[pl.ds(72 + axis * SEG, SEG), :] = total

    if direct:
        steps = (red.to_s, red.to_x, red.to_y, (f, ctx + 1 - 2 * (ctx % 2), tp), (f, (ctx + 2) % 4, tp))

        def few_copy(n):
            return remote(few_in.at[5 + n], few_in.at[n], steps[n], few_s.at[n], few_r.at[n])

        def few_start(n):
            few_in[5 + n] = few_out[...]
            few_copy(n).start()

        def few_add(n):
            few_copy(n).wait_recv()
            few_out[...] = few_out[...] + few_in[n]

        few_start(0)
        red.z_end(1, 0)
        red.z_out(0, 0)
        red.z_mid(2, 0)
        for w in (3, 4, 5):
            red.x_add(w, own)
        few_add(0)
        few_start(1)
        red.y_add(3)
        red.z_end(1, 1)
        red.z_out(0, 1)
        red.z_end(0, 0)
        red.y_add(4)
        red.z_mid(3, 0)
        red.z_out(2, 0)
        few_add(1)
        few_start(2)
        red.y_add(5)
        red.z_mid(4, 0)
        red.z_out(3, 0)
        red.z_end(0, 1)
        red.z_end(2, 0)
        few_add(2)
        few_start(3)
        red.z_mid(5, 0)
        red.z_out(4, 0)
        red.z_end(3, 0)
        few_add(3)
        few_start(4)
        red.z_out(5, 0)
        red.z_end(4, 0)
        red.z_end(5, 0)
        few_add(4)
        for w in range(6):
            red.sent(w)
        for n in range(5):
            few_copy(n).wait_send()
    else:
        for n, src in enumerate((wu, wd, wp, dwq.at[0], dwq.at[1], dwq.at[2])):
            cp = pltpu.make_async_copy(src, outs[n], ls.at[n])
            cp.start()
            cp.wait()
    tokens_done(0, dg)
    tokens_done(1, cot)


def backward(inputs, small, images, direct):
    any_spec = pl.BlockSpec(memory_space=pl.ANY)
    vmem = pl.BlockSpec(memory_space=pltpu.VMEM)
    dma = pltpu.SemaphoreType.DMA
    shape = jax.ShapeDtypeStruct
    n_places = NFULL * PAIRS + NPART * (4 + PAIRS)
    wholes = ((4 * D, D), (4 * D, D), (D, D), (D, D), (D, D), (D, D))
    out_shape = [shape((2, images, 2, PIECE, D), BF), shape((FEW, 128), F32)]
    out_shape += [shape(s, BF) for s in (HALVES if direct else wholes)[:3]]
    out_shape += [shape((576, 384) if direct else (3, D, D), BF)]
    v = pltpu.VMEM
    scratch = [v((ROWS, D), BF)] * 6 + [v((ROWS, D), F32)] * 2
    scratch += [
        v((4 * D, D), BF), v((4 * D, D), BF), v((D, D), BF), v((3, D, D), BF), v((3, D, D), BF),
        v((ROWS, 3 * D), BF), v((2, FULL, HALF_HEADS * 256), BF), v((1 + NPART, 3, FULL, 256), BF), v((HALF, 512), BF),
        v((FULL, 512), BF), v((FULL, HALF), F32),
        v((1, D), F32), v((1, D), F32), v((SUMS, D), F32), v((ROWS, 1), F32), v((ROWS, 1), F32), v((16, D), F32),
        dma((24,)), dma((2, n_places)), dma((2, images, 2, 5)),
    ]
    if direct:
        scratch += [v((2, D, D), BF), v((2, D, D), BF), v((2, 192, D), BF)]
        scratch += [v((2,) + s, BF) for s in HALVES]
        scratch += [v(s, BF) for s in HALVES]
        scratch += [v((2,) + s, BF) for s in HALVES]
        scratch += [v((10, FEW, 128), F32)]
        scratch += [dma((6, 2)), dma((6, 2)), dma((6, 2)), dma((6, 2)), dma((6,)), dma((6,)), dma((6, 2, 2)), dma((6, 2, 3)), dma((6, 2))]
        scratch += [dma((5,)), dma((5,))]
    return pl.pallas_call(
        functools.partial(backward_kernel, images, direct),
        out_shape=out_shape,
        in_specs=[any_spec] * len(inputs) + [vmem] * len(small),
        out_specs=[any_spec, vmem] + [any_spec] * 4,
        scratch_shapes=scratch,
        compiler_params=pltpu.CompilerParams(
            collective_id=1, has_side_effects=True, vmem_limit_bytes=VMEM_BACK
        ),
        name="backward",
    )(*inputs, *small)


SMALL = (0, 1, 4, 5, 6, 7)


def results_kernel(images, n_grads, staged, few, *refs):
    grads, refs = refs[:n_grads], refs[n_grads:]
    tokens, small, (qv, up, rel_h, rel_w), outs = refs[:2], refs[2:8], refs[8:12], refs[12:]
    unpack = pack_matrix()
    for a in range(2):
        for i in range(images):
            for u in range(2):
                tokens[a][i, pl.ds(u * 128, 128)] = tn(unpack, staged[a, i, u]).astype(BF)
    for row, out in zip(SMALL, small):
        out[...] = few[pl.ds(row * 6, 6), :]
    for n in range(2):
        for k in range(6):
            qv[pl.ds(n, 1), pl.ds(k * 128, 128)] = few[pl.ds((2 + n) * 6 + k, 1), :]
    up[...] = few[pl.ds(48, 24), :]
    for axis, out in enumerate((rel_h, rel_w)):
        table = few[pl.ds(72 + axis * SEG, SEG), :]
        table = table + pltpu.roll(table, HEAD_DIM, 1)
        for j in range(RELS):
            out[pl.ds(j, 1), :] = table[26 - j:27 - j, :HEAD_DIM]
    for src, dst in zip(grads, outs):
        rows = src.shape[0]

        @pl.loop(0, rows // 64)
        def _(k, src=src, dst=dst):
            here = pl.ds(pl.multiple_of(k * 64, 16), 64)
            dst[here] = src[here].astype(F32)


def results(staged, few, grads):
    images = staged.shape[1]
    vmem = pl.BlockSpec(memory_space=pltpu.VMEM)
    shape = jax.ShapeDtypeStruct
    outs = [shape((images, 256, D), BF)] * 2 + [shape((6, 128), F32)] * 6
    outs += [shape((2, D), F32), shape((24, 128), F32), shape((RELS, HEAD_DIM), F32), shape((RELS, HEAD_DIM), F32)]
    outs += [shape(g.shape, F32) for g in grads]
    return pl.pallas_call(
        functools.partial(results_kernel, images, len(grads)),
        out_shape=outs,
        in_specs=[vmem] * (2 + len(grads)),
        out_specs=[vmem] * len(outs),
        compiler_params=pltpu.CompilerParams(vmem_limit_bytes=VMEM_LIMIT),
        name="results",
    )(staged, few, *grads)


def gelu_both(u):
    x = jnp.abs(u) * math.sqrt(0.5)
    t = 1.0 / (1.0 + 0.3275911 * x)
    e = jnp.exp(-0.5 * u * u)
    poly = t * (0.254829592 + t * (-0.284496736 + t * (1.421413741 + t * (-1.453152027 + t * 1.061405429))))
    tail = 0.5 * poly * e
    phi = jnp.where(u >= 0, 1.0 - tail, tail)
    return u * phi, phi + u * e * (1.0 / math.sqrt(2 * math.pi))


def whole_weights(shards):
    wq, wp, wu, wd = shards
    wq = lax.all_gather(lax.all_gather(wq, "fsdp", axis=2, tiled=True), "tp", axis=1, tiled=True)
    wp = lax.all_gather(lax.all_gather(wp, "fsdp", axis=1, tiled=True), "tp", axis=0, tiled=True)
    wu = lax.all_gather(lax.all_gather(wu, "fsdp", axis=0, tiled=True), "tp", axis=1, tiled=True)
    wd = lax.all_gather(lax.all_gather(wd, "fsdp", axis=1, tiled=True), "tp", axis=0, tiled=True)
    return wq, wp, wu, wd


def summed_weights(grads):
    out = []
    for w, grad in enumerate(grads):
        part = lax.psum_scatter(grad, "tp", scatter_dimension=0, tiled=True)
        part = lax.psum_scatter(part, "fsdp", scatter_dimension=0 if w == 0 else 1, tiled=True)
        out.append(lax.psum(part, "ctx").astype(F32))
    return out


def local(direct, block_input, ln1_gain, ln1_bias, w_qkv, qkv_bias, rel_h, rel_w, w_proj, proj_bias,
          ln2_gain, ln2_bias, w_up, up_bias, w_down, down_bias, cotangent):
    images = block_input.shape[1]
    x3 = jnp.transpose(block_input, (1, 0, 2))
    c3 = jnp.transpose(cotangent, (1, 0, 2))
    shards = (jnp.transpose(w_qkv, (0, 2, 1)), w_proj, w_up, w_down)
    front = (ln1_gain, ln1_bias, qkv_bias, ln2_gain, ln2_bias, proj_bias, down_bias, rel_h, rel_w)
    if direct:
        kept = forward(x3, c3, shards, None, front)
    else:
        wq, wp, wu, wd = whole_weights(shards)
        wu = jnp.swapaxes(wu.reshape(D, 4, D), 0, 1).reshape(4 * D, D)
        kept = forward(x3, c3, None, (wq, wp), front)
        kept = [*kept[:10], wq, wp, wu, wd, *kept[10:]]
    staged, few, *grads = backward(kept, (ln1_gain, ln2_gain, qkv_bias, up_bias), images, direct)
    if direct:
        small = results(staged, few, grads)
        ou, od, op, oq = small[12:]
        oq = oq.reshape(3, 192, 384)
    else:
        few = lax.psum(few, ("fsdp", "ctx", "tp"))
        small = results(staged, few, ())
        ou, od, op, oq, ok, ov = summed_weights(grads[:3] + [grads[3][k] for k in range(3)])
        oq = jnp.stack([oq, ok, ov])
    out3, dx3, s_g1, s_b1, s_proj, s_g2, s_b2, s_down, s_qv, s_up, s_relh, s_relw = small[:12]
    return (
        jnp.transpose(out3, (1, 0, 2)), jnp.transpose(dx3, (1, 0, 2)), s_g1.reshape(D), s_b1.reshape(D),
        jnp.transpose(oq, (0, 2, 1)), s_qv, s_relh, s_relw,
        op, s_proj.reshape(D), s_g2.reshape(D), s_b2.reshape(D), ou, s_up.reshape(4 * D), od, s_down.reshape(D),
    )


def solution(mesh):
    direct = mesh.shape["fsdp"] == 2
    rows = P(("ctx", "tp"), "fsdp", None)
    w_specs = (P(None, "fsdp", "tp"), P("tp", "fsdp"), P("fsdp", "tp"), P("tp", "fsdp"))
    return jax.shard_map(
        functools.partial(local, direct),
        mesh=mesh,
        in_specs=(rows, P(), P(), w_specs[0], P(), P(), P(), w_specs[1], P(), P(), P(), w_specs[2], P(), w_specs[3], P(), rows),
        out_specs=(rows, rows, P(), P(), w_specs[0], P(), P(), P(), w_specs[1], P(), P(), P(), w_specs[2], P(), w_specs[3], P()),
        check_vma=False,
    )
```

```python
import functools
import math

import jax
import jax.numpy as jnp
from jax import lax
from jax.experimental import pallas as pl
from jax.experimental.pallas import tpu as pltpu
from jax.sharding import PartitionSpec as P

HEAD_DIM = 64
HEADS = 12
WIN = 14
SIDE = 64
BANDS = 4
PAIRS = 7
D = 768
EPSILON = 1e-06
MESH = pl.DeviceIdType.MESH
BF = jnp.bfloat16
F32 = jnp.float32

FULL = 224
PART = 128
NFULL = 3
NPART = 2
PBASE = NFULL * FULL
ROWS = PBASE + NPART * PART
PIECE = 144
HALF_HEADS = 6
HALF = HALF_HEADS * HEAD_DIM
RELS = 2 * WIN - 1
SEG = 32
MASKED = -1e9
VMEM_LIMIT = 60 * 2**20
VMEM_BACK = 63 * 2**20


def coords():
    return lax.axis_index("fsdp"), lax.axis_index("ctx"), lax.axis_index("tp")


def part_kind(ctx, tp, k, images):
    return (3 - ctx) * 8 + tp * 2 + k


def pack_matrix():
    row = lax.broadcasted_iota(jnp.int32, (PIECE, 128), 0)
    col = lax.broadcasted_iota(jnp.int32, (PIECE, 128), 1)
    wide = row < 128
    c = jnp.where(wide, row // 32, 4)
    u = jnp.where(wide, (row % 32) // 16, (row - 128) // 8)
    b = jnp.where(wide, row % 16, (row - 128) % 8)
    source = u * SIDE + c * WIN + b
    return ((source == col) & (b < WIN)).astype(BF)


def piece_places(ctx, tp, images):
    dev = ctx * 4 + tp
    out = []
    for i in range(images):
        for u in range(2):
            m = dev * 2 + u
            band = m // PAIRS
            p = m % PAIRS
            low = band == BANDS
            for c in range(5):
                q_low = i * 5 + c
                if c < 4:
                    f = i * 4 + c
                    d_ctx = jnp.where(low, 3 - q_low // 8, band)
                    d_tp = jnp.where(low, (q_low % 8) // 2, f // 3)
                    slot = jnp.where(low, NFULL + q_low % 2, f % 3)
                    d_row = jnp.where(low, PBASE + (q_low % 2) * PART, (f % 3) * FULL) + p * 32
                    out.append((i, u, c, d_ctx, d_tp, d_row, slot, p))
                else:
                    q = jnp.where(low, q_low, 15 + (3 - band) * 3 + i)
                    d_ctx = 3 - q // 8
                    d_tp = (q % 8) // 2
                    d_row = PBASE + (q % 2) * PART + p * 16
                    out.append((i, u, c, d_ctx, d_tp, d_row, NFULL + q % 2, p))
    return out


def window_places(ctx, tp):
    out = []
    for k in range(NFULL):
        f = tp * 3 + k
        for p in range(PAIRS):
            m = ctx * PAIRS + p
            dev = m // 2
            out.append((k, p, 32, None, f // 4, m % 2, f % 4, dev // 4, dev % 4, k * FULL + p * 32))
    for k in range(NPART):
        q = (3 - ctx) * 8 + tp * 2 + k
        bottom = q < 15
        corner = bottom & (q % 5 == 4)
        right = (q >= 15) & (q < 27)
        qr = jnp.where(right, q - 15, 0)
        band = jnp.where(bottom, BANDS, 3 - qr // 3)
        image = jnp.where(bottom, q // 5, qr % 3)
        base = PBASE + k * PART
        for p in range(PAIRS):
            m = band * PAIRS + p
            dev = jnp.minimum(m // 2, 15)
            place = (image, m % 2, dev // 4, dev % 4)
            if p < 4:
                wide = bottom & jnp.logical_not(corner)
                out.append((NFULL + k, p, 32, wide, image, m % 2, q % 5, dev // 4, dev % 4, base + p * 32))
            narrow = (corner | right) if p < 4 else right
            out.append((NFULL + k, p, 16, narrow, image, m % 2, 4, dev // 4, dev % 4, base + p * 16))
    return out


def group_barrier(extra=()):
    f, c, t = coords()
    sem = pltpu.get_barrier_semaphore()
    count = 0
    for dc in range(4):
        for dt in range(4):
            if dc == 0 and dt == 0:
                continue
            pl.semaphore_signal(sem, inc=1, device_id=(f, (c + dc) % 4, (t + dt) % 4), device_id_type=MESH)
            count += 1
    for dest in extra:
        pl.semaphore_signal(sem, inc=1, device_id=dest, device_id_type=MESH)
        count += 1
    pl.semaphore_wait(sem, count)


def send_or_copy(src, dst, dest, me, send_sem, recv_sem):
    (d_ctx, d_tp), (f, ctx, tp) = dest, me
    here = (d_ctx == ctx) & (d_tp == tp)

    @pl.when(here)
    def _():
        pltpu.make_async_copy(src, dst, recv_sem).start()

    @pl.when(jnp.logical_not(here))
    def _():
        pltpu.make_async_remote_copy(
            src_ref=src, dst_ref=dst, send_sem=send_sem, recv_sem=recv_sem,
            device_id=(f, d_ctx, d_tp), device_id_type=MESH,
        ).start()


def wait_sent(src, dest, me, send_sem):
    (d_ctx, d_tp), (f, ctx, tp) = dest, me
    away = jnp.logical_not((d_ctx == ctx) & (d_tp == tp))

    @pl.when(away)
    def _():
        pltpu.make_async_copy(src, src, send_sem).wait()


def start_pieces(stage, out, a, images, me, ss, rs):
    _, ctx, tp = me
    for n, (i, u, c, d_ctx, d_tp, d_row, slot, p) in enumerate(piece_places(ctx, tp, images)):
        rows = 32 if c < 4 else 16
        src = stage.at[a, i, u, pl.ds(c * 32, rows)]
        dst = out.at[pl.ds(pl.multiple_of(d_row, 16), rows)]
        send_or_copy(src, dst, (d_ctx, d_tp), me, ss.at[a, n], rs.at[a, slot, p])


def finish_piece_sends(stage, a, images, me, ss):
    _, ctx, tp = me
    for n, (i, u, c, d_ctx, d_tp, d_row, slot, p) in enumerate(piece_places(ctx, tp, images)):
        rows = 32 if c < 4 else 16
        wait_sent(stage.at[a, i, u, pl.ds(c * 32, rows)], (d_ctx, d_tp), me, ss.at[a, n])


def wait_pieces(out, a, me, rs):
    _, ctx, tp = me
    for slot, p, rows, exists, *_rest, row in window_places(ctx, tp):
        dst = out.at[pl.ds(row, rows)]
        wait = pltpu.make_async_copy(dst, dst, rs.at[a, slot, p]).wait
        if exists is None:
            wait()
        else:
            pl.when(exists)(wait)


UNITS = 6
BLOCKS = ((192, 384), (192, 384), (192, 384), (192, 384), (384, 768), (768, 384))
Z_UNITS = (4, 5)


def block(ref, w, t, f, part=None):
    rows, cols = BLOCKS[w]
    start, size = part if part is not None else (0, rows)
    if w == 4:
        return ref.at[pl.ds(pl.multiple_of(t * D + f * rows + start, 16), size)]
    return ref.at[
        pl.ds(pl.multiple_of(t * rows + start, 16), size),
        pl.ds(pl.multiple_of(f * cols, 128), cols),
    ]


def remote(src, dst, dest, send_sem, recv_sem):
    return pltpu.make_async_remote_copy(
        src_ref=src, dst_ref=dst, send_sem=send_sem, recv_sem=recv_sem, device_id=dest, device_id_type=MESH
    )


class Gather:
    def __init__(self, shards, wholes, me, ss, rs, ls):
        self.shards, self.wholes = shards, wholes
        self.ss, self.rs, self.ls = ss, rs, ls
        f, c, t = me
        self.me = me
        self.g, self.y, self.s = 1 - f, (t + 2) % 4, t + 1 - 2 * (t % 2)
        self.to_x, self.to_y, self.to_s = (self.g, c, t), (f, c, self.y), (f, c, self.s)
        self.to_z = (f, c + 1 - 2 * (c % 2), t)
        self.parity = c % 2

    def copies(self, w):
        return range(13) if w in Z_UNITS else range(7)

    def part(self, w, theirs=False):
        if w not in Z_UNITS:
            return None
        half = BLOCKS[w][0] // 2
        return ((1 - self.parity if theirs else self.parity) * half, half)

    def own(self, w, part):
        if part is None:
            return self.shards[w]
        return self.shards[w].at[pl.ds(pl.multiple_of(part[0], 16), part[1])]

    def copy(self, w, k):
        f, _, t = self.me
        g, y = self.g, self.y
        whole = self.wholes[w]
        part, other = self.part(w), self.part(w, True)
        if k < 3:
            part = None if k == 2 else part
            src, dst = self.own(w, part), block(whole, w, t, f, part)
            dest = (self.to_x, self.to_y, self.to_s)[k]
        else:
            src = dst = block(whole, w, *(
                (y, f, part), (t, g, part), (y, f, part), (y, g, part),
                (t, g, part), (y, f, part), (y, g, part), (t, g, other), (y, f, other), (y, g, other),
            )[k - 3])
            dest = (self.to_x,) + (self.to_s,) * 3 + (self.to_z,) * 3 + (self.to_s,) * 3
            dest = dest[k - 3]
        return remote(src, dst, dest, self.ss.at[w, k], self.rs.at[w, k])

    def landed(self, w, k):
        f, _, t = self.me
        g, y, s = self.g, self.y, self.s
        sy = (s + 2) % 4
        part, other = self.part(w), self.part(w, True)
        place = (
            (t, g, part), (y, f, part), (s, f), (y, g, part), (s, g, part), (sy, f, part), (sy, g, part),
            (t, g, other), (y, f, other), (y, g, other), (s, g, other), (sy, f, other), (sy, g, other),
        )[k]
        return block(self.wholes[w], w, *place)

    def wait_recv(self, w, k):
        dst = self.landed(w, k)
        pltpu.make_async_copy(dst, dst, self.rs.at[w, k]).wait()

    def start_own(self, w, ks=(0, 1, 2)):
        f, _, t = self.me
        for k in ks:
            self.copy(w, k).start()
        if 2 in ks:
            pltpu.make_async_copy(self.shards[w], block(self.wholes[w], w, t, f), self.ls.at[w]).start()

    def on(self, w, arrived, sends):
        self.wait_recv(w, arrived)
        for k in sends:
            if k in self.copies(w):
                self.copy(w, k).start()

    def forward_x(self, w):
        self.on(w, 0, (7, 4))

    def forward_y(self, w):
        self.on(w, 1, (3, 8, 5))

    def forward_second(self, w):
        self.on(w, 3, (9, 6))

    def forward_z(self, w):
        for k in range(3):
            self.on(w, 7 + k, (10 + k,))

    def arrived(self, w, ks=(2, 4, 5, 6, 10, 11, 12)):
        f, _, t = self.me
        for k in ks:
            if k in self.copies(w):
                self.wait_recv(w, k)
        if 2 in ks:
            pltpu.make_async_copy(self.shards[w], block(self.wholes[w], w, t, f), self.ls.at[w]).wait()

    def sent(self, w):
        for k in self.copies(w):
            self.copy(w, k).wait_send()


def part_facts(k):
    _, ctx, tp = coords()
    q = (3 - ctx) * 8 + tp * 2 + k
    bottom = q < 15
    corner = bottom & (q % 5 == 4)
    right = (q >= 15) & (q < 27)
    return bottom, corner, right


def row_real(slot, rows):
    r = lax.broadcasted_iota(jnp.int32, (rows, 1), 0)
    wide = (r % 16) < WIN
    if slot < NFULL:
        return wide
    bottom, corner, right = part_facts(slot - NFULL)
    limit = jnp.where(corner, 64, jnp.where(right, 112, jnp.where(bottom, PART, 0)))
    narrow = jnp.where(corner | right, 1, 0)
    return (r < limit) & (wide | (narrow > 0))


def key_places(kind, shape):
    r = lax.broadcasted_iota(jnp.int32, shape, 0)
    a, b = r // 16, r % 16
    if kind == 0:
        return a, b
    _, corner, right = part_facts(kind - 1)
    corner, right = jnp.where(corner, 1, 0), jnp.where(right, 1, 0)
    a_right = jnp.where(r < 112, r // 8, (r - 112) // 8)
    b_right = jnp.where(r < 112, r % 8, 8 + (r - 112) % 8)
    a_corner = jnp.where(r < 64, r // 8, jnp.where(r < 128, (r - 64) // 8, 8 + (r - 128) // 16))
    b_corner = jnp.where(r < 64, r % 8, jnp.where(r < 128, 8 + (r - 64) % 8, (r - 128) % 16))
    a = jnp.where(corner > 0, a_corner, jnp.where(right > 0, a_right, a))
    b = jnp.where(corner > 0, b_corner, jnp.where(right > 0, b_right, b))
    return a, b


def build_keys(e_ref):
    shape = (FULL, 128)
    col = lax.broadcasted_iota(jnp.int32, shape, 1)
    j = col % 16
    for kind in range(1 + NPART):
        a, b = key_places(kind, shape)
        ok = b < WIN
        along_a = jnp.where(ok & (j == a) & (j < WIN), 1.0, 0.0)
        along_a = jnp.where(jnp.logical_not(ok) & (col % SEG == 15), MASKED, along_a)
        along_b = jnp.where(ok & (j == b) & (j < WIN), 1.0, 0.0)
        for head in range(3):
            mine = col // SEG == head
            e_ref[kind, head, :, pl.ds(0, 128)] = jnp.where(mine, along_a, 0.0).astype(BF)
            e_ref[kind, head, :, pl.ds(128, 128)] = jnp.where(mine, along_b, 0.0).astype(BF)


def build_relative(rel_refs, out_ref):
    out_ref[...] = jnp.zeros(out_ref.shape, BF)
    i = lax.broadcasted_iota(jnp.int32, (RELS, 128), 0)
    lane = lax.broadcasted_iota(jnp.int32, (RELS, 128), 1)
    turn = (lane % SEG == 26 - i).astype(BF)
    lane64 = lax.broadcasted_iota(jnp.int32, (HEAD_DIM, 128), 1) // SEG
    for axis in range(2):
        rev = tn(rel_refs[axis][...], turn)
        for h in range(HALF_HEADS):
            out_ref[pl.ds(h * HEAD_DIM, HEAD_DIM), pl.ds((h // 3) * 256 + axis * 128, 128)] = (
                jnp.where(lane64 == h % 3, rev, 0.0).astype(BF)
            )


def slots():
    return [(k, k * FULL, FULL) for k in range(NFULL)] + [
        (NFULL + k, PBASE + k * PART, PART) for k in range(NPART)
    ]


def half_cols(start, half):
    return pl.ds(pl.multiple_of(start + half * HALF, 128), HALF)


def norm(rows):
    centered = rows - jnp.mean(rows, axis=-1, keepdims=True)
    r = lax.rsqrt(jnp.mean(centered * centered, axis=-1, keepdims=True) + EPSILON)
    return centered * r, r


def forward_kernel(images, direct, *refs):
    it = iter(refs)

    def take(n):
        return [next(it) for _ in range(n)]

    x_ref, c_ref = take(2)
    weights = take(4 if direct else 2)
    g1_ref, b1_ref, qkv_b, g2_ref, b2_ref, pb_ref, db_ref, relh_ref, relw_ref = take(9)
    x_o, c_o, n1_o, qkv_o, att_o, p_o, mid_o, xhat_o, n2_o, r2_o = take(10)
    if direct:
        wq_o, wp_o, wu, wd = take(4)
    e_o, rel_o = take(2)
    stage, xw, cw, n1, qkv, att, p_buf, mid, xhat2, n2, r2 = take(11)
    wq, wp, e, rel_blk, x_scr, bias_v, vec, ss, rs = take(9)
    if direct:
        gss, grs, gls = take(3)
    os, = take(1)
    me = coords()
    f, ctx, tp = me
    pack = pack_matrix()

    def stage_tokens(a, src):
        for i in range(images):
            for u in range(2):
                stage[a, i, u] = jnp.dot(
                    pack, src[i, pl.ds(u * 128, 128)], preferred_element_type=F32
                ).astype(BF)

    out_copies = []

    def write(src, dst):
        cp = pltpu.make_async_copy(src, dst, os.at[len(out_copies)])
        cp.start()
        out_copies.append(cp)

    stage_tokens(0, x_ref)
    group_barrier(((1 - f, ctx, tp),) if direct else ())
    start_pieces(stage, xw, 0, images, me, ss, rs)
    if direct:
        wq_s, wp_s, wu_s, wd_s = weights
        shards = (wq_s.at[0], wq_s.at[1], wq_s.at[2], wp_s, wu_s, wd_s)
        gather = Gather(shards, (wq.at[0], wq.at[1], wq.at[2], wp, wu, wd), me, gss, grs, gls)
        for w in range(3):
            gather.start_own(w, (0, 2))
    else:
        load = (pltpu.make_async_copy(weights[0], wq, os.at[18]), pltpu.make_async_copy(weights[1], wp, os.at[19]))
        for cp in load:
            cp.start()
    build_keys(e)
    build_relative((relh_ref, relw_ref), rel_blk)
    write(e, e_o)
    write(rel_blk, rel_o)
    rows = [g1_ref[...], b1_ref[...], qkv_b[0, :], None, qkv_b[1, :], g2_ref[...], b2_ref[...], pb_ref[...], db_ref[...]]
    for n, row in enumerate(rows):
        vec[n:n + 1, :] = jnp.zeros((1, D), F32) if row is None else row.astype(F32).reshape(1, D)
    bias_v[...] = vec[4:5, :]
    stage_tokens(1, c_ref)
    if direct:
        for w in range(3):
            gather.on(w, 0, (4,))
        for w in (4, 5, 3):
            gather.start_own(w, (0, 2))
    wait_pieces(xw, 0, me, rs)
    if direct:
        for w in range(3):
            gather.start_own(w, (1,))
    for slot, base, rows in slots():
        here = pl.ds(base, rows)
        real = row_real(slot, rows)
        x = jnp.where(real, xw[here].astype(F32), 0.0)
        xw[here] = x.astype(BF)
        xhat, _ = norm(x)
        n1[here] = jnp.where(real, xhat * vec[0:1, :] + vec[1:2, :], 0.0).astype(BF)
    write(xw, x_o)
    write(n1, n1_o)
    if direct:
        for w in range(3):
            gather.arrived(w, (2, 4))
    else:
        for cp in load:
            cp.wait()
        start_pieces(stage, cw, 1, images, me, ss, rs)

    for turn in range(2):
        half = tp // 2 if turn == 0 else 1 - tp // 2

        @pl.loop(0, 3)
        def _(n, half=half):
            out = nt(n1[...], wq[n, half_cols(0, half), :]) + vec[pl.ds(2 + n, 1), half_cols(0, half)]
            qkv[:, half_cols(n * D, half)] = out.astype(BF)

        @pl.loop(0, NFULL)
        def _(n, half=half, turn=turn):
            attention_half(qkv, rel_blk, bias_v, e.at[0], att, p_buf, pl.multiple_of(n * FULL, 16), FULL, None, x_scr, half)
            if not direct:
                return
            if turn == 0:
                @pl.when(n == 0)
                def _():
                    for w in range(3):
                        gather.on(w, 1, (3, 5))
                    for w in (3, 4, 5):
                        gather.start_own(w, (1,))
                    for w in (4, 5, 3):
                        gather.forward_x(w)

                @pl.when(n == 2)
                def _():
                    pass
            else:
                @pl.when(n == 0)
                def _():
                    gather.forward_y(3)
                    start_pieces(stage, cw, 1, images, me, ss, rs)

                @pl.when(n == 1)
                def _():
                    gather.forward_y(5)

                @pl.when(n == 2)
                def _():
                    gather.forward_second(3)

        @pl.loop(0, NPART)
        def _(n, half=half):
            attention_half(qkv, rel_blk, bias_v, e.at[1 + n], att, p_buf,
                           pl.multiple_of(PBASE + n * PART, 16), PART, narrow_flag(n), x_scr, half)

        if direct:
            if turn == 0:
                for w in range(3):
                    gather.on(w, 3, (6,))
                gather.forward_y(4)
                for w in range(3):
                    gather.arrived(w, (5, 6))
                write(wq, wq_o)
            else:
                gather.forward_second(4)

    write(qkv, qkv_o)
    write(att, att_o)
    write(p_buf, p_o)
    if direct:
        gather.arrived(3)
        write(wp, wp_o)

    @pl.loop(0, ROWS // CHUNK)
    def _(n):
        here = pl.ds(pl.multiple_of(n * CHUNK, 16), CHUNK)
        middle = xw[here].astype(F32) + jnp.dot(att[here], wp[...], preferred_element_type=F32) + vec[7:8, :]
        xhat, r = norm(middle)
        r2[here] = r
        xhat2[here] = xhat.astype(BF)
        n2[here] = (xhat * vec[5:6, :] + vec[6:7, :]).astype(BF)
        mid[here] = middle + vec[8:9, :]

    for src, dst in ((n2, n2_o), (mid, mid_o), (xhat2, xhat_o), (r2, r2_o)):
        write(src, dst)
    if direct:
        gather.forward_second(5)
        gather.forward_z(4)
        gather.forward_z(5)
    wait_pieces(cw, 1, me, rs)
    for slot, base, rows in slots():
        here = pl.ds(base, rows)
        cw[here] = jnp.where(row_real(slot, rows), cw[here].astype(F32), 0.0).astype(BF)
    write(cw, c_o)
    if direct:
        for w in (4, 5):
            gather.arrived(w)
        for w in range(UNITS):
            gather.sent(w)
    for a in range(2):
        finish_piece_sends(stage, a, images, me, ss)
    for cp in out_copies:
        cp.wait()


def forward(x3, c3, shards, whole, small):
    images = x3.shape[0]
    any_spec = pl.BlockSpec(memory_space=pl.ANY)
    vmem = pl.BlockSpec(memory_space=pltpu.VMEM)
    direct = whole is None
    dma = pltpu.SemaphoreType.DMA
    shape = jax.ShapeDtypeStruct
    tokens = shape((ROWS, D), BF)
    keys = (1 + NPART, 3, FULL, 256)
    outs = [tokens, tokens, tokens, shape((ROWS, 3 * D), BF), tokens, shape((ROWS, HEADS * 256), BF)]
    outs += [shape((ROWS, D), F32), tokens, tokens, shape((ROWS, 1), F32)]
    if direct:
        outs += [shape(s, BF) for s in ((3, D, D), (D, D), (4 * D, D), (4 * D, D))]
    outs += [shape(keys, BF), shape((HALF, 512), BF)]
    v = pltpu.VMEM
    scratch = [v((2, images, 2, PIECE, D), BF)] + [v((ROWS, D), BF)] * 3
    scratch += [v((ROWS, 3 * D), BF), v((ROWS, D), BF), v((ROWS, HEADS * 256), BF)]
    scratch += [v((ROWS, D), F32), v((ROWS, D), BF), v((ROWS, D), BF), v((ROWS, 1), F32)]
    scratch += [v((3, D, D), BF), v((D, D), BF), v(keys, BF), v((HALF, 512), BF), v((FULL, 512), BF)]
    scratch += [v((1, D), F32), v((16, D), F32)]
    scratch += [dma((2, images * 10)), dma((2, NFULL + NPART, PAIRS))]
    if direct:
        scratch += [dma((UNITS, 13)), dma((UNITS, 13)), dma((UNITS,))]
    scratch += [dma((20,))]
    weights = list(shards) if direct else list(whole)
    return pl.pallas_call(
        functools.partial(forward_kernel, images, direct),
        out_shape=outs,
        in_specs=[vmem, vmem] + [any_spec] * len(weights) + [vmem] * len(small),
        out_specs=[any_spec] * len(outs),
        scratch_shapes=scratch,
        compiler_params=pltpu.CompilerParams(
            collective_id=0, has_side_effects=True, vmem_limit_bytes=VMEM_LIMIT
        ),
        name="forward",
    )(x3, c3, *weights, *small)


def barrel(x, shift, left):
    lanes = x.shape[-1]
    for bit in (1, 2, 4, 8):
        moved = pltpu.roll(x, lanes - bit if left else bit, 1)
        x = jnp.where((shift // bit) % 2 == 1, moved, x)
    return x


def row_places(rows, narrow):
    r = lax.broadcasted_iota(jnp.int32, (rows, 128), 0)
    if narrow is None:
        return r // 16, r % 16
    is_narrow = narrow > 0
    return jnp.where(is_narrow, r // 8, r // 16), jnp.where(is_narrow, r % 8, r % 16)


def half_mask(hh):
    lane = lax.broadcasted_iota(jnp.int32, (1, 128), 1)
    return ((lane // 64) == hh).astype(BF)


def nt(a, b):
    return lax.dot_general(a, b, (((1,), (1,)), ((), ())), preferred_element_type=F32)


def tn(a, b):
    return lax.dot_general(a, b, (((0,), (0,)), ((), ())), preferred_element_type=F32)


def key_rows(ref, base, rows, col, fill):
    part = ref[pl.ds(base, rows), pl.ds(pl.multiple_of(col, 128), 128)]
    if rows == FULL:
        return part
    return jnp.concatenate([part, jnp.broadcast_to(fill, (FULL - rows, 128)).astype(BF)], axis=0)


def attention_half(qkv, rel_blk, bias_v, e_at, o_ref, p_ref, base, rows, narrow, x_scr, half):
    a_row, b_row = row_places(rows, narrow)
    here = pl.ds(base, rows)
    q_all = qkv[here, half_cols(0, half)]
    lane = lax.broadcasted_iota(jnp.int32, (rows, 128), 1) % SEG
    raw = jnp.dot(q_all, rel_blk[...], preferred_element_type=F32)
    for g in range(2):
        for axis, pos in ((0, a_row), (1, b_row)):
            at = g * 256 + axis * 128
            v = barrel(raw[:, at:at + 128], jnp.maximum(13 - pos, 0), True)
            hi = v.astype(BF).astype(F32)
            lo = pltpu.roll(v - hi, 16, 1)
            mix = jnp.where(lane < WIN, hi, jnp.where(lane >= 16, lo, 0.0))
            if axis == 0:
                mix = jnp.where(lane == 15, 1.0, mix)
            x_scr[pl.ds(0, rows), pl.ds(at, 128)] = mix.astype(BF)
    for hp in range(3):
        cols = pl.ds(pl.multiple_of(half * HALF + hp * 128, 128), 128)
        q = q_all[:, hp * 128:(hp + 1) * 128]
        k = key_rows(qkv, base, rows, D + half * HALF + hp * 128, jnp.zeros((1, 128), BF))
        v = key_rows(qkv, base, rows, 2 * D + half * HALF + hp * 128, bias_v[:, cols])
        out = jnp.zeros((rows, 128), F32)
        for hh in range(2):
            h = hp * 2 + hh
            x = x_scr[pl.ds(0, rows), pl.ds((h // 3) * 256, 256)]
            s = nt(q, k * (half_mask(hh) * 0.125)) + nt(x, e_at[h % 3])
            p = jnp.exp(s - jnp.max(s, axis=-1, keepdims=True))
            p = (p * (1.0 / jnp.sum(p, axis=-1, keepdims=True))).astype(BF)
            p_ref[here, pl.ds(pl.multiple_of((half * HALF_HEADS + h) * 256, 128), FULL)] = p
            out = out + jnp.dot(p, v * half_mask(hh), preferred_element_type=F32)
        o_ref[here, cols] = out.astype(BF)


def narrow_flag(k):
    _, ctx, tp = coords()
    q = (3 - ctx) * 8 + tp * 2 + k
    is_narrow = ((q < 15) & (q % 5 == 4)) | ((q >= 15) & (q < 27))
    return jnp.where(is_narrow, 1, 0)


def attention_back_half(qkv, do_ref, rel_blk, bias_v, e_at, p_ref, d_scr, acc_scr, pad_acc, rel_acc, base, rows,
                        narrow, half):
    a_row, b_row = row_places(rows, narrow)
    here = pl.ds(base, rows)
    dx = [jnp.zeros((rows, 256), F32)] * 2
    for hp in range(3):
        cols = pl.ds(pl.multiple_of(half * HALF + hp * 128, 128), 128)
        k_at, v_at = D + half * HALF + hp * 128, 2 * D + half * HALF + hp * 128
        q = qkv[here, cols]
        k = key_rows(qkv, base, rows, k_at, jnp.zeros((1, 128), BF))
        v = key_rows(qkv, base, rows, v_at, bias_v[:, cols])
        do = do_ref[here, cols]
        dq = jnp.zeros((rows, 128), F32)
        dk = jnp.zeros((FULL, 128), F32)
        dv = jnp.zeros((FULL, 128), F32)
        for hh in range(2):
            h = hp * 2 + hh
            mask = half_mask(hh)
            do_m = do * mask
            dp = nt(do_m, v)
            p_low = p_ref[pl.ds(0, rows), pl.ds(h * 256, FULL)]
            t = p_low.astype(F32)
            tp = t * dp
            ds = (tp - t * jnp.sum(tp, axis=-1, keepdims=True)).astype(BF)
            dq = dq + jnp.dot(ds, k * (mask * 0.125), preferred_element_type=F32)
            dx[h // 3] = dx[h // 3] + jnp.dot(ds, e_at[h % 3], preferred_element_type=F32)
            dk = dk + tn(ds, q * (mask * 0.125))
            dv = dv + tn(p_low, do_m)
        acc_scr[pl.ds(0, rows), pl.ds(hp * 128, 128)] = dq
        qkv[here, pl.ds(pl.multiple_of(k_at, 128), 128)] = dk[:rows].astype(BF)
        qkv[here, pl.ds(pl.multiple_of(v_at, 128), 128)] = dv[:rows].astype(BF)
        if rows < FULL:
            pad_acc[:, cols] += jnp.sum(dv[rows:], axis=0, keepdims=True)
    lane = lax.broadcasted_iota(jnp.int32, (rows, 128), 1) % SEG
    for g in range(2):
        for axis, pos in ((0, a_row), (1, b_row)):
            v = jnp.where(lane < WIN, dx[g][:, axis * 128:(axis + 1) * 128], 0.0)
            v = barrel(v, jnp.maximum(13 - pos, 0), False)
            d_scr[pl.ds(0, rows), pl.ds(g * 256 + axis * 128, 128)] = v.astype(BF)
    d = d_scr[pl.ds(0, rows), :]
    rel_acc[pl.ds(0, 512), pl.ds(0, HALF)] += tn(d, qkv[here, half_cols(0, half)])
    qkv[here, half_cols(0, half)] = (acc_scr[pl.ds(0, rows), :] + nt(d, rel_blk[...])).astype(BF)


TILE = (D, D, 192, 192, 192, 192)
HALVES = ((384, D), (D, 384), (192, 384), (192, 384), (192, 384), (192, 384))
Z_PIECES = (2, 2, 1, 1, 1, 1)
CHUNK = ROWS // 2
SUMS = 16
FEW = 12 * 6 + 2 * SEG


def add_rows(dst, src):
    rows = dst.shape[0]
    size = 64

    @pl.loop(0, rows // size)
    def _(n):
        here = pl.ds(pl.multiple_of(n * size, 16), size)
        dst[here] = (dst[here].astype(F32) + src[here].astype(F32)).astype(BF)


class Reduce:
    def __init__(self, grads, me, outs, r1, rx, ry, rz, s1, v1, s2, v2, s3, v3, sz, vz, so):
        self.grads, self.outs = grads, outs
        self.r1u, self.r1d, self.r1p = r1
        self.rx, self.ry, self.rz = rx, ry, rz
        self.s1, self.v1, self.s2, self.v2, self.s3, self.v3 = s1, v1, s2, v2, s3, v3
        self.sz, self.vz, self.so = sz, vz, so
        f, ctx, tp = me
        self.f, self.g = f, 1 - f
        self.c, self.own = tp % 2, tp // 2
        self.to_s = (f, ctx, tp + 1 - 2 * self.c)
        self.to_x = (1 - f, ctx, tp)
        self.to_y = (f, ctx, (tp + 2) % 4)
        self.outer = (ctx == 0) | (ctx == 3)
        self.inner = jnp.logical_not(self.outer)
        self.to_mid = (f, 3 - ctx, tp)
        self.to_in = (f, jnp.where(ctx == 0, 1, 2), tp)
        self.to_out = (f, jnp.where(ctx == 1, 0, 3), tp)

    def tile(self, w, t):
        return self.grads[w].at[pl.ds(pl.multiple_of(t * TILE[w], 16), TILE[w])]

    def half(self, w, t, f):
        if w == 0:
            return self.grads[w].at[pl.ds(pl.multiple_of(t * D + f * 384, 16), 384)]
        return self.grads[w].at[
            pl.ds(pl.multiple_of(t * TILE[w], 16), TILE[w]), pl.ds(pl.multiple_of(f * 384, 128), 384)
        ]

    def landing(self, w, j):
        if w < 2:
            return (self.r1u, self.r1d)[w].at[j]
        if w == 2:
            return self.r1p.at[j]
        return self.r1d.at[(w - 3) // 2, pl.ds(pl.multiple_of(((w - 3) % 2) * 384 + j * 192, 16), 192)]

    def core_copy(self, w, j):
        src = self.tile(w, 1 - self.c + 2 * j)
        return remote(src, self.landing(w, j), self.to_s, self.s1.at[w, j], self.v1.at[w, j])

    def core_send(self, w, j):
        self.core_copy(w, j).start()

    def x_copy(self, w, j):
        if w == 0:
            src = self.half(0, self.c + 2 * self.own, self.g)
            return remote(src, self.rx[0].at[0], self.to_x, self.s2.at[0, 0], self.v2.at[0, 0])
        src = self.half(w, self.c + 2 * j, self.g)
        return remote(src, self.rx[w].at[j], self.to_x, self.s2.at[w, j], self.v2.at[w, j])

    def core_add(self, w, j):
        self.core_copy(w, j).wait_recv()
        add_rows(self.tile(w, self.c + 2 * j), self.landing(w, j))
        if w == 0:
            @pl.when(self.own != j)
            def _():
                self.y_copy(0).start()
        else:
            self.x_copy(w, j).start()

    def y_copy(self, w):
        if w == 0:
            src = self.tile(0, self.c + 2 * (1 - self.own))
            return remote(src, self.ry[0], self.to_y, self.s3.at[0], self.v3.at[0])
        src = self.half(w, self.c + 2 * (1 - self.own), self.f)
        return remote(src, self.ry[w], self.to_y, self.s3.at[w], self.v3.at[w])

    def x_add(self, w, j):
        self.x_copy(w, j).wait_recv()
        add_rows(self.half(w, self.c + 2 * j, self.f), self.rx[w].at[j])

        @pl.when(self.own != j)
        def _():
            self.y_copy(w).start()

    def up_y_add(self):
        self.y_copy(0).wait_recv()
        add_rows(self.tile(0, self.c + 2 * self.own), self.ry[0])
        self.x_copy(0, 0).start()

    def up_x_add(self):
        self.x_copy(0, 0).wait_recv()
        add_rows(self.mine(0), self.rx[0].at[0])
        for h in range(Z_PIECES[0]):
            self.z_in(0, h)

    def mine(self, w):
        return self.half(w, self.c + 2 * self.own, self.f)

    def y_add(self, w):
        self.y_copy(w).wait_recv()
        add_rows(self.mine(w), self.ry[w])

        for h in range(Z_PIECES[w]):
            self.z_in(w, h)

    def z_view(self, ref, w, h):
        size = HALVES[w][0] // Z_PIECES[w]
        return ref.at[pl.ds(h * size, size)]

    def z_mine(self, w, h):
        t, size = self.c + 2 * self.own, HALVES[w][0] // Z_PIECES[w]
        if w == 0:
            return self.grads[w].at[pl.ds(pl.multiple_of(t * D + self.f * 384 + h * size, 16), size)]
        return self.grads[w].at[
            pl.ds(pl.multiple_of(t * TILE[w] + h * size, 16), size), pl.ds(pl.multiple_of(self.f * 384, 128), 384)
        ]

    def z_slot(self, w, slot, h):
        return self.z_view(self.rz[w].at[slot], w, h)

    def z_in(self, w, h):
        @pl.when(self.outer)
        def _():
            remote(
                self.z_mine(w, h), self.z_slot(w, 0, h), self.to_in, self.sz.at[w, h, 0], self.vz.at[w, h, 0]
            ).start()

    def z_wait(self, w, h, sem):
        view = self.z_slot(w, 0, h)
        pltpu.make_async_copy(view, view, sem).wait()

    def z_mid(self, w, h):
        @pl.when(self.inner)
        def _():
            self.z_wait(w, h, self.vz.at[w, h, 0])
            mine = self.z_mine(w, h)
            add_rows(mine, self.z_slot(w, 0, h))
            remote(mine, self.z_slot(w, 1, h), self.to_mid, self.sz.at[w, h, 0], self.vz.at[w, h, 1]).start()

    def z_out(self, w, h):
        @pl.when(self.inner)
        def _():
            self.z_wait(w, h, self.vz.at[w, h, 1])
            total = self.z_slot(w, 1, h)
            add_rows(total, self.z_mine(w, h))
            remote(total, self.z_slot(w, 0, h), self.to_out, self.sz.at[w, h, 1], self.vz.at[w, h, 2]).start()
            pltpu.make_async_copy(total, self.z_view(self.outs[w], w, h), self.so.at[w, h]).start()

    def z_end(self, w, h):
        @pl.when(self.outer)
        def _():
            self.z_wait(w, h, self.vz.at[w, h, 2])
            pltpu.make_async_copy(self.z_slot(w, 0, h), self.z_view(self.outs[w], w, h), self.so.at[w, h]).start()

    def sent(self, w):
        for j in range(2):
            self.core_copy(w, j).wait_send()
            if w or j == 0:
                self.x_copy(w, j).wait_send()
        self.y_copy(w).wait_send()
        for h in range(Z_PIECES[w]):
            self.z_wait(w, h, self.sz.at[w, h, 0])

            @pl.when(self.inner)
            def _(h=h):
                self.z_wait(w, h, self.sz.at[w, h, 1])

            self.z_wait(w, h, self.so.at[w, h])


def backward_kernel(images, direct, *refs):
    it = iter(refs)

    def take(n):
        return [next(it) for _ in range(n)]

    x_h, c_h, n1_h, qkv_h, att_h, p_h, mid_h, xhat_h, n2_h, r2_h, wq_h, wp_h, wu_h, wd_h, e_h, rel_h = take(16)
    g1_ref, g2_ref, qkv_b, up_ref = take(4)
    staged, few_out = take(2)
    outs = take(4)
    outs = outs[:3] + [outs[3].at[pl.ds(k * 192, 192)] if direct else outs[3].at[k] for k in range(3)]
    cot, att, n2, xhat2, hid, dg = take(6)
    acc, dn2 = take(2)
    wu, wd, wp, wq, dwq, qkv, p_buf, e, rel_blk, d_scr, acc_scr = take(11)
    bias_v, pad_acc, sums, r2, real, vec = take(6)
    ls, ss, rs = take(3)
    if direct:
        r1 = take(3)
        rx, ry, rz = take(6), take(6), take(6)
        few_in, = take(1)
        sems = take(9)
        few_s, few_r = take(2)
    me = coords()
    f, ctx, tp = me
    c, own = tp % 2, tp // 2
    pair_at = (1 - own, own)
    tile_at = [2 * pair_at[n // 2] + n % 2 for n in range(4)]
    loads = {}

    def load(name, src, dst):
        loads[name] = pltpu.make_async_copy(src, dst, ls.at[len(loads)])
        loads[name].start()

    def rows_of(t):
        return pl.ds(pl.multiple_of(t * D, 16), D)

    load("n2", n2_h, n2)
    for n, t in enumerate(tile_at):
        load(("wu", n), wu_h.at[rows_of(t)], wu.at[rows_of(t)])
        if n == 0:
            load("cot", c_h, cot)
        load(("wd", n), wd_h.at[rows_of(t)], wd.at[rows_of(t)])
        if n == 0:
            load("acc", mid_h, acc)
    load("xhat", xhat_h, xhat2)
    load("r2", r2_h, r2)
    load("wp", wp_h, wp)
    load("att", att_h, att)
    load("qkv", qkv_h, qkv)
    load("e", e_h, e)
    load("rel", rel_h, rel_blk)
    load("wq", wq_h, wq)
    steps = [(turn, slot) for turn in range(2) for slot in range(NFULL + NPART)]

    def p_copy(n):
        turn, slot = steps[n]
        base, rows = (slot * FULL, FULL) if slot < NFULL else (PBASE + (slot - NFULL) * PART, PART)
        cols = pl.ds(pl.multiple_of(pair_at[turn] * HALF_HEADS * 256, 128), HALF_HEADS * 256)
        return pltpu.make_async_copy(
            p_h.at[pl.ds(base, rows), cols], p_buf.at[n % 2, pl.ds(0, rows)], ls.at[20 + n % 2]
        )

    p_copy(0).start()
    p_copy(1).start()
    group_barrier(((1 - f, ctx, tp),) if direct else ())
    grads = (wu, wd, wp, dwq.at[0], dwq.at[1], dwq.at[2])
    red = Reduce(grads, me, outs, r1, rx, ry, rz, *sems) if direct else None
    sums[...] = jnp.zeros_like(sums)
    pad_acc[...] = jnp.zeros_like(pad_acc)
    vec[0:1, :] = g1_ref[...].astype(F32).reshape(1, D)
    vec[5:6, :] = g2_ref[...].astype(F32).reshape(1, D)
    bias_v[...] = qkv_b[1, :].astype(F32).reshape(1, D)
    up_all = up_ref[...].astype(F32)
    for k in range(4):
        vec[9 + k:10 + k, :] = up_all[k * D:(k + 1) * D].reshape(1, D)
    for slot, base, rows in slots():
        real[pl.ds(base, rows)] = jnp.where(row_real(slot, rows), 1.0, 0.0)

    def row_chunks(body):
        @pl.loop(0, ROWS // CHUNK)
        def _(n):
            body(pl.ds(pl.multiple_of(n * CHUNK, 16), CHUNK))

    for name in ("n2", "cot"):
        loads[name].wait()
    for n in range(4):
        loads["wu", n].wait()
        loads["wd", n].wait()
        pair = pair_at[n // 2]
        t = tile_at[n]
        base = pl.multiple_of(t * D, 16)

        for j in range(3):
            units = pl.ds(j * 256, 256)
            there = pl.ds(pl.multiple_of(base + j * 256, 16), 256)
            for r in range(ROWS // CHUNK):
                here = pl.ds(r * CHUNK, CHUNK)
                d_hidden = nt(cot[here, :], wd[there, :])
                gate = jnp.dot(n2[here, :], wu[pl.ds(base, D), units], preferred_element_type=F32)
                hidden, slope = gelu_both(gate + vec[pl.ds(9 + t, 1), units])
                hid[here, units] = hidden.astype(BF)
                d_gate = (d_hidden * slope).astype(BF)
                dg[here, units] = d_gate
                sums[pl.ds(8 + t, 1), units] += jnp.sum(d_gate.astype(F32), axis=0, keepdims=True)

        if direct and n:
            @pl.when(c == (n - 1) % 2)
            def _(n=n):
                red.core_add(1, pair_at[(n - 1) // 2])
                red.core_add(0, pair_at[(n - 1) // 2])

        tile = pl.ds(base, D)

        if n == 0:
            loads["acc"].wait()

        for r in range(ROWS // CHUNK):
            here = pl.ds(r * CHUNK, CHUNK)
            acc[here] += jnp.dot(hid[here], wd[tile, :], preferred_element_type=F32)
            more = nt(dg[here], wu[tile, :])
            dn2[here] = dn2[here] + more if n else more
        for j in range(3):
            part = pl.ds(j * 256, 256)
            there = pl.ds(pl.multiple_of(base + j * 256, 16), 256)
            wd[there, :] = tn(hid[:, part], cot[...]).astype(BF)
            wu[there, :] = tn(n2[:, part], dg[...]).astype(BF)

        if direct:
            @pl.when(c != n % 2)
            def _(pair=pair):
                red.core_send(1, pair)
                red.core_send(0, pair)

    for name in ("xhat", "r2", "wp", "att"):
        loads[name].wait()
    load_n1 = pltpu.make_async_copy(n1_h, n2, ls.at[22])
    load_n1.start()

    def back_two(here):
        n = dn2[here]
        xhat = xhat2[here].astype(F32)
        c_rows = cot[here].astype(F32)
        m = n * vec[5:6, :]
        sums[5:6, :] += jnp.sum(n * xhat, axis=0, keepdims=True)
        sums[6:7, :] += jnp.sum(n, axis=0, keepdims=True)
        sums[7:8, :] += jnp.sum(c_rows, axis=0, keepdims=True)
        mean = jnp.mean(m, axis=-1, keepdims=True)
        mean_x = jnp.mean(m * xhat, axis=-1, keepdims=True)
        d_mid = c_rows + r2[here] * (m - mean - xhat * mean_x)
        dn2[here] = d_mid
        branch = d_mid.astype(BF)
        xhat2[here] = branch
        sums[4:5, :] += jnp.sum(branch.astype(F32), axis=0, keepdims=True)
        dg[here] = acc[here].astype(BF)
        hid[here] = nt(branch, wp[...]).astype(BF)

    for n in range(ROWS // CHUNK):
        back_two(pl.ds(n * CHUNK, CHUNK))
        if direct and n == 0:
            @pl.when(c == 1)
            def _():
                red.core_add(1, own)
                red.core_add(0, own)

            red.x_add(1, pair_at[0])
            red.up_y_add()
    places = window_places(ctx, tp)

    def tokens_out(a, src_ref, which=range(NFULL + NPART)):
        for n, (slot, p, rows, exists, image, u, col, d_ctx, d_tp, row) in enumerate(places):
            if slot not in which:
                continue

            def go(n=n, rows=rows, image=image, u=u, col=col, d_ctx=d_ctx, d_tp=d_tp, row=row):
                src = src_ref.at[pl.ds(row, rows)]
                dst = staged.at[a, image, u, pl.ds(pl.multiple_of(col * 32, 16), rows)]
                send_or_copy(src, dst, (d_ctx, d_tp), me, ss.at[a, n], rs.at[a, image, u, col])
            if exists is None:
                go()
            else:
                pl.when(exists)(go)

    def tokens_done(a, src_ref):
        for i in range(images):
            for u in range(2):
                for col in range(5):
                    dst = staged.at[a, i, u, pl.ds(col * 32, 32 if col < 4 else 16)]
                    pltpu.make_async_copy(dst, dst, rs.at[a, i, u, col]).wait()
        for n, (slot, p, rows, exists, image, u, col, d_ctx, d_tp, row) in enumerate(places):
            def done(n=n, rows=rows, d_ctx=d_ctx, d_tp=d_tp, row=row):
                wait_sent(src_ref.at[pl.ds(row, rows)], (d_ctx, d_tp), me, ss.at[a, n])
            if exists is None:
                done()
            else:
                pl.when(exists)(done)

    @pl.loop(0, 3)
    def _(j):
        part = pl.ds(pl.multiple_of(j * 256, 128), 256)
        wp[pl.ds(pl.multiple_of(j * 256, 16), 256), :] = tn(att[:, part], xhat2[...]).astype(BF)

    if direct:
        red.core_send(2, 0)
        red.core_send(2, 1)

    load_x = pltpu.make_async_copy(x_h, xhat2, ls.at[23])
    load_x.start()
    for name in ("qkv", "e", "rel"):
        loads[name].wait()
    load_n1.wait()
    acc[pl.ds(0, 512), pl.ds(0, HALF)] = jnp.zeros((512, HALF), F32)
    for n, (turn, slot) in enumerate(steps):
        pair = pair_at[turn]
        p_copy(n).wait()
        base, rows = (slot * FULL, FULL) if slot < NFULL else (PBASE + (slot - NFULL) * PART, PART)
        kind = 0 if slot < NFULL else 1 + slot - NFULL
        narrow = None if slot < NFULL else narrow_flag(slot - NFULL)
        attention_back_half(qkv, hid, rel_blk, bias_v, e.at[kind], p_buf.at[n % 2], d_scr, acc_scr,
                            pad_acc, acc, base, rows, narrow, pair)
        if n + 2 < len(steps):
            p_copy(n + 2).start()
        if slot == NFULL + NPART - 1:
            for w in range(3):
                d_cols = half_cols(w * D, pair)
                dwq[w, half_cols(0, pair), :] = tn(qkv[:, d_cols], n2[...]).astype(BF)
                if direct:
                    red.core_send(3 + w, pair)
        if n == 4:
            tokens_out(0, dg)
        if not direct:
            continue
        if n == 0:
            red.core_add(2, 0)
            red.core_add(2, 1)
        elif n == 2:
            red.x_add(1, own)
        elif n == 3:
            red.y_add(1)
        elif n == 4:
            red.up_x_add()
        elif n == 5:
            for w in (3, 4, 5):
                red.core_add(w, pair_at[0])
        elif n == 7:
            red.z_mid(1, 0)
        elif n == 8:
            red.z_mid(1, 1)
            red.x_add(2, 0)
            red.x_add(2, 1)
        elif n == 9:
            for w in (3, 4, 5):
                red.core_add(w, own)
            red.z_out(1, 0)

    load_x.wait()
    loads["wq"].wait()

    def back_one(here):
        d_qkv = qkv[here, :]
        n = jnp.zeros((CHUNK, D), F32)
        for w in range(3):
            n = n + jnp.dot(d_qkv[:, w * D:(w + 1) * D], wq[w], preferred_element_type=F32)
        sums[2:3, :] += jnp.sum(d_qkv[:, :D].astype(F32), axis=0, keepdims=True)
        sums[3:4, :] += jnp.sum(d_qkv[:, 2 * D:].astype(F32), axis=0, keepdims=True)
        n = n * real[here]
        rows = xhat2[here].astype(F32)
        centered = rows - jnp.mean(rows, axis=-1, keepdims=True)
        r = lax.rsqrt(jnp.mean(centered * centered, axis=-1, keepdims=True) + EPSILON)
        xhat = centered * r
        sums[0:1, :] += jnp.sum(n * xhat, axis=0, keepdims=True)
        sums[1:2, :] += jnp.sum(n, axis=0, keepdims=True)
        m = n * vec[0:1, :]
        mean = jnp.mean(m, axis=-1, keepdims=True)
        mean_x = jnp.mean(m * xhat, axis=-1, keepdims=True)
        cot[here] = (dn2[here] + r * (m - mean - xhat * mean_x)).astype(BF)

    if direct:
        red.z_mid(0, 0)
        for w in (3, 4, 5):
            red.x_add(w, pair_at[0])
        red.y_add(2)
    back_one(pl.ds(0, CHUNK))
    tokens_out(1, cot, (0, 1))
    if direct:
        red.z_out(1, 1)
        red.z_mid(0, 1)
    back_one(pl.ds(CHUNK, CHUNK))
    tokens_out(1, cot, (2, 3, 4))

    sums[3:4, :] += pad_acc[...]
    order = (0, 1, 2, 3, 4, 5, 6, 7, 8, 9, 10, 11)
    for n, row in enumerate(order):
        for k in range(6):
            few_out[pl.ds(n * 6 + k, 1), :] = sums[pl.ds(row, 1), pl.ds(k * 128, 128)]
    lane = lax.broadcasted_iota(jnp.int32, (SEG, 128), 1) // HEAD_DIM
    for axis in range(2):
        total = jnp.zeros((SEG, 128), F32)
        for h in range(HALF_HEADS):
            piece = acc[pl.ds((h // 3) * 256 + axis * 128 + (h % 3) * SEG, SEG), pl.ds((h // 2) * 128, 128)]
            total = total + jnp.where(lane == h % 2, piece, 0.0)
        few_out[pl.ds(72 + axis * SEG, SEG), :] = total

    if direct:
        steps = (red.to_s, red.to_x, red.to_y, (f, ctx + 1 - 2 * (ctx % 2), tp), (f, (ctx + 2) % 4, tp))

        def few_copy(n):
            return remote(few_in.at[5 + n], few_in.at[n], steps[n], few_s.at[n], few_r.at[n])

        def few_start(n):
            few_in[5 + n] = few_out[...]
            few_copy(n).start()

        def few_add(n):
            few_copy(n).wait_recv()
            few_out[...] = few_out[...] + few_in[n]

        few_start(0)
        red.z_end(1, 0)
        red.z_out(0, 0)
        red.z_mid(2, 0)
        for w in (3, 4, 5):
            red.x_add(w, own)
        red.z_end(1, 1)
        red.z_out(0, 1)
        few_add(0)
        few_start(1)
        red.y_add(3)
        red.z_out(2, 0)
        red.z_end(0, 0)
        red.y_add(4)
        red.z_mid(3, 0)
        red.y_add(5)
        few_add(1)
        few_start(2)
        red.z_end(0, 1)
        red.z_mid(4, 0)
        red.z_out(3, 0)
        red.z_end(2, 0)
        few_add(2)
        few_start(3)
        red.z_mid(5, 0)
        red.z_out(4, 0)
        red.z_end(3, 0)
        few_add(3)
        few_start(4)
        red.z_out(5, 0)
        red.z_end(4, 0)
        red.z_end(5, 0)
        few_add(4)
        for w in range(6):
            red.sent(w)
        for n in range(5):
            few_copy(n).wait_send()
    else:
        for n, src in enumerate((wu, wd, wp, dwq.at[0], dwq.at[1], dwq.at[2])):
            cp = pltpu.make_async_copy(src, outs[n], ls.at[n])
            cp.start()
            cp.wait()
    tokens_done(0, dg)
    tokens_done(1, cot)


def backward(inputs, small, images, direct):
    any_spec = pl.BlockSpec(memory_space=pl.ANY)
    vmem = pl.BlockSpec(memory_space=pltpu.VMEM)
    dma = pltpu.SemaphoreType.DMA
    shape = jax.ShapeDtypeStruct
    n_places = NFULL * PAIRS + NPART * (4 + PAIRS)
    wholes = ((4 * D, D), (4 * D, D), (D, D), (D, D), (D, D), (D, D))
    out_shape = [shape((2, images, 2, PIECE, D), BF), shape((FEW, 128), F32)]
    out_shape += [shape(s, BF) for s in (HALVES if direct else wholes)[:3]]
    out_shape += [shape((576, 384) if direct else (3, D, D), BF)]
    v = pltpu.VMEM
    scratch = [v((ROWS, D), BF)] * 6 + [v((ROWS, D), F32)] * 2
    scratch += [
        v((4 * D, D), BF), v((4 * D, D), BF), v((D, D), BF), v((3, D, D), BF), v((3, D, D), BF),
        v((ROWS, 3 * D), BF), v((2, FULL, HALF_HEADS * 256), BF), v((1 + NPART, 3, FULL, 256), BF), v((HALF, 512), BF),
        v((FULL, 512), BF), v((FULL, HALF), F32),
        v((1, D), F32), v((1, D), F32), v((SUMS, D), F32), v((ROWS, 1), F32), v((ROWS, 1), F32), v((16, D), F32),
        dma((24,)), dma((2, n_places)), dma((2, images, 2, 5)),
    ]
    if direct:
        scratch += [v((2, D, D), BF), v((2, D, D), BF), v((2, 192, D), BF)]
        scratch += [v((2 if w else 1,) + s, BF) for w, s in enumerate(HALVES)]
        scratch += [v(s if w else (D, D), BF) for w, s in enumerate(HALVES)]
        scratch += [v((2,) + s, BF) for s in HALVES]
        scratch += [v((10, FEW, 128), F32)]
        scratch += [dma((6, 2)), dma((6, 2)), dma((6, 2)), dma((6, 2)), dma((6,)), dma((6,)), dma((6, 2, 2)), dma((6, 2, 3)), dma((6, 2))]
        scratch += [dma((5,)), dma((5,))]
    return pl.pallas_call(
        functools.partial(backward_kernel, images, direct),
        out_shape=out_shape,
        in_specs=[any_spec] * len(inputs) + [vmem] * len(small),
        out_specs=[any_spec, vmem] + [any_spec] * 4,
        scratch_shapes=scratch,
        compiler_params=pltpu.CompilerParams(
            collective_id=1, has_side_effects=True, vmem_limit_bytes=VMEM_BACK
        ),
        name="backward",
    )(*inputs, *small)


SMALL = (0, 1, 4, 5, 6, 7)


def results_kernel(images, n_grads, staged, few, *refs):
    grads, refs = refs[:n_grads], refs[n_grads:]
    tokens, small, (qv, up, rel_h, rel_w), outs = refs[:2], refs[2:8], refs[8:12], refs[12:]
    unpack = pack_matrix()
    for a in range(2):
        for i in range(images):
            for u in range(2):
                tokens[a][i, pl.ds(u * 128, 128)] = tn(unpack, staged[a, i, u]).astype(BF)
    for row, out in zip(SMALL, small):
        out[...] = few[pl.ds(row * 6, 6), :]
    for n in range(2):
        for k in range(6):
            qv[pl.ds(n, 1), pl.ds(k * 128, 128)] = few[pl.ds((2 + n) * 6 + k, 1), :]
    up[...] = few[pl.ds(48, 24), :]
    for axis, out in enumerate((rel_h, rel_w)):
        table = few[pl.ds(72 + axis * SEG, SEG), :]
        table = table + pltpu.roll(table, HEAD_DIM, 1)
        for j in range(RELS):
            out[pl.ds(j, 1), :] = table[26 - j:27 - j, :HEAD_DIM]
    for src, dst in zip(grads, outs):
        rows = src.shape[0]

        @pl.loop(0, rows // 64)
        def _(k, src=src, dst=dst):
            here = pl.ds(pl.multiple_of(k * 64, 16), 64)
            dst[here] = src[here].astype(F32)


def results(staged, few, grads):
    images = staged.shape[1]
    vmem = pl.BlockSpec(memory_space=pltpu.VMEM)
    shape = jax.ShapeDtypeStruct
    outs = [shape((images, 256, D), BF)] * 2 + [shape((6, 128), F32)] * 6
    outs += [shape((2, D), F32), shape((24, 128), F32), shape((RELS, HEAD_DIM), F32), shape((RELS, HEAD_DIM), F32)]
    outs += [shape(g.shape, F32) for g in grads]
    return pl.pallas_call(
        functools.partial(results_kernel, images, len(grads)),
        out_shape=outs,
        in_specs=[vmem] * (2 + len(grads)),
        out_specs=[vmem] * len(outs),
        compiler_params=pltpu.CompilerParams(vmem_limit_bytes=VMEM_LIMIT),
        name="results",
    )(staged, few, *grads)


def gelu_both(u):
    x = jnp.abs(u) * math.sqrt(0.5)
    t = 1.0 / (1.0 + 0.3275911 * x)
    e = jnp.exp(-0.5 * u * u)
    poly = t * (0.254829592 + t * (-0.284496736 + t * (1.421413741 + t * (-1.453152027 + t * 1.061405429))))
    tail = 0.5 * poly * e
    phi = jnp.where(u >= 0, 1.0 - tail, tail)
    return u * phi, phi + u * e * (1.0 / math.sqrt(2 * math.pi))


def whole_weights(shards):
    wq, wp, wu, wd = shards
    wq = lax.all_gather(lax.all_gather(wq, "fsdp", axis=2, tiled=True), "tp", axis=1, tiled=True)
    wp = lax.all_gather(lax.all_gather(wp, "fsdp", axis=1, tiled=True), "tp", axis=0, tiled=True)
    wu = lax.all_gather(lax.all_gather(wu, "fsdp", axis=0, tiled=True), "tp", axis=1, tiled=True)
    wd = lax.all_gather(lax.all_gather(wd, "fsdp", axis=1, tiled=True), "tp", axis=0, tiled=True)
    return wq, wp, wu, wd


def summed_weights(grads):
    out = []
    for w, grad in enumerate(grads):
        part = lax.psum_scatter(grad, "tp", scatter_dimension=0, tiled=True)
        part = lax.psum_scatter(part, "fsdp", scatter_dimension=0 if w == 0 else 1, tiled=True)
        out.append(lax.psum(part, "ctx").astype(F32))
    return out


def local(direct, block_input, ln1_gain, ln1_bias, w_qkv, qkv_bias, rel_h, rel_w, w_proj, proj_bias,
          ln2_gain, ln2_bias, w_up, up_bias, w_down, down_bias, cotangent):
    images = block_input.shape[1]
    x3 = jnp.transpose(block_input, (1, 0, 2))
    c3 = jnp.transpose(cotangent, (1, 0, 2))
    shards = (jnp.transpose(w_qkv, (0, 2, 1)), w_proj, w_up, w_down)
    front = (ln1_gain, ln1_bias, qkv_bias, ln2_gain, ln2_bias, proj_bias, down_bias, rel_h, rel_w)
    if direct:
        kept = forward(x3, c3, shards, None, front)
    else:
        wq, wp, wu, wd = whole_weights(shards)
        wu = jnp.swapaxes(wu.reshape(D, 4, D), 0, 1).reshape(4 * D, D)
        kept = forward(x3, c3, None, (wq, wp), front)
        kept = [*kept[:10], wq, wp, wu, wd, *kept[10:]]
    staged, few, *grads = backward(kept, (ln1_gain, ln2_gain, qkv_bias, up_bias), images, direct)
    if direct:
        small = results(staged, few, grads)
        ou, od, op, oq = small[12:]
        oq = oq.reshape(3, 192, 384)
    else:
        few = lax.psum(few, ("fsdp", "ctx", "tp"))
        small = results(staged, few, ())
        ou, od, op, oq, ok, ov = summed_weights(grads[:3] + [grads[3][k] for k in range(3)])
        oq = jnp.stack([oq, ok, ov])
    out3, dx3, s_g1, s_b1, s_proj, s_g2, s_b2, s_down, s_qv, s_up, s_relh, s_relw = small[:12]
    return (
        jnp.transpose(out3, (1, 0, 2)), jnp.transpose(dx3, (1, 0, 2)), s_g1.reshape(D), s_b1.reshape(D),
        jnp.transpose(oq, (0, 2, 1)), s_qv, s_relh, s_relw,
        op, s_proj.reshape(D), s_g2.reshape(D), s_b2.reshape(D), ou, s_up.reshape(4 * D), od, s_down.reshape(D),
    )


def solution(mesh):
    direct = mesh.shape["fsdp"] == 2
    rows = P(("ctx", "tp"), "fsdp", None)
    w_specs = (P(None, "fsdp", "tp"), P("tp", "fsdp"), P("fsdp", "tp"), P("tp", "fsdp"))
    return jax.shard_map(
        functools.partial(local, direct),
        mesh=mesh,
        in_specs=(rows, P(), P(), w_specs[0], P(), P(), P(), w_specs[1], P(), P(), P(), w_specs[2], P(), w_specs[3], P(), rows),
        out_specs=(rows, rows, P(), P(), w_specs[0], P(), P(), P(), w_specs[1], P(), P(), P(), w_specs[2], P(), w_specs[3], P()),
        check_vma=False,
    )
```
